256 devices in a mesh: src: 32 (over y, x, core), tgt: 8 (over z).
Axes of the slice: x: 4, y: 4, z: 8, core: 2. Of those that a mesh axis runs over, the one named last changes fastest.
Arguments:
- src_points: bfloat16 [32, 524288], P(None, 'src'), may hold values from -24 to 24
- tgt_points: bfloat16 [32, 524288], P(None, 'tgt'), may hold values from -6 to 6
- tgt_potential: float32 [524288], P('tgt'), may hold values from -2 to 2
- support: int32 [4096, 8, 6], P('src', 'tgt'), may hold values from 0 to 511, as said below
- counts: int32 [4096, 8], P('src', 'tgt'), may hold values from 1 to 6, as said below
Outputs:
- src_potential: float32 [524288], P('src')
- new_tgt_potential: float32 [524288], P('tgt')
The draws below stay inside these ranges and needn't reach their ends.
Inputs may be any that keep to these rules, and one draw needn't show every extreme that they name: support[r, t, k] names target block t * 512 + support[r, t, k]; the first counts[r, t] entries of a list are distinct; every target block is named in the used part of some list. `counts`: for every source block the list of some target shard is full.
All inputs are finite; a program needn't handle non-finite values.
Results may differ from the reference program's by a relative error of at most 0.0004.
Values sent between devices are 32-bit elements; how exact they have to be, the bound alone decides.
A program may use at most 128 MiB of HBM per device.

```python
import math
import jax
import jax.numpy as jnp
from jax import lax

DIM = 32
BLK = 128
K = 6
RB = 4096
TBLK_DEV = 512
NS = 524288
NT = 524288
N_TGT = 8


def draw_src_points(key, part):
    values = jax.random.normal(jax.random.fold_in(key, 1), (DIM, NS), jnp.float32)
    return jnp.clip(values, -24.0, 24.0).astype(jnp.bfloat16)


def support_tables(key):
    shifts = jax.random.randint(jax.random.fold_in(key, 11), (N_TGT,), 0, TBLK_DEV)
    list_keys = jax.random.split(jax.random.fold_in(key, 12), RB * N_TGT)

    def one_list(list_key):
        return jax.random.permutation(list_key, TBLK_DEV - 1)[:K - 1] + 1
    others = jax.vmap(one_list)(list_keys).reshape(RB, N_TGT, K - 1).astype(jnp.int32)
    starts = (jnp.arange(RB, dtype=jnp.int32)[:, None] + shifts[None, :]) % TBLK_DEV
    steps_from = jnp.concatenate([jnp.zeros((RB, N_TGT, 1), jnp.int32), others], axis=2)
    block_lists = (starts[:, :, None] + steps_from) % TBLK_DEV
    full_shard = jax.random.randint(jax.random.fold_in(key, 13), (RB,), 0, N_TGT)
    partial_counts = jax.random.randint(jax.random.fold_in(key, 14), (RB, N_TGT), 1, K + 1)
    list_counts = jnp.where(jnp.arange(N_TGT, dtype=jnp.int32)[None, :] == full_shard[:, None], K, partial_counts)
    return (block_lists.astype(jnp.int32), list_counts.astype(jnp.int32))


def draw_support(key, part):
    return support_tables(key)[0]


def draw_counts(key, part):
    return support_tables(key)[1]


def block_levels(rng, shape, cuts, low, largest):
    factor_of, own = 1.0, jax.random.fold_in(rng, 6)
    for axis_at, parts in cuts:
        steps = jnp.exp(jax.random.uniform(jax.random.fold_in(own, axis_at), (parts,), jnp.float32, low / len(cuts), largest / len(cuts)))
        factor_of = factor_of * jnp.repeat(steps, shape[axis_at] // parts).reshape([-1 if axis == axis_at else 1 for axis in range(len(shape))])
    return factor_of


def scatter_about(own_key, extent, width, bound, pieces=(), kind=jnp.bfloat16):
    loudness = block_levels(own_key, extent, pieces, -0.22, 0.18) if pieces else 1.0
    drawn = jax.random.normal(own_key, extent, jnp.float32) * width * loudness
    return jnp.minimum(jnp.maximum(drawn, -bound), bound).astype(kind)


def setup_inputs(seed: int = 0) -> dict:
    seeds = jax.random.split(jax.random.key(seed), 6)
    return {
        "src_points": draw_src_points(jax.random.fold_in(seeds[5], 71), 0),
        "tgt_points": scatter_about(seeds[1], (DIM, NT), 1.0, 6.0, ((1, 8),)),
        "tgt_potential": scatter_about(seeds[2], (NT,), 0.3, 2.0, ((0, 8),), jnp.float32),
        "support": draw_support(jax.random.fold_in(seeds[5], 71), 0),
        "counts": draw_counts(jax.random.fold_in(seeds[5], 71), 0),
    }


entropy_blur = 0.05
neg_fill = -1.0e30


def reference(src_points, tgt_points, tgt_potential, support, counts):
    tgt_blocks = NT // BLK
    list_width = N_TGT * K
    offsets = (jnp.arange(N_TGT, dtype=jnp.int32) * TBLK_DEV)[None, :, None]
    block_lists = (support + offsets).reshape(RB, list_width).astype(jnp.int32)
    live_slots = (jnp.arange(K, dtype=jnp.int32)[None, None, :] < counts[:, :, None]).reshape(RB, list_width)
    src_sq = jnp.sum(jnp.square(src_points.astype(jnp.float32)), axis=0).reshape(RB, BLK)
    tgt_cube = tgt_points.reshape(DIM, tgt_blocks, BLK)
    tgt_sq = jnp.sum(jnp.square(tgt_points.astype(jnp.float32)), axis=0).reshape(tgt_blocks, BLK)
    tgt_pot = tgt_potential.reshape(tgt_blocks, BLK)
    per_step = math.gcd(RB, 16)
    step_count = RB // per_step

    def block_pass(step_index):
        first_block = step_index * per_step
        src_rows = lax.dynamic_slice_in_dim(src_points, first_block * BLK, per_step * BLK, 1)
        src_rows = src_rows.reshape(DIM, per_step, BLK).astype(jnp.float32)
        picked = lax.dynamic_slice_in_dim(block_lists, first_block, per_step, 0)
        live_mask = lax.dynamic_slice_in_dim(live_slots, first_block, per_step, 0)
        rows_sq = lax.dynamic_slice_in_dim(src_sq, first_block, per_step, 0)
        near_points = jnp.take(tgt_cube, picked.reshape(-1), axis=1)
        near_points = near_points.reshape(DIM, per_step, list_width, BLK).astype(jnp.float32)
        inner_prod = jnp.einsum("dgi,dgkj->gikj", src_rows, near_points, precision=lax.Precision.HIGHEST)
        cost_tile = (rows_sq[:, :, None, None] + tgt_sq[picked][:, None, :, :]) / (2.0 * DIM) - inner_prod / DIM
        row_score = jnp.where(live_mask[:, None, :, None], (tgt_pot[picked][:, None, :, :] - cost_tile) / entropy_blur, neg_fill)
        highest = jnp.max(row_score, axis=(2, 3))
        summed = jnp.sum(jnp.exp(row_score - highest[:, :, None, None]), axis=(2, 3))
        src_block_pot = -entropy_blur * (highest + jnp.log(summed) - math.log(NT))
        col_score = jnp.where(live_mask[:, None, :, None], (src_block_pot[:, :, None, None] - cost_tile) / entropy_blur, neg_fill)
        col_high = jnp.max(col_score, axis=1)
        col_total = jnp.sum(jnp.exp(col_score - col_high[:, None]), axis=1)
        return src_block_pot, col_high, col_total

    src_pot, tile_high, tile_total = lax.map(block_pass, jnp.arange(step_count, dtype=jnp.int32))
    tile_high = tile_high.reshape(RB * list_width, BLK)
    tile_total = tile_total.reshape(RB * list_width, BLK)
    owners = jnp.where(live_slots, block_lists, tgt_blocks).reshape(-1).astype(jnp.int32)
    seg_high = jax.ops.segment_max(tile_high, owners, num_segments=tgt_blocks + 1)
    seg_total = jax.ops.segment_sum(tile_total * jnp.exp(tile_high - seg_high[owners]), owners, num_segments=tgt_blocks + 1)
    new_pot = -entropy_blur * (seg_high[:tgt_blocks] + jnp.log(seg_total[:tgt_blocks]) - math.log(NS))
    return src_pot.reshape(NS), new_pot.reshape(NT)
```

```python
import functools
import math

import jax
import jax.numpy as jnp
from jax import lax
from jax.experimental import pallas as pl
from jax.experimental.pallas import tpu as pltpu
from jax.sharding import PartitionSpec as P

BLK = 128
BLUR = 0.05
NEG = -1e30
TO_LOG2 = math.log2(math.e) / BLUR
FROM_LOG2 = BLUR * math.log(2.0)
DEPTH = 80
GROUP = 4
F32 = jnp.float32
BF16 = jnp.bfloat16
MESH = pl.DeviceIdType.MESH


def three_parts(v):
    hi = v.astype(BF16).astype(F32)
    mid = (v - hi).astype(BF16).astype(F32)
    return hi, mid, v - hi - mid


def source_rows(x, scale, extra):
    scaled = x.astype(F32) * scale
    hi = scaled.astype(BF16).astype(F32)
    pad = jnp.zeros((BLK - 2 * x.shape[0] - 8, BLK), F32)
    stacked = jnp.concatenate([hi, scaled - hi, extra, pad], axis=0)
    return stacked.T.astype(BF16)[:, :DEPTH]


def sort_by_count(counts_ref, order_ref, start_ref, blocks, slots):
    for c in range(slots + 1):
        start_ref[c] = 0

    def tally(r, _):
        c = counts_ref[r]
        start_ref[c] = start_ref[c] + 1
        return 0

    lax.fori_loop(0, blocks, tally, 0)
    total = 0
    for c in range(1, slots + 1):
        here = start_ref[c]
        start_ref[c] = total
        total = total + here

    def place(r, _):
        c = counts_ref[r]
        at = start_ref[c]
        order_ref[at] = r
        start_ref[c] = at + 1
        return 0

    lax.fori_loop(0, blocks, place, 0)


def by_group(counts_ref, order_ref, blocks, slots, work):
    def step(g, _):
        rows = [order_ref[g * GROUP + q] for q in range(GROUP)]
        most = counts_ref[rows[-1]]
        for c in range(1, slots + 1):
            pl.when(most == c)(functools.partial(work, rows, c))
        return 0

    lax.fori_loop(0, blocks // GROUP, step, 0)


def lane_block(ref, index):
    return ref[:, pl.ds(pl.multiple_of(index * BLK, BLK), BLK)]


def row_kernel(support_ref, counts_ref, x_ref, y_ref, g_ref, out_ref, order_ref, start_ref, extra_ref, score_ref):
    blocks = out_ref.shape[0]
    slots = support_ref.shape[0] // blocks
    features = x_ref.shape[0]
    tgt_blocks = g_ref.shape[0]
    sort_by_count(counts_ref, order_ref, start_ref, blocks, slots)
    sub = lax.broadcasted_iota(jnp.int32, (16, BLK), 0)

    def prepare(step, _):
        wide = y_ref[:, pl.ds(pl.multiple_of(step * 8 * BLK, 8 * BLK), 8 * BLK)].astype(F32)
        sq = jnp.sum(wide * wide, axis=0, keepdims=True)
        pot = g_ref[pl.ds(pl.multiple_of(step * 8, 8), 8), :]
        for q in range(8):
            bias = TO_LOG2 * pot[q : q + 1] - (TO_LOG2 / (2 * features)) * sq[:, q * BLK : (q + 1) * BLK]
            hi, mid, lo = three_parts(bias)
            rows = jnp.where(sub == 0, hi, jnp.where(sub == 1, mid, jnp.where(sub == 2, lo, 0.0)))
            extra_ref[step * 8 + q] = rows.astype(BF16)
        return 0

    lax.fori_loop(0, tgt_blocks // 8, prepare, 0)
    extra_ref[tgt_blocks] = jnp.where(sub == 0, NEG, 0.0).astype(BF16)
    ones = jnp.where(lax.broadcasted_iota(jnp.int32, (8, BLK), 0) < 3, 1.0, 0.0)
    lane = lax.broadcasted_iota(jnp.int32, (BLK, BLK), 1)
    diagonal = lane == lax.broadcasted_iota(jnp.int32, (BLK, BLK), 0)

    def work(rows, c):
        highs = []
        for q, r in enumerate(rows):
            left = source_rows(lane_block(x_ref, r), TO_LOG2 / features, ones)
            live = counts_ref[r]
            high = None
            for k in range(c):
                t = support_ref[r * slots + k]
                y = lane_block(y_ref, t)
                right = jnp.concatenate([y, y, extra_ref[jnp.where(k < live, t, tgt_blocks)]], axis=0)
                score = jnp.dot(left, right, preferred_element_type=F32)
                score_ref[q * slots + k] = score
                high = score if high is None else jnp.maximum(high, score)
            highs.append(jnp.max(high, axis=1, keepdims=True))
        for q, r in enumerate(rows):
            total = None
            for k in range(c):
                term = jnp.exp2(score_ref[q * slots + k] - highs[q])
                total = term if total is None else total + term
            lse = highs[q] + jnp.log2(jnp.sum(total, axis=1, keepdims=True))
            flat = jnp.sum(jnp.where(diagonal, lse, 0.0), axis=0, keepdims=True)
            out_ref[pl.ds(r, 1), :] = flat

    by_group(counts_ref, order_ref, blocks, slots, work)


def col_kernel(log_total, support_ref, counts_ref, x_ref, y_ref, lse_ref, pot_ref, out_ref, order_ref, start_ref, high_ref, total_ref):
    blocks = lse_ref.shape[0]
    slots = support_ref.shape[0] // blocks
    features = x_ref.shape[0]
    tgt_blocks = out_ref.shape[0]
    sort_by_count(counts_ref, order_ref, start_ref, blocks, slots)

    def clear(step, _):
        at = pl.ds(pl.multiple_of(step * 64, 64), 64)
        high_ref[at, :] = jnp.full((64, BLK), NEG, F32)
        total_ref[at, :] = jnp.zeros((64, BLK), F32)
        return 0

    lax.fori_loop(0, high_ref.shape[0] // 64, clear, 0)
    pad_ones = jnp.where(lax.broadcasted_iota(jnp.int32, (16, BLK), 0) < 3, 1.0, 0.0).astype(BF16)
    sub = lax.broadcasted_iota(jnp.int32, (8, BLK), 0)

    def work(rows, c):
        for r in rows:
            x = lane_block(x_ref, r)
            xf = x.astype(F32)
            pot = -FROM_LOG2 * lse_ref[pl.ds(r, 1), :] + BLUR * log_total
            pot_ref[pl.ds(r, 1), :] = pot + jnp.sum(xf * xf, axis=0, keepdims=True) * (1.0 / (2 * features))
            hi, mid, lo = three_parts(TO_LOG2 * pot)
            extra = jnp.where(sub == 0, hi, jnp.where(sub == 1, mid, jnp.where(sub == 2, lo, 0.0)))
            left = source_rows(x, TO_LOG2 / features, extra)
            live = counts_ref[r]
            places, news_high, news_total = [], [], []
            for k in range(c):
                t = support_ref[r * slots + k]
                y = lane_block(y_ref, t)
                right = jnp.concatenate([y, y, pad_ones], axis=0)
                score = jnp.dot(left, right, preferred_element_type=F32).reshape(BLK // 8, 8, BLK)
                at = pl.ds(pl.multiple_of(jnp.where(k < live, t, tgt_blocks + k) * 8, 8), 8)
                own = jnp.max(score, axis=0)
                own_total = jnp.sum(jnp.exp2(score - own[None]), axis=0)
                old = high_ref[at, :]
                high = jnp.maximum(own, old)
                places.append(at)
                news_high.append(high)
                news_total.append(own_total * jnp.exp2(own - high) + total_ref[at, :] * jnp.exp2(old - high))
            for at, high, total in zip(places, news_high, news_total):
                high_ref[at, :] = high
                total_ref[at, :] = total

    by_group(counts_ref, order_ref, blocks, slots, work)

    def finish(step, _):
        at = [pl.ds(step * 64 + s, 8, stride=8) for s in range(8)]
        highs = [high_ref[a, :] for a in at]
        high = functools.reduce(jnp.maximum, highs)
        total = sum(total_ref[a, :] * jnp.exp2(h - high) for a, h in zip(at, highs))
        out_ref[pl.ds(pl.multiple_of(step * 8, 8), 8), :] = jnp.where(total > 0.0, high + jnp.log2(total), NEG)
        return 0

    lax.fori_loop(0, tgt_blocks // 8, finish, 0)


def exchange_kernel(axis, n, part_ref, out_ref, parts, whole, send_sem, recv_sem, send_sem2, recv_sem2):
    me = lax.axis_index(axis)
    rows = part_ref.shape[0] // n
    barrier = pltpu.get_barrier_semaphore()
    peers = [lax.rem(me + s, n) for s in range(1, n)]
    for peer in peers:
        pl.semaphore_signal(barrier, inc=1, device_id={axis: peer}, device_id_type=MESH)
    pl.semaphore_wait(barrier, n - 1)

    def chunk(i):
        return pl.ds(pl.multiple_of(i * rows, rows), rows)

    copies = []
    for s, peer in enumerate(peers):
        copy = pltpu.make_async_remote_copy(
            src_ref=part_ref.at[chunk(peer)],
            dst_ref=parts.at[s],
            send_sem=send_sem.at[s],
            recv_sem=recv_sem.at[s],
            device_id={axis: peer},
            device_id_type=MESH,
        )
        copy.start()
        copies.append(copy)
    mine = part_ref[chunk(me), :]
    for copy in copies:
        copy.wait()
    high = mine
    for s in range(n - 1):
        high = jnp.maximum(high, parts[s])
    total = jnp.exp2(mine - high)
    for s in range(n - 1):
        total = total + jnp.exp2(parts[s] - high)
    whole[chunk(me), :] = high + jnp.log2(total)
    copies = []
    for s, peer in enumerate(peers):
        copy = pltpu.make_async_remote_copy(
            src_ref=whole.at[chunk(me)],
            dst_ref=whole.at[chunk(me)],
            send_sem=send_sem2.at[s],
            recv_sem=recv_sem2.at[s],
            device_id={axis: peer},
            device_id_type=MESH,
        )
        copy.start()
        copies.append(copy)
    for copy in copies:
        copy.wait()
    out_ref[...] = whole[...]


def exchange(axis, n, cid, part):
    return pl.pallas_call(
        functools.partial(exchange_kernel, axis, n),
        out_shape=jax.ShapeDtypeStruct(part.shape, F32),
        in_specs=[pl.BlockSpec(memory_space=pltpu.VMEM)],
        out_specs=pl.BlockSpec(memory_space=pltpu.VMEM),
        scratch_shapes=[
            pltpu.VMEM((n - 1, part.shape[0] // n, BLK), F32),
            pltpu.VMEM(part.shape, F32),
            pltpu.SemaphoreType.DMA((n - 1,)),
            pltpu.SemaphoreType.DMA((n - 1,)),
            pltpu.SemaphoreType.DMA((n - 1,)),
            pltpu.SemaphoreType.DMA((n - 1,)),
        ],
        compiler_params=pltpu.CompilerParams(collective_id=cid, has_side_effects=True),
        name="exchange_" + axis,
    )(part)


VMEM = pl.BlockSpec(memory_space=pltpu.VMEM)
SMEM = pl.BlockSpec(memory_space=pltpu.SMEM)


def row_pass(support, counts, x, y, g):
    blocks, slots, tgt_blocks = counts.shape[0], support.shape[0] // counts.shape[0], g.shape[0]
    return pl.pallas_call(
        row_kernel,
        out_shape=jax.ShapeDtypeStruct((blocks, BLK), F32),
        in_specs=[SMEM, SMEM, VMEM, VMEM, VMEM],
        out_specs=VMEM,
        scratch_shapes=[
            pltpu.SMEM((blocks,), jnp.int32),
            pltpu.SMEM((slots + 2,), jnp.int32),
            pltpu.VMEM((tgt_blocks + 1, 16, BLK), BF16),
            pltpu.VMEM((GROUP * slots, BLK, BLK), F32),
        ],
        compiler_params=pltpu.CompilerParams(vmem_limit_bytes=48 * 2**20),
        name="row_pass",
    )(support, counts, x, y, g)


def col_pass(log_total, support, counts, x, y, lse):
    blocks, slots, tgt_blocks = counts.shape[0], support.shape[0] // counts.shape[0], y.shape[1] // BLK
    return pl.pallas_call(
        functools.partial(col_kernel, log_total),
        out_shape=(jax.ShapeDtypeStruct((blocks, BLK), F32), jax.ShapeDtypeStruct((tgt_blocks, BLK), F32)),
        in_specs=[SMEM, SMEM, VMEM, VMEM, VMEM],
        out_specs=(VMEM, VMEM),
        scratch_shapes=[
            pltpu.SMEM((blocks,), jnp.int32),
            pltpu.SMEM((slots + 2,), jnp.int32),
            pltpu.VMEM((tgt_blocks * 8 + 64, BLK), F32),
            pltpu.VMEM((tgt_blocks * 8 + 64, BLK), F32),
        ],
        compiler_params=pltpu.CompilerParams(vmem_limit_bytes=48 * 2**20),
        name="col_pass",
    )(support, counts, x, y, lse)


def body(src_points, tgt_points, tgt_potential, support, counts):
    features = src_points.shape[0]
    total_src = src_points.shape[1] * lax.axis_size("src")
    total_tgt = tgt_points.shape[1] * lax.axis_size("tgt")
    flat_support = support.reshape(-1)
    flat_counts = counts.reshape(-1)
    row_part = row_pass(flat_support, flat_counts, src_points, tgt_points, tgt_potential.reshape(-1, BLK))
    row_lse = exchange("tgt", lax.axis_size("tgt"), 0, row_part)
    src_potential, col_part = col_pass(math.log(total_tgt), flat_support, flat_counts, src_points, tgt_points, row_lse)
    col_lse = exchange("src", lax.axis_size("src"), 1, col_part)
    tgt_sq = jnp.sum(jnp.square(tgt_points.astype(F32)), axis=0)
    new_tgt = tgt_sq / (2 * features) - FROM_LOG2 * col_lse.reshape(-1) + BLUR * math.log(total_src)
    return src_potential.reshape(-1), new_tgt


def solution(mesh):
    return jax.shard_map(
        body,
        mesh=mesh,
        in_specs=(P(None, "src"), P(None, "tgt"), P("tgt"), P("src", "tgt", None), P("src", "tgt")),
        out_specs=(P("src"), P("tgt")),
        check_vma=False,
    )
```

```python
import functools
import math

import jax
import jax.numpy as jnp
from jax import lax
from jax.experimental import pallas as pl
from jax.experimental.pallas import tpu as pltpu
from jax.sharding import PartitionSpec as P

BLK = 128
BLUR = 0.05
NEG = -1e30
TO_LOG2 = math.log2(math.e) / BLUR
FROM_LOG2 = BLUR * math.log(2.0)
GROUP = 32
F32 = jnp.float32
BF16 = jnp.bfloat16
MESH = pl.DeviceIdType.MESH


def three_parts(v):
    hi = v.astype(BF16).astype(F32)
    mid = (v - hi).astype(BF16).astype(F32)
    return hi, mid, v - hi - mid


def split_source(x, scale):
    scaled = x.astype(F32) * scale
    hi = scaled.astype(BF16)
    return hi, (scaled - hi.astype(F32)).astype(BF16)


def list_tiles(support_ref, counts_ref, list_ref, blocks, slots):
    def place(r, at):
        for k in range(slots):
            list_ref[at + k] = support_ref[k * blocks + r] * (8 * blocks) + (r * 8 + k)
        return at + counts_ref[r]

    live = lax.fori_loop(0, blocks, place, 0)
    for q in range(2 * GROUP):
        list_ref[live + q] = 7
    return (live + (GROUP - 1)) // GROUP


def lane_block(ref, index):
    return ref[:, pl.ds(pl.multiple_of(index * BLK, BLK), BLK)]


def eight_rows(index):
    return pl.ds(pl.multiple_of(index * 8, 8), 8)


def tile_score(left, right):
    return lax.dot_general(left, right, (((0,), (0,)), ((), ())), preferred_element_type=F32)


def tile_sums(score):
    score = score.reshape(BLK // 8, 8, BLK)
    high = jnp.max(score, axis=0)
    return high, jnp.sum(jnp.exp2(score - high[None]), axis=0)


def pipeline(list_ref, steps, score_ref, begin, end):
    for q in range(GROUP):
        score_ref[q] = begin(list_ref[q])

    def step(i, _):
        for q in range(GROUP):
            end(list_ref[i * GROUP + q], score_ref[q])
            score_ref[q] = begin(list_ref[(i + 1) * GROUP + q])
        return 0

    lax.fori_loop(0, steps, step, 0)


def merged_rows(high_ref, total_ref, step, stride):
    at = [pl.ds(step * 8 * stride + s, 8, stride=stride) for s in range(8)]
    highs = [high_ref[a, :] for a in at]
    high = functools.reduce(jnp.maximum, highs)
    total = sum(total_ref[a, :] * jnp.exp2(h - high) for a, h in zip(at, highs))
    return jnp.where(total > 0.0, high + jnp.log2(total), NEG)


def row_kernel(support_ref, counts_ref, x_any, y_any, g_any, out_ref, list_ref, x_ref, y_ref, g_ref, right_ref, high_ref, total_ref, score_ref, sem):
    blocks = out_ref.shape[0]
    slots = support_ref.shape[0] // blocks
    features = x_ref.shape[0]
    copies = [pltpu.make_async_copy(a, b, sem.at[i]) for i, (a, b) in enumerate(((x_any, x_ref), (y_any, y_ref), (g_any, g_ref)))]
    for copy in copies:
        copy.start()
    steps = list_tiles(support_ref, counts_ref, list_ref, blocks, slots)

    def clear(step, _):
        at = pl.ds(pl.multiple_of(step * 64, 64), 64)
        high_ref[at, :] = jnp.full((64, BLK), NEG, F32)
        total_ref[at, :] = jnp.zeros((64, BLK), F32)
        return 0

    lax.fori_loop(0, blocks, clear, 0)
    copies[0].wait()
    ones = jnp.where(lax.broadcasted_iota(jnp.int32, (32, BLK), 0) < 24, 1.0, 0.0).astype(BF16)

    def prepare(r, _):
        hi, lo = split_source(lane_block(x_ref, r), TO_LOG2 / features)
        right_ref[r] = jnp.concatenate([hi, lo, ones], axis=0)
        return 0

    lax.fori_loop(0, blocks, prepare, 0, unroll=4)
    copies[1].wait()
    copies[2].wait()

    slot_bits = (8 * blocks).bit_length() - 1

    def begin(code):
        t = lax.shift_right_logical(code, slot_bits)
        r = lax.shift_right_logical(jnp.bitwise_and(code, 8 * blocks - 1), 3)
        y = lane_block(y_ref, t)
        yf = y.astype(F32)
        sq = yf * yf
        sq = functools.reduce(jnp.add, [sq[i : i + 8] for i in range(0, features, 8)])
        bias = (TO_LOG2 / 8) * g_ref[pl.ds(t, 1), :] - (TO_LOG2 / (2 * features)) * sq
        hi, mid, lo = three_parts(bias)
        extra = jnp.concatenate([hi, mid, lo, jnp.zeros((8, BLK), F32)], axis=0).astype(BF16)
        return tile_score(jnp.concatenate([y, y, extra], axis=0), right_ref[r])

    def end(code, score):
        slot = jnp.bitwise_and(code, 8 * blocks - 1)
        high, total = tile_sums(score)
        high_ref[eight_rows(slot), :] = high
        total_ref[eight_rows(slot), :] = total

    pipeline(list_ref, steps, score_ref, begin, end)

    def merge(step, _):
        for q in range(8):
            r = step * 8 + q
            highs = [high_ref[eight_rows(r * 8 + k), :] for k in range(slots)]
            high = functools.reduce(jnp.maximum, highs)
            total = sum(total_ref[eight_rows(r * 8 + k), :] * jnp.exp2(h - high) for k, h in enumerate(highs))
            high_ref[eight_rows(r * 8), :] = high
            total_ref[eight_rows(r * 8), :] = total
        out_ref[eight_rows(step), :] = merged_rows(high_ref, total_ref, step, 64)
        return 0

    lax.fori_loop(0, blocks // 8, merge, 0)


def col_kernel(log_total, support_ref, counts_ref, x_ref, y_ref, lse_ref, pot_ref, out_any, list_ref, out_ref, left_ref, high_ref, total_ref, score_ref, sem):
    blocks = pot_ref.shape[0]
    slots = support_ref.shape[0] // blocks
    features = x_ref.shape[0]
    tgt_blocks = out_ref.shape[0]
    steps = list_tiles(support_ref, counts_ref, list_ref, blocks, slots)

    def clear(step, _):
        at = pl.ds(pl.multiple_of(step * 64, 64), 64)
        high_ref[at, :] = jnp.full((64, BLK), NEG, F32)
        total_ref[at, :] = jnp.zeros((64, BLK), F32)
        return 0

    lax.fori_loop(0, high_ref.shape[0] // 64, clear, 0)
    sub = lax.broadcasted_iota(jnp.int32, (16, BLK), 0)
    ones = jnp.where(sub < 3, 1.0, 0.0).astype(BF16)

    def prepare(r, _):
        x = lane_block(x_ref, r)
        xf = x.astype(F32)
        pot = -FROM_LOG2 * lse_ref[pl.ds(r, 1), :] + BLUR * log_total
        pot_ref[pl.ds(r, 1), :] = pot + jnp.sum(xf * xf, axis=0, keepdims=True) * (1.0 / (2 * features))
        hi, mid, lo = three_parts(TO_LOG2 * pot)
        extra = jnp.where(sub == 0, hi, jnp.where(sub == 1, mid, jnp.where(sub == 2, lo, 0.0))).astype(BF16)
        left_ref[r] = jnp.concatenate([*split_source(x, TO_LOG2 / features), extra], axis=0)
        return 0

    lax.fori_loop(0, blocks, prepare, 0, unroll=4)

    slot_bits = (8 * blocks).bit_length() - 1

    def begin(code):
        y = lane_block(y_ref, lax.shift_right_logical(code, slot_bits))
        r = lax.shift_right_logical(jnp.bitwise_and(code, 8 * blocks - 1), 3)
        return tile_score(left_ref[r], jnp.concatenate([y, y, ones], axis=0))

    def end(code, score):
        t = lax.shift_right_logical(code, slot_bits)
        own, own_total = tile_sums(score)
        at = eight_rows(jnp.where(jnp.bitwise_and(code, 7) == 7, tgt_blocks, t))
        old = high_ref[at, :]
        high = jnp.maximum(own, old)
        high_ref[at, :] = high
        total_ref[at, :] = own_total * jnp.exp2(own - high) + total_ref[at, :] * jnp.exp2(old - high)

    pipeline(list_ref, steps, score_ref, begin, end)

    def finish(step, _):
        out_ref[eight_rows(step), :] = merged_rows(high_ref, total_ref, step, 8)
        return 0

    pieces = 4
    size = tgt_blocks // pieces
    copies = []
    for piece in range(pieces):
        lax.fori_loop(piece * size // 8, (piece + 1) * size // 8, finish, 0, unroll=2)
        rows = pl.ds(piece * size, size)
        copies.append(pltpu.make_async_copy(out_ref.at[rows], out_any.at[rows], sem.at[piece]))
        copies[-1].start()
    for copy in copies:
        copy.wait()


def exchange_kernel(axis, n, shift, part_any, y_any, out_ref, mine_ref, parts, whole, y_ref, sq_ref, local_sem, send_sem, recv_sem, send_sem2, recv_sem2):
    me = lax.axis_index(axis)
    rows = part_any.shape[0] // n

    def chunk(i):
        return pl.ds(pl.multiple_of(i * rows, rows), rows)

    mine_copy = pltpu.make_async_copy(part_any.at[chunk(me)], mine_ref, local_sem.at[0])
    mine_copy.start()
    barrier = pltpu.get_barrier_semaphore()
    peers = [lax.rem(me + s, n) for s in range(1, n)]
    for peer in peers:
        pl.semaphore_signal(barrier, inc=1, device_id={axis: peer}, device_id_type=MESH)
    if y_any is not None:
        width = rows * BLK
        y_copy = pltpu.make_async_copy(y_any.at[:, pl.ds(pl.multiple_of(me * width, width), width)], y_ref, local_sem.at[1])
        y_copy.start()
        y_copy.wait()
        y = y_ref[...].astype(F32)
        sq = jnp.sum(y * y, axis=0, keepdims=True) * (1.0 / (2 * y.shape[0]))
        for q in range(rows):
            sq_ref[pl.ds(q, 1), :] = sq[:, q * BLK : (q + 1) * BLK]
    mine_copy.wait()
    pl.semaphore_wait(barrier, n - 1)

    copies = []
    for s, peer in enumerate(peers):
        copy = pltpu.make_async_remote_copy(
            src_ref=part_any.at[chunk(peer)],
            dst_ref=parts.at[s],
            send_sem=send_sem.at[s],
            recv_sem=recv_sem.at[s],
            device_id={axis: peer},
            device_id_type=MESH,
        )
        copy.start()
        copies.append(copy)
    mine = mine_ref[...]
    for copy in copies:
        copy.wait()
    high = mine
    for s in range(n - 1):
        high = jnp.maximum(high, parts[s])
    total = jnp.exp2(mine - high)
    for s in range(n - 1):
        total = total + jnp.exp2(parts[s] - high)
    result = high + jnp.log2(total)
    if y_any is not None:
        result = sq_ref[...] - FROM_LOG2 * result + shift
    whole[chunk(me), :] = result
    copies = []
    for s, peer in enumerate(peers):
        copy = pltpu.make_async_remote_copy(
            src_ref=whole.at[chunk(me)],
            dst_ref=whole.at[chunk(me)],
            send_sem=send_sem2.at[s],
            recv_sem=recv_sem2.at[s],
            device_id={axis: peer},
            device_id_type=MESH,
        )
        copy.start()
        copies.append(copy)
    for copy in copies:
        copy.wait()
    out_ref[...] = whole[...]


def row_exchange_kernel(axis, n, part_any, out_ref, *scratch):
    exchange_kernel(axis, n, 0.0, part_any, None, out_ref, *scratch[:3], None, None, *scratch[3:])


def exchange(axis, n, cid, shift, part, y=None):
    rows = part.shape[0] // n
    extra = [] if y is None else [pltpu.VMEM((y.shape[0], rows * BLK), BF16), pltpu.VMEM((rows, BLK), F32)]
    kernel = functools.partial(row_exchange_kernel, axis, n) if y is None else functools.partial(exchange_kernel, axis, n, shift)
    operands = (part,) if y is None else (part, y)
    return pl.pallas_call(
        kernel,
        out_shape=jax.ShapeDtypeStruct(part.shape, F32),
        in_specs=[pl.BlockSpec(memory_space=pl.ANY)] * len(operands),
        out_specs=pl.BlockSpec(memory_space=pltpu.VMEM),
        scratch_shapes=[
            pltpu.VMEM((rows, BLK), F32),
            pltpu.VMEM((n - 1, rows, BLK), F32),
            pltpu.VMEM(part.shape, F32),
            *extra,
            pltpu.SemaphoreType.DMA((2,)),
            pltpu.SemaphoreType.DMA((n - 1,)),
            pltpu.SemaphoreType.DMA((n - 1,)),
            pltpu.SemaphoreType.DMA((n - 1,)),
            pltpu.SemaphoreType.DMA((n - 1,)),
        ],
        compiler_params=pltpu.CompilerParams(collective_id=cid, has_side_effects=True, vmem_limit_bytes=8 * 2**20),
        name="exchange_" + axis,
    )(*operands)


VMEM = pl.BlockSpec(memory_space=pltpu.VMEM)
SMEM = pl.BlockSpec(memory_space=pltpu.SMEM)
ANY = pl.BlockSpec(memory_space=pl.ANY)


def row_pass(support, counts, x, y, g):
    blocks, slots = counts.shape[0], support.shape[0] // counts.shape[0]
    return pl.pallas_call(
        row_kernel,
        out_shape=jax.ShapeDtypeStruct((blocks, BLK), F32),
        in_specs=[SMEM, SMEM, ANY, ANY, ANY],
        out_specs=VMEM,
        scratch_shapes=[
            pltpu.SMEM((blocks * slots + 2 * GROUP + 8,), jnp.int32),
            pltpu.VMEM(x.shape, BF16),
            pltpu.VMEM(y.shape, BF16),
            pltpu.VMEM(g.shape, F32),
            pltpu.VMEM((blocks, 2 * x.shape[0] + 32, BLK), BF16),
            pltpu.VMEM((blocks * 64, BLK), F32),
            pltpu.VMEM((blocks * 64, BLK), F32),
            pltpu.VMEM((GROUP, BLK, BLK), F32),
            pltpu.SemaphoreType.DMA((3,)),
        ],
        name="row_pass",
        compiler_params=pltpu.CompilerParams(vmem_limit_bytes=56 * 2**20),
    )(support, counts, x, y, g)


def col_pass(log_total, support, counts, x, y, lse):
    blocks, slots, tgt_blocks = counts.shape[0], support.shape[0] // counts.shape[0], y.shape[1] // BLK
    return pl.pallas_call(
        functools.partial(col_kernel, log_total),
        out_shape=(jax.ShapeDtypeStruct((blocks, BLK), F32), jax.ShapeDtypeStruct((tgt_blocks, BLK), F32)),
        in_specs=[SMEM, SMEM, VMEM, VMEM, VMEM],
        out_specs=(VMEM, ANY),
        scratch_shapes=[
            pltpu.SMEM((blocks * slots + 2 * GROUP + 8,), jnp.int32),
            pltpu.VMEM((tgt_blocks, BLK), F32),
            pltpu.VMEM((blocks, 2 * x.shape[0] + 16, BLK), BF16),
            pltpu.VMEM((tgt_blocks * 8 + 64, BLK), F32),
            pltpu.VMEM((tgt_blocks * 8 + 64, BLK), F32),
            pltpu.VMEM((GROUP, BLK, BLK), F32),
            pltpu.SemaphoreType.DMA((4,)),
        ],
        name="col_pass",
        compiler_params=pltpu.CompilerParams(vmem_limit_bytes=40 * 2**20),
    )(support, counts, x, y, lse)


def body(src_points, tgt_points, tgt_potential, support, counts):
    total_src = src_points.shape[1] * lax.axis_size("src")
    total_tgt = tgt_points.shape[1] * lax.axis_size("tgt")
    flat_support = support.transpose(2, 1, 0).reshape(-1)
    flat_counts = counts.reshape(-1)
    row_part = row_pass(flat_support, flat_counts, src_points, tgt_points, tgt_potential.reshape(-1, BLK))
    row_lse = exchange("tgt", lax.axis_size("tgt"), 0, 0.0, row_part)
    src_potential, col_part = col_pass(math.log(total_tgt), flat_support, flat_counts, src_points, tgt_points, row_lse)
    new_tgt = exchange("src", lax.axis_size("src"), 1, BLUR * math.log(total_src), col_part, tgt_points)
    return src_potential.reshape(-1), new_tgt.reshape(-1)


def solution(mesh):
    return jax.shard_map(
        body,
        mesh=mesh,
        in_specs=(P(None, "src"), P(None, "tgt"), P("tgt"), P("src", "tgt", None), P("src", "tgt")),
        out_specs=(P("src"), P("tgt")),
        check_vma=False,
    )
```

```python
import functools
import math

import jax
import jax.numpy as jnp
from jax import lax
from jax.experimental import pallas as pl
from jax.experimental.pallas import tpu as pltpu
from jax.sharding import PartitionSpec as P

BLK = 128
BLUR = 0.05
NEG = -1e30
TO_LOG2 = math.log2(math.e) / BLUR
FROM_LOG2 = BLUR * math.log(2.0)
GROUP = 32
F32 = jnp.float32
BF16 = jnp.bfloat16
MESH = pl.DeviceIdType.MESH


def three_parts(v):
    hi = v.astype(BF16).astype(F32)
    mid = (v - hi).astype(BF16).astype(F32)
    return hi, mid, v - hi - mid


def split_source(x, scale):
    scaled = x.astype(F32) * scale
    hi = scaled.astype(BF16)
    return hi, (scaled - hi.astype(F32)).astype(BF16)


def list_tiles(support_ref, counts_ref, list_ref, blocks, slots):
    def place(r, at):
        for k in range(slots):
            list_ref[at + k] = support_ref[k, 0, r] * (8 * blocks) + (r * 8 + k)
        return at + counts_ref[r]

    live = lax.fori_loop(0, blocks, place, 0)
    for q in range(2 * GROUP):
        list_ref[live + q] = 7
    list_ref[list_ref.shape[0] - 1] = (live + (GROUP - 1)) // GROUP


def lane_block(ref, index):
    return ref[:, pl.ds(pl.multiple_of(index * BLK, BLK), BLK)]


def eight_rows(index):
    return pl.ds(pl.multiple_of(index * 8, 8), 8)


def tile_score(left, right):
    return lax.dot_general(left, right, (((0,), (0,)), ((), ())), preferred_element_type=F32)


def tile_sums(score):
    score = score.reshape(BLK // 8, 8, BLK)
    high = jnp.max(score, axis=0)
    return high, jnp.sum(jnp.exp2(score - high[None]), axis=0)


def pipeline(list_ref, score_ref, begin, end):
    for q in range(GROUP):
        score_ref[q] = begin(list_ref[q])

    def step(i, _):
        for q in range(GROUP):
            end(list_ref[i * GROUP + q], score_ref[q])
            score_ref[q] = begin(list_ref[(i + 1) * GROUP + q])
        return 0

    lax.fori_loop(0, list_ref[list_ref.shape[0] - 1], step, 0)


def merged_rows(high_ref, total_ref, step, stride):
    at = [pl.ds(step * 8 * stride + s, 8, stride=stride) for s in range(8)]
    highs = [high_ref[a, :] for a in at]
    high = functools.reduce(jnp.maximum, highs)
    total = sum(total_ref[a, :] * jnp.exp2(h - high) for a, h in zip(at, highs))
    return jnp.where(total > 0.0, high + jnp.log2(total), NEG)


def row_kernel(support_any, counts_any, x_any, y_any, g_any, out_ref, list_any, support_ref, counts_ref, list_ref, x_ref, y_ref, g_ref, right_ref, high_ref, total_ref, score_ref, sem):
    blocks = out_ref.shape[0]
    slots = support_ref.shape[0]
    features = x_ref.shape[0]
    pairs = ((support_any, support_ref), (counts_any, counts_ref), (x_any, x_ref), (y_any, y_ref), (g_any, g_ref))
    copies = [pltpu.make_async_copy(a, b, sem.at[i]) for i, (a, b) in enumerate(pairs)]
    for copy in copies:
        copy.start()
    copies[0].wait()
    copies[1].wait()
    list_tiles(support_ref, counts_ref, list_ref, blocks, slots)
    list_copy = pltpu.make_async_copy(list_ref, list_any, sem.at[5])
    list_copy.start()

    def clear(step, _):
        at = pl.ds(pl.multiple_of(step * 64, 64), 64)
        high_ref[at, :] = jnp.full((64, BLK), NEG, F32)
        total_ref[at, :] = jnp.zeros((64, BLK), F32)
        return 0

    lax.fori_loop(0, blocks, clear, 0)
    copies[2].wait()
    ones = jnp.where(lax.broadcasted_iota(jnp.int32, (32, BLK), 0) < 24, 1.0, 0.0).astype(BF16)

    def prepare(r, _):
        hi, lo = split_source(lane_block(x_ref, r), TO_LOG2 / features)
        right_ref[r] = jnp.concatenate([hi, lo, ones], axis=0)
        return 0

    lax.fori_loop(0, blocks, prepare, 0, unroll=16)
    copies[3].wait()
    copies[4].wait()

    slot_bits = (8 * blocks).bit_length() - 1

    def begin(code):
        t = lax.shift_right_logical(code, slot_bits)
        r = lax.shift_right_logical(jnp.bitwise_and(code, 8 * blocks - 1), 3)
        y = lane_block(y_ref, t)
        yf = y.astype(F32)
        sq = yf * yf
        sq = functools.reduce(jnp.add, [sq[i : i + 8] for i in range(0, features, 8)])
        bias = (TO_LOG2 / 8) * g_ref[pl.ds(t, 1), :] - (TO_LOG2 / (2 * features)) * sq
        hi, mid, lo = three_parts(bias)
        extra = jnp.concatenate([hi, mid, lo, jnp.zeros((8, BLK), F32)], axis=0).astype(BF16)
        return tile_score(jnp.concatenate([y, y, extra], axis=0), right_ref[r])

    def end(code, score):
        slot = jnp.bitwise_and(code, 8 * blocks - 1)
        high, total = tile_sums(score)
        high_ref[eight_rows(slot), :] = high
        total_ref[eight_rows(slot), :] = total

    pipeline(list_ref, score_ref, begin, end)

    def merge(step, _):
        for q in range(8):
            r = step * 8 + q
            highs = [high_ref[eight_rows(r * 8 + k), :] for k in range(slots)]
            high = functools.reduce(jnp.maximum, highs)
            total = sum(total_ref[eight_rows(r * 8 + k), :] * jnp.exp2(h - high) for k, h in enumerate(highs))
            high_ref[eight_rows(r * 8), :] = high
            total_ref[eight_rows(r * 8), :] = total
        out_ref[eight_rows(step), :] = merged_rows(high_ref, total_ref, step, 64)
        return 0

    lax.fori_loop(0, blocks // 8, merge, 0, unroll=4)
    list_copy.wait()


def col_kernel(log_total, list_any, x_ref, y_ref, lse_ref, pot_any, out_any, list_ref, pot_ref, out_ref, left_ref, high_ref, total_ref, score_ref, sem):
    blocks = pot_ref.shape[0]
    features = x_ref.shape[0]
    tgt_blocks = out_ref.shape[0]

    list_copy = pltpu.make_async_copy(list_any, list_ref, sem.at[4])
    list_copy.start()

    def clear(step, _):
        at = pl.ds(pl.multiple_of(step * 64, 64), 64)
        high_ref[at, :] = jnp.full((64, BLK), NEG, F32)
        total_ref[at, :] = jnp.zeros((64, BLK), F32)
        return 0

    lax.fori_loop(0, high_ref.shape[0] // 64, clear, 0)
    sub = lax.broadcasted_iota(jnp.int32, (16, BLK), 0)
    ones = jnp.where(sub < 3, 1.0, 0.0).astype(BF16)

    def prepare(r, _):
        x = lane_block(x_ref, r)
        xf = x.astype(F32)
        pot = -FROM_LOG2 * lse_ref[pl.ds(r, 1), :] + BLUR * log_total
        pot_ref[pl.ds(r, 1), :] = pot + jnp.sum(xf * xf, axis=0, keepdims=True) * (1.0 / (2 * features))
        hi, mid, lo = three_parts(TO_LOG2 * pot)
        extra = jnp.where(sub == 0, hi, jnp.where(sub == 1, mid, jnp.where(sub == 2, lo, 0.0))).astype(BF16)
        left_ref[r] = jnp.concatenate([*split_source(x, TO_LOG2 / features), extra], axis=0)
        return 0

    lax.fori_loop(0, blocks, prepare, 0, unroll=16)
    pot_copy = pltpu.make_async_copy(pot_ref, pot_any, sem.at[5])
    pot_copy.start()
    list_copy.wait()

    slot_bits = (8 * blocks).bit_length() - 1

    def begin(code):
        y = lane_block(y_ref, lax.shift_right_logical(code, slot_bits))
        r = lax.shift_right_logical(jnp.bitwise_and(code, 8 * blocks - 1), 3)
        return tile_score(left_ref[r], jnp.concatenate([y, y, ones], axis=0))

    def end(code, score):
        t = lax.shift_right_logical(code, slot_bits)
        own, own_total = tile_sums(score)
        at = eight_rows(jnp.where(jnp.bitwise_and(code, 7) == 7, tgt_blocks, t))
        old = high_ref[at, :]
        high = jnp.maximum(own, old)
        high_ref[at, :] = high
        total_ref[at, :] = own_total * jnp.exp2(own - high) + total_ref[at, :] * jnp.exp2(old - high)

    pipeline(list_ref, score_ref, begin, end)

    def finish(step, _):
        out_ref[eight_rows(step), :] = merged_rows(high_ref, total_ref, step, 8)
        return 0

    pieces = 4
    size = tgt_blocks // pieces
    copies = []
    for piece in range(pieces):
        lax.fori_loop(piece * size // 8, (piece + 1) * size // 8, finish, 0, unroll=8)
        rows = pl.ds(piece * size, size)
        copies.append(pltpu.make_async_copy(out_ref.at[rows], out_any.at[rows], sem.at[piece]))
        copies[-1].start()
    for copy in copies + [pot_copy]:
        copy.wait()


def remote(source, target, send_sem, recv_sem, axis, peer):
    copy = pltpu.make_async_remote_copy(
        src_ref=source,
        dst_ref=target,
        send_sem=send_sem,
        recv_sem=recv_sem,
        device_id={axis: peer},
        device_id_type=MESH,
    )
    copy.start()
    return copy


def greet(axis, peers):
    barrier = pltpu.get_barrier_semaphore()
    for peer in peers:
        pl.semaphore_signal(barrier, inc=1, device_id={axis: peer}, device_id_type=MESH)
    return lambda: pl.semaphore_wait(barrier, len(peers))


def combined(terms):
    high = functools.reduce(jnp.maximum, terms)
    return high + jnp.log2(sum(jnp.exp2(term - high) for term in terms))


def row_exchange_kernel(axis, n, part_any, out_ref, mine_ref, parts, whole, local_sem, send_sem, recv_sem, send_sem2, recv_sem2):
    me = lax.axis_index(axis)
    rows = part_any.shape[0] // n

    def chunk(i):
        return pl.ds(pl.multiple_of(i * rows, rows), rows)

    peers = [lax.rem(me + s, n) for s in range(1, n)]
    all_here = greet(axis, peers)
    mine_copy = pltpu.make_async_copy(part_any.at[chunk(me)], mine_ref, local_sem.at[0])
    mine_copy.start()
    mine_copy.wait()
    all_here()
    copies = [
        remote(part_any.at[chunk(peer)], parts.at[s], send_sem.at[s], recv_sem.at[s], axis, peer) for s, peer in enumerate(peers)
    ]
    for copy in copies:
        copy.wait_recv()
    whole[chunk(me), :] = combined([mine_ref[...]] + [parts[s] for s in range(n - 1)])
    after = [
        remote(whole.at[chunk(me)], whole.at[chunk(me)], send_sem2.at[s], recv_sem2.at[s], axis, peer) for s, peer in enumerate(peers)
    ]
    for copy in after:
        copy.wait_recv()
    out_ref[...] = whole[...]
    for copy in copies + after:
        copy.wait_send()


def row_exchange(axis, n, cid, part):
    rows = part.shape[0] // n
    return pl.pallas_call(
        functools.partial(row_exchange_kernel, axis, n),
        out_shape=jax.ShapeDtypeStruct(part.shape, F32),
        in_specs=[ANY],
        out_specs=VMEM,
        scratch_shapes=[
            pltpu.VMEM((rows, BLK), F32),
            pltpu.VMEM((n - 1, rows, BLK), F32),
            pltpu.VMEM(part.shape, F32),
            pltpu.SemaphoreType.DMA((1,)),
            pltpu.SemaphoreType.DMA((n - 1,)),
            pltpu.SemaphoreType.DMA((n - 1,)),
            pltpu.SemaphoreType.DMA((n - 1,)),
            pltpu.SemaphoreType.DMA((n - 1,)),
        ],
        compiler_params=pltpu.CompilerParams(collective_id=cid, has_side_effects=True, vmem_limit_bytes=8 * 2**20),
        name="exchange_" + axis,
    )(part)


PIECES = 4


def col_exchange_kernel(axis, n, shift, part_any, y_any, out_ref, mine_ref, twin_ref, pair_ref, parts, whole, y_ref, sq_ref, local_sem, send_a, recv_a, send_b, recv_b, send_c, recv_c, send_d, recv_d):
    me = lax.axis_index(axis)
    chips = n // 2
    core = lax.rem(me, 2)
    chip = lax.div(me, 2)
    twin = me + 1 - 2 * core
    rows = part_any.shape[0] // n
    half = chips * rows
    size = half // PIECES
    others = [lax.rem(chip + s, chips) for s in range(1, chips)]

    def chunk(where, i):
        return pl.ds(pl.multiple_of((where * chips + i) * rows, rows), rows)

    def local(i):
        return pl.ds(pl.multiple_of(i * rows, rows), rows)

    def piece(where, p):
        return pl.ds(pl.multiple_of(where * half + p * size, size), size)

    all_here = greet(axis, [twin] + [2 * other + core for other in others])
    mine_copy = pltpu.make_async_copy(part_any.at[pl.ds(pl.multiple_of(core * half, half), half)], mine_ref, local_sem.at[0])
    mine_copy.start()
    width = rows * BLK
    own = core * chips + chip
    y_copy = pltpu.make_async_copy(y_any.at[:, pl.ds(pl.multiple_of(own * width, width), width)], y_ref, local_sem.at[1])
    y_copy.start()
    y_copy.wait()
    y = y_ref[...].astype(F32)
    sq = jnp.sum(y * y, axis=0, keepdims=True) * (1.0 / (2 * y.shape[0]))
    for q in range(rows):
        sq_ref[pl.ds(q, 1), :] = sq[:, q * BLK : (q + 1) * BLK]
    mine_copy.wait()
    all_here()

    first = [
        remote(part_any.at[piece(1 - core, p)], twin_ref.at[pl.ds(p * size, size)], send_a.at[p], recv_a.at[p], axis, twin)
        for p in range(PIECES)
    ]
    for p in range(PIECES):
        first[p].wait_recv()
        at = pl.ds(p * size, size)
        pair_ref[at, :] = combined([mine_ref[at, :], twin_ref[at, :]])
    second = [
        remote(pair_ref.at[local(other)], parts.at[s], send_b.at[s], recv_b.at[s], axis, 2 * other + core)
        for s, other in enumerate(others)
    ]
    for copy in second:
        copy.wait_recv()
    result = combined([pair_ref[local(chip), :]] + [parts[s] for s in range(chips - 1)])
    mine = chunk(core, chip)
    whole[mine, :] = sq_ref[...] - FROM_LOG2 * result + shift
    third = [
        remote(whole.at[mine], whole.at[mine], send_c.at[s], recv_c.at[s], axis, 2 * other + core) for s, other in enumerate(others)
    ]
    fourth = [remote(whole.at[mine], whole.at[mine], send_d.at[chips - 1], recv_d.at[chips - 1], axis, twin)]
    for s in range(chips - 1):
        third[s].wait_recv()
        came = chunk(core, lax.rem(chip + chips - 1 - s, chips))
        fourth.append(remote(whole.at[came], whole.at[came], send_d.at[s], recv_d.at[s], axis, twin))
    for copy in fourth:
        copy.wait_recv()
    out_ref[...] = whole[...]
    for copy in first + second + third + fourth:
        copy.wait_send()


def col_exchange(axis, n, cid, shift, part, y):
    rows, chips = part.shape[0] // n, n // 2
    half = chips * rows
    sems = [pltpu.SemaphoreType.DMA((count,)) for count in (2, PIECES, PIECES, chips - 1, chips - 1, chips - 1, chips - 1, chips, chips)]
    return pl.pallas_call(
        functools.partial(col_exchange_kernel, axis, n, shift),
        out_shape=jax.ShapeDtypeStruct(part.shape, F32),
        in_specs=[ANY, ANY],
        out_specs=VMEM,
        scratch_shapes=[
            pltpu.VMEM((half, BLK), F32),
            pltpu.VMEM((half, BLK), F32),
            pltpu.VMEM((half, BLK), F32),
            pltpu.VMEM((chips - 1, rows, BLK), F32),
            pltpu.VMEM(part.shape, F32),
            pltpu.VMEM((y.shape[0], rows * BLK), BF16),
            pltpu.VMEM((rows, BLK), F32),
            *sems,
        ],
        compiler_params=pltpu.CompilerParams(collective_id=cid, has_side_effects=True, vmem_limit_bytes=8 * 2**20),
        name="exchange_" + axis,
    )(part, y)


VMEM = pl.BlockSpec(memory_space=pltpu.VMEM)
SMEM = pl.BlockSpec(memory_space=pltpu.SMEM)
ANY = pl.BlockSpec(memory_space=pl.ANY)


def row_pass(support, counts, x, y, g):
    blocks, slots = counts.shape[0], support.shape[0]
    return pl.pallas_call(
        row_kernel,
        out_shape=(jax.ShapeDtypeStruct((blocks, BLK), F32), jax.ShapeDtypeStruct((blocks * slots + 2 * GROUP + BLK,), jnp.int32)),
        in_specs=[ANY] * 5,
        out_specs=(VMEM, ANY),
        scratch_shapes=[
            pltpu.SMEM(support.shape, jnp.int32),
            pltpu.SMEM(counts.shape, jnp.int32),
            pltpu.SMEM((blocks * slots + 2 * GROUP + BLK,), jnp.int32),
            pltpu.VMEM(x.shape, BF16),
            pltpu.VMEM(y.shape, BF16),
            pltpu.VMEM(g.shape, F32),
            pltpu.VMEM((blocks, 2 * x.shape[0] + 32, BLK), BF16),
            pltpu.VMEM((blocks * 64, BLK), F32),
            pltpu.VMEM((blocks * 64, BLK), F32),
            pltpu.VMEM((GROUP, BLK, BLK), F32),
            pltpu.SemaphoreType.DMA((6,)),
        ],
        name="row_pass",
        compiler_params=pltpu.CompilerParams(vmem_limit_bytes=56 * 2**20),
    )(support, counts, x, y, g)


def col_pass(log_total, tiles, x, y, lse):
    blocks, tgt_blocks = lse.shape[0], y.shape[1] // BLK
    return pl.pallas_call(
        functools.partial(col_kernel, log_total),
        out_shape=(jax.ShapeDtypeStruct((blocks, BLK), F32), jax.ShapeDtypeStruct((tgt_blocks, BLK), F32)),
        in_specs=[ANY, VMEM, VMEM, VMEM],
        out_specs=(ANY, ANY),
        scratch_shapes=[
            pltpu.SMEM(tiles.shape, jnp.int32),
            pltpu.VMEM((blocks, BLK), F32),
            pltpu.VMEM((tgt_blocks, BLK), F32),
            pltpu.VMEM((blocks, 2 * x.shape[0] + 16, BLK), BF16),
            pltpu.VMEM((tgt_blocks * 8 + 64, BLK), F32),
            pltpu.VMEM((tgt_blocks * 8 + 64, BLK), F32),
            pltpu.VMEM((GROUP, BLK, BLK), F32),
            pltpu.SemaphoreType.DMA((6,)),
        ],
        name="col_pass",
        compiler_params=pltpu.CompilerParams(vmem_limit_bytes=40 * 2**20),
    )(tiles, x, y, lse)


def body(src_points, tgt_points, tgt_potential, support, counts):
    total_src = src_points.shape[1] * lax.axis_size("src")
    total_tgt = tgt_points.shape[1] * lax.axis_size("tgt")
    flat_support = support.transpose(2, 1, 0)
    flat_counts = counts.reshape(-1)
    row_part, tiles = row_pass(flat_support, flat_counts, src_points, tgt_points, tgt_potential.reshape(-1, BLK))
    row_lse = row_exchange("tgt", lax.axis_size("tgt"), 0, row_part)
    src_potential, col_part = col_pass(math.log(total_tgt), tiles, src_points, tgt_points, row_lse)
    new_tgt = col_exchange("src", lax.axis_size("src"), 1, BLUR * math.log(total_src), col_part, tgt_points)
    return src_potential.reshape(-1), new_tgt.reshape(-1)


def solution(mesh):
    return jax.shard_map(
        body,
        mesh=mesh,
        in_specs=(P(None, "src"), P(None, "tgt"), P("tgt"), P("src", "tgt", None), P("src", "tgt")),
        out_specs=(P("src"), P("tgt")),
        check_vma=False,
    )
```

```python
import functools
import math

import jax
import jax.numpy as jnp
from jax import lax
from jax.experimental import pallas as pl
from jax.experimental.pallas import tpu as pltpu
from jax.sharding import PartitionSpec as P

BLK = 128
BLUR = 0.05
NEG = -1e30
TO_LOG2 = math.log2(math.e) / BLUR
FROM_LOG2 = BLUR * math.log(2.0)
GROUP = 48
BUNCH = 8
Y_PARTS = 8
F32 = jnp.float32
BF16 = jnp.bfloat16
MESH = pl.DeviceIdType.MESH


def three_parts(v):
    hi = v.astype(BF16).astype(F32)
    mid = (v - hi).astype(BF16).astype(F32)
    return hi, mid, v - hi - mid


def split_source(x, scale):
    scaled = x.astype(F32) * scale
    hi = scaled.astype(BF16)
    return hi, (scaled - hi.astype(F32)).astype(BF16)


def lane_block(ref, index):
    return ref[:, pl.ds(pl.multiple_of(index * BLK, BLK), BLK)]


def eight_rows(index):
    return pl.ds(pl.multiple_of(index * 8, 8), 8)


def tile_score(left, right):
    return lax.dot_general(left, right, (((0,), (0,)), ((), ())), preferred_element_type=F32)


def tile_sums(score):
    score = score.reshape(BLK // 8, 8, BLK)
    high = jnp.max(score, axis=0)
    return high, jnp.sum(jnp.exp2(score - high[None]), axis=0)


def pipeline(list_ref, steps, score_ref, begin, end):
    for q in range(GROUP):
        score_ref[q] = begin(list_ref[q])

    def step(i, _):
        for q in range(GROUP):
            end(list_ref[i * GROUP + q], score_ref[q])
            score_ref[q] = begin(list_ref[(i + 1) * GROUP + q])
        return 0

    lax.fori_loop(0, steps, step, 0)


def merged_rows(high_ref, total_ref, step, stride):
    at = [pl.ds(step * 8 * stride + s, 8, stride=stride) for s in range(8)]
    highs = [high_ref[a, :] for a in at]
    high = functools.reduce(jnp.maximum, highs)
    total = sum(total_ref[a, :] * jnp.exp2(h - high) for a, h in zip(at, highs))
    return jnp.where(total > 0.0, high + jnp.log2(total), NEG)


def chunk_offset(c, n):
    return lax.rem(n // 2 + lax.div(c + 1, 2) * (1 - 2 * lax.rem(c + 1, 2)) + n, n)


def row_kernel(axis, n, support_any, counts_any, x_any, y_any, g_any, out_ref, support_ref, counts_ref, x_ref, y_ref, g_ref, left_ref, right_ref, score_ref, high_ref, total_ref, part_ref, parts, whole, sem, send_sem, recv_sem, send_sem2, recv_sem2):
    blocks = out_ref.shape[0]
    slots = support_ref.shape[0]
    features = x_ref.shape[0]
    rows = blocks // n
    bunches = rows // BUNCH
    me = lax.axis_index(axis)
    tgt_blocks = g_ref.shape[0]
    wide = y_ref.shape[1] // Y_PARTS
    strips = [pl.ds(i * wide, wide) for i in range(Y_PARTS)]
    pairs = ((support_any, support_ref), (counts_any, counts_ref), (x_any, x_ref), (g_any, g_ref))
    pairs = pairs + tuple((y_any.at[:, strip], y_ref.at[:, strip]) for strip in strips)
    fetches = [pltpu.make_async_copy(a, b, sem.at[i]) for i, (a, b) in enumerate(pairs)]
    for fetch in fetches:
        fetch.start()
    all_here = greet(axis, [lax.rem(me + s, n) for s in range(1, n)])
    ones = jnp.where(lax.broadcasted_iota(jnp.int32, (32, BLK), 0) < 24, 1.0, 0.0).astype(BF16)
    fetches[2].wait()

    def prepare(r, _):
        hi, lo = split_source(lane_block(x_ref, r), TO_LOG2 / features)
        right_ref[r] = jnp.concatenate([hi, lo, ones], axis=0)
        return 0

    lax.fori_loop(0, blocks, prepare, 0, unroll=16)
    for i in (0, 1, 3):
        fetches[i].wait()

    def extend(step, _):
        pot = (TO_LOG2 / 8) * g_ref[eight_rows(step), :]
        for q in range(8):
            t = step * 8 + q
            y = lane_block(y_ref, t)
            yf = y.astype(F32)
            sq = yf * yf
            sq = functools.reduce(jnp.add, [sq[i : i + 8] for i in range(0, features, 8)])
            hi, mid, lo = three_parts(pot[q : q + 1] - (TO_LOG2 / (2 * features)) * sq)
            extra = jnp.concatenate([hi, mid, lo, jnp.zeros((8, BLK), F32)], axis=0).astype(BF16)
            left_ref[t] = jnp.concatenate([y, y, extra], axis=0)
        return 0

    each = tgt_blocks // 8 // Y_PARTS
    for i in range(Y_PARTS):
        fetches[4 + i].wait()
        lax.fori_loop(i * each, (i + 1) * each, extend, 0)
    height = left_ref.shape[1]
    first = lax.broadcasted_iota(jnp.int32, (height, BLK), 0) == 2 * features
    left_ref[tgt_blocks] = jnp.where(first, NEG, 0.0).astype(BF16)

    def chunk(i):
        return pl.ds(pl.multiple_of(i * rows, rows), rows)

    def first_row(i):
        owner = lax.rem(me + chunk_offset(lax.div(i, bunches), n), n)
        return owner * rows + lax.rem(i, bunches) * BUNCH

    def begin(r):
        lefts = [left_ref[jnp.where(k < counts_ref[r], support_ref[k, 0, r], tgt_blocks)] for k in range(slots)]
        return jnp.split(tile_score(jnp.concatenate(lefts, axis=1), right_ref[r]), slots, axis=0)

    def end(q):
        sums = [tile_sums(score_ref[q * slots + k]) for k in range(slots)]
        high = functools.reduce(jnp.maximum, [h for h, _ in sums])
        return high, sum(t * jnp.exp2(h - high) for h, t in sums)

    for q in range(BUNCH):
        for k, score in enumerate(begin(first_row(0) + q)):
            score_ref[q * slots + k] = score

    def send(c):
        target = lax.rem(me + chunk_offset(c, n), n)
        return pltpu.make_async_remote_copy(
            src_ref=part_ref.at[chunk(target)],
            dst_ref=parts.at[c],
            send_sem=send_sem.at[c],
            recv_sem=recv_sem.at[c],
            device_id={axis: target},
            device_id_type=MESH,
        )

    def chunk_step(c, _):
        def step(b, _):
            after = first_row(c * bunches + b + 1)
            for q in range(BUNCH):
                at = eight_rows(b * BUNCH + q)
                high_ref[at, :], total_ref[at, :] = end(q)
                for k, score in enumerate(begin(after + q)):
                    score_ref[q * slots + k] = score
            return 0

        lax.fori_loop(0, bunches, step, 0)
        owner = lax.rem(me + chunk_offset(c, n), n)
        for h in range(rows // 8):
            part_ref[eight_rows(owner * (rows // 8) + h), :] = merged_rows(high_ref, total_ref, h, 8)

        @pl.when(c == 0)
        def _():
            all_here()

        @pl.when(c < n - 1)
        def _():
            send(c).start()

        return 0

    lax.fori_loop(0, n, chunk_step, 0)
    for c in range(n - 1):
        send(jnp.int32(c)).wait_recv()
    whole[chunk(me), :] = combined([part_ref[chunk(me), :]] + [parts[c] for c in range(n - 1)])
    after = [
        remote(whole.at[chunk(me)], whole.at[chunk(me)], send_sem2.at[s], recv_sem2.at[s], axis, lax.rem(me + s + 1, n))
        for s in range(n - 1)
    ]
    for copy in after:
        copy.wait_recv()
    out_ref[...] = whole[...]
    for c in range(n - 1):
        send(jnp.int32(c)).wait_send()
    for copy in after:
        copy.wait_send()


def col_kernel(log_total, support_any, counts_any, x_ref, y_ref, lse_ref, pot_any, out_any, support_ref, counts_ref, list_ref, pot_ref, out_ref, left_ref, high_ref, total_ref, score_ref, sem):
    blocks = pot_ref.shape[0]
    features = x_ref.shape[0]
    tgt_blocks = out_ref.shape[0]

    slots = support_ref.shape[0]
    fetches = [
        pltpu.make_async_copy(a, b, sem.at[4 + i]) for i, (a, b) in enumerate(((support_any, support_ref), (counts_any, counts_ref)))
    ]
    for fetch in fetches:
        fetch.start()

    def clear(step, _):
        at = pl.ds(pl.multiple_of(step * 64, 64), 64)
        high_ref[at, :] = jnp.full((64, BLK), NEG, F32)
        total_ref[at, :] = jnp.zeros((64, BLK), F32)
        return 0

    lax.fori_loop(0, high_ref.shape[0] // 64, clear, 0)
    sub = lax.broadcasted_iota(jnp.int32, (16, BLK), 0)
    ones = jnp.where(sub < 3, 1.0, 0.0).astype(BF16)

    for fetch in fetches:
        fetch.wait()

    def prepare(r, tail):
        for k in range(slots):
            list_ref[tail + k] = support_ref[k, 0, r] * (8 * blocks) + (r * 8 + k)
        x = lane_block(x_ref, r)
        xf = x.astype(F32)
        pot = -FROM_LOG2 * lse_ref[pl.ds(r, 1), :] + BLUR * log_total
        pot_ref[pl.ds(r, 1), :] = pot + jnp.sum(xf * xf, axis=0, keepdims=True) * (1.0 / (2 * features))
        hi, mid, lo = three_parts(TO_LOG2 * pot)
        extra = jnp.where(sub == 0, hi, jnp.where(sub == 1, mid, jnp.where(sub == 2, lo, 0.0))).astype(BF16)
        left_ref[r] = jnp.concatenate([*split_source(x, TO_LOG2 / features), extra], axis=0)
        return tail + counts_ref[r]

    live = lax.fori_loop(0, blocks, prepare, 0, unroll=16)
    for q in range(2 * GROUP):
        list_ref[live + q] = 7
    pot_copy = pltpu.make_async_copy(pot_ref, pot_any, sem.at[6])
    pot_copy.start()

    slot_bits = (8 * blocks).bit_length() - 1

    def begin(code):
        y = lane_block(y_ref, lax.shift_right_logical(code, slot_bits))
        r = lax.shift_right_logical(jnp.bitwise_and(code, 8 * blocks - 1), 3)
        return tile_score(left_ref[r], jnp.concatenate([y, y, ones], axis=0))

    def end(code, score):
        t = lax.shift_right_logical(code, slot_bits)
        own, own_total = tile_sums(score)
        at = eight_rows(jnp.where(jnp.bitwise_and(code, 7) == 7, tgt_blocks, t))
        old = high_ref[at, :]
        high = jnp.maximum(own, old)
        high_ref[at, :] = high
        total_ref[at, :] = own_total * jnp.exp2(own - high) + total_ref[at, :] * jnp.exp2(old - high)

    pipeline(list_ref, lax.div(live + (GROUP - 1), GROUP), score_ref, begin, end)

    def finish(step, _):
        out_ref[eight_rows(step), :] = merged_rows(high_ref, total_ref, step, 8)
        return 0

    pieces = 4
    size = tgt_blocks // pieces
    copies = []
    for piece in range(pieces):
        lax.fori_loop(piece * size // 8, (piece + 1) * size // 8, finish, 0, unroll=8)
        rows = pl.ds(piece * size, size)
        copies.append(pltpu.make_async_copy(out_ref.at[rows], out_any.at[rows], sem.at[piece]))
        copies[-1].start()
    for copy in copies + [pot_copy]:
        copy.wait()


def remote(source, target, send_sem, recv_sem, axis, peer):
    copy = pltpu.make_async_remote_copy(
        src_ref=source,
        dst_ref=target,
        send_sem=send_sem,
        recv_sem=recv_sem,
        device_id={axis: peer},
        device_id_type=MESH,
    )
    copy.start()
    return copy


def greet(axis, peers):
    barrier = pltpu.get_barrier_semaphore()
    for peer in peers:
        pl.semaphore_signal(barrier, inc=1, device_id={axis: peer}, device_id_type=MESH)
    return lambda: pl.semaphore_wait(barrier, len(peers))


def combined(terms):
    high = functools.reduce(jnp.maximum, terms)
    return high + jnp.log2(sum(jnp.exp2(term - high) for term in terms))


PIECES = 4


def col_exchange_kernel(axis, n, shift, part_any, y_any, out_ref, mine_ref, twin_ref, pair_ref, parts, whole, y_ref, sq_ref, local_sem, send_a, recv_a, send_b, recv_b, send_c, recv_c, send_d, recv_d):
    me = lax.axis_index(axis)
    chips = n // 2
    core = lax.rem(me, 2)
    chip = lax.div(me, 2)
    twin = me + 1 - 2 * core
    rows = part_any.shape[0] // n
    half = chips * rows
    size = half // PIECES
    others = [lax.rem(chip + s, chips) for s in range(1, chips)]

    def chunk(where, i):
        return pl.ds(pl.multiple_of((where * chips + i) * rows, rows), rows)

    def local(i):
        return pl.ds(pl.multiple_of(i * rows, rows), rows)

    def piece(where, p):
        return pl.ds(pl.multiple_of(where * half + p * size, size), size)

    all_here = greet(axis, [twin] + [2 * other + core for other in others])
    mine_copy = pltpu.make_async_copy(part_any.at[pl.ds(pl.multiple_of(core * half, half), half)], mine_ref, local_sem.at[0])
    mine_copy.start()
    width = rows * BLK
    own = core * chips + chip
    y_copy = pltpu.make_async_copy(y_any.at[:, pl.ds(pl.multiple_of(own * width, width), width)], y_ref, local_sem.at[1])
    y_copy.start()
    y_copy.wait()
    y = y_ref[...].astype(F32)
    sq = jnp.sum(y * y, axis=0, keepdims=True) * (1.0 / (2 * y.shape[0]))
    for q in range(rows):
        sq_ref[pl.ds(q, 1), :] = sq[:, q * BLK : (q + 1) * BLK]
    mine_copy.wait()
    all_here()

    first = [
        remote(part_any.at[piece(1 - core, p)], twin_ref.at[pl.ds(p * size, size)], send_a.at[p], recv_a.at[p], axis, twin)
        for p in range(PIECES)
    ]
    for p in range(PIECES):
        first[p].wait_recv()
        at = pl.ds(p * size, size)
        pair_ref[at, :] = combined([mine_ref[at, :], twin_ref[at, :]])
    second = [
        remote(pair_ref.at[local(other)], parts.at[s], send_b.at[s], recv_b.at[s], axis, 2 * other + core)
        for s, other in enumerate(others)
    ]
    for copy in second:
        copy.wait_recv()
    result = combined([pair_ref[local(chip), :]] + [parts[s] for s in range(chips - 1)])
    mine = chunk(core, chip)
    whole[mine, :] = sq_ref[...] - FROM_LOG2 * result + shift
    third = [
        remote(whole.at[mine], whole.at[mine], send_c.at[s], recv_c.at[s], axis, 2 * other + core) for s, other in enumerate(others)
    ]
    fourth = [remote(whole.at[mine], whole.at[mine], send_d.at[chips - 1], recv_d.at[chips - 1], axis, twin)]
    for s in range(chips - 1):
        third[s].wait_recv()
        came = chunk(core, lax.rem(chip + chips - 1 - s, chips))
        fourth.append(remote(whole.at[came], whole.at[came], send_d.at[s], recv_d.at[s], axis, twin))
    for copy in fourth:
        copy.wait_recv()
    out_ref[...] = whole[...]
    for copy in first + second + third + fourth:
        copy.wait_send()


def col_exchange(axis, n, cid, shift, part, y):
    rows, chips = part.shape[0] // n, n // 2
    half = chips * rows
    sems = [pltpu.SemaphoreType.DMA((count,)) for count in (2, PIECES, PIECES, chips - 1, chips - 1, chips - 1, chips - 1, chips, chips)]
    return pl.pallas_call(
        functools.partial(col_exchange_kernel, axis, n, shift),
        out_shape=jax.ShapeDtypeStruct(part.shape, F32),
        in_specs=[ANY, ANY],
        out_specs=VMEM,
        scratch_shapes=[
            pltpu.VMEM((half, BLK), F32),
            pltpu.VMEM((half, BLK), F32),
            pltpu.VMEM((half, BLK), F32),
            pltpu.VMEM((chips - 1, rows, BLK), F32),
            pltpu.VMEM(part.shape, F32),
            pltpu.VMEM((y.shape[0], rows * BLK), BF16),
            pltpu.VMEM((rows, BLK), F32),
            *sems,
        ],
        compiler_params=pltpu.CompilerParams(collective_id=cid, has_side_effects=True, vmem_limit_bytes=8 * 2**20),
        name="exchange_" + axis,
    )(part, y)


VMEM = pl.BlockSpec(memory_space=pltpu.VMEM)
SMEM = pl.BlockSpec(memory_space=pltpu.SMEM)
ANY = pl.BlockSpec(memory_space=pl.ANY)


def row_pass(axis, n, cid, support, counts, x, y, g):
    blocks, slots = counts.shape[0], support.shape[0]
    rows = blocks // n
    return pl.pallas_call(
        functools.partial(row_kernel, axis, n),
        out_shape=jax.ShapeDtypeStruct((blocks, BLK), F32),
        in_specs=[ANY] * 5,
        out_specs=VMEM,
        scratch_shapes=[
            pltpu.SMEM(support.shape, jnp.int32),
            pltpu.SMEM(counts.shape, jnp.int32),
            pltpu.VMEM(x.shape, BF16),
            pltpu.VMEM(y.shape, BF16),
            pltpu.VMEM(g.shape, F32),
            pltpu.VMEM((g.shape[0] + 1, 2 * x.shape[0] + 32, BLK), BF16),
            pltpu.VMEM((blocks, 2 * x.shape[0] + 32, BLK), BF16),
            pltpu.VMEM((BUNCH * slots, BLK, BLK), F32),
            pltpu.VMEM((rows * 8, BLK), F32),
            pltpu.VMEM((rows * 8, BLK), F32),
            pltpu.VMEM((blocks, BLK), F32),
            pltpu.VMEM((n - 1, rows, BLK), F32),
            pltpu.VMEM((blocks, BLK), F32),
            pltpu.SemaphoreType.DMA((4 + Y_PARTS,)),
            pltpu.SemaphoreType.DMA((n - 1,)),
            pltpu.SemaphoreType.DMA((n - 1,)),
            pltpu.SemaphoreType.DMA((n - 1,)),
            pltpu.SemaphoreType.DMA((n - 1,)),
        ],
        compiler_params=pltpu.CompilerParams(collective_id=cid, has_side_effects=True, vmem_limit_bytes=40 * 2**20),
        name="row_pass",
    )(support, counts, x, y, g)


def col_pass(log_total, support, counts, x, y, lse):
    blocks, tgt_blocks = lse.shape[0], y.shape[1] // BLK
    return pl.pallas_call(
        functools.partial(col_kernel, log_total),
        out_shape=(jax.ShapeDtypeStruct((blocks, BLK), F32), jax.ShapeDtypeStruct((tgt_blocks, BLK), F32)),
        in_specs=[ANY, ANY, VMEM, VMEM, VMEM],
        out_specs=(ANY, ANY),
        scratch_shapes=[
            pltpu.SMEM(support.shape, jnp.int32),
            pltpu.SMEM(counts.shape, jnp.int32),
            pltpu.SMEM((blocks * support.shape[0] + 2 * GROUP + 8,), jnp.int32),
            pltpu.VMEM((blocks, BLK), F32),
            pltpu.VMEM((tgt_blocks, BLK), F32),
            pltpu.VMEM((blocks, 2 * x.shape[0] + 16, BLK), BF16),
            pltpu.VMEM((tgt_blocks * 8 + 64, BLK), F32),
            pltpu.VMEM((tgt_blocks * 8 + 64, BLK), F32),
            pltpu.VMEM((GROUP, BLK, BLK), F32),
            pltpu.SemaphoreType.DMA((7,)),
        ],
        name="col_pass",
        compiler_params=pltpu.CompilerParams(vmem_limit_bytes=40 * 2**20),
    )(support, counts, x, y, lse)


def body(src_points, tgt_points, tgt_potential, support, counts):
    total_src = src_points.shape[1] * lax.axis_size("src")
    total_tgt = tgt_points.shape[1] * lax.axis_size("tgt")
    flat_support = support.transpose(2, 1, 0)
    flat_counts = counts.reshape(-1)
    pot = tgt_potential.reshape(-1, BLK)
    row_lse = row_pass("tgt", lax.axis_size("tgt"), 0, flat_support, flat_counts, src_points, tgt_points, pot)
    src_potential, col_part = col_pass(math.log(total_tgt), flat_support, flat_counts, src_points, tgt_points, row_lse)
    new_tgt = col_exchange("src", lax.axis_size("src"), 1, BLUR * math.log(total_src), col_part, tgt_points)
    return src_potential.reshape(-1), new_tgt.reshape(-1)


def solution(mesh):
    return jax.shard_map(
        body,
        mesh=mesh,
        in_specs=(P(None, "src"), P(None, "tgt"), P("tgt"), P("src", "tgt", None), P("src", "tgt")),
        out_specs=(P("src"), P("tgt")),
        check_vma=False,
    )
```

```python
import functools
import math

import jax
import jax.numpy as jnp
from jax import lax
from jax.experimental import pallas as pl
from jax.experimental.pallas import tpu as pltpu
from jax.sharding import PartitionSpec as P

BLK = 128
BLUR = 0.05
NEG = -1e30
TO_LOG2 = math.log2(math.e) / BLUR
FROM_LOG2 = BLUR * math.log(2.0)
GROUP = 64
BUNCH = 16
Y_PARTS = 8
F32 = jnp.float32
BF16 = jnp.bfloat16
MESH = pl.DeviceIdType.MESH


def three_parts(v):
    hi = v.astype(BF16).astype(F32)
    mid = (v - hi).astype(BF16).astype(F32)
    return hi, mid, v - hi - mid


def split_source(x, scale):
    scaled = x.astype(F32) * scale
    hi = scaled.astype(BF16)
    return hi, (scaled - hi.astype(F32)).astype(BF16)


def lane_block(ref, index):
    return ref[:, pl.ds(pl.multiple_of(index * BLK, BLK), BLK)]


def eight_rows(index):
    return pl.ds(pl.multiple_of(index * 8, 8), 8)


def tile_score(left, right):
    return lax.dot_general(left, right, (((0,), (0,)), ((), ())), preferred_element_type=F32)


def tile_sums(score):
    score = score.reshape(BLK // 8, 8, BLK)
    high = jnp.max(score, axis=0)
    return high, jnp.sum(jnp.exp2(score - high[None]), axis=0)


def pipeline(list_ref, steps, score_ref, begin, end):
    for q in range(GROUP):
        score_ref[q] = begin(list_ref[q])

    def step(i, _):
        for q in range(GROUP):
            end(list_ref[i * GROUP + q], score_ref[q])
            score_ref[q] = begin(list_ref[(i + 1) * GROUP + q])
        return 0

    lax.fori_loop(0, steps, step, 0)


def merged_rows(high_ref, total_ref, step, stride):
    at = [pl.ds(step * 8 * stride + s, 8, stride=stride) for s in range(8)]
    highs = [high_ref[a, :] for a in at]
    high = functools.reduce(jnp.maximum, highs)
    total = sum(total_ref[a, :] * jnp.exp2(h - high) for a, h in zip(at, highs))
    return jnp.where(total > 0.0, high + jnp.log2(total), NEG)


def chunk_offset(c, n):
    return lax.rem(n // 2 + lax.div(c + 1, 2) * (1 - 2 * lax.rem(c + 1, 2)) + n, n)


def row_kernel(axis, n, support_any, counts_any, x_any, y_any, g_any, out_ref, support_ref, counts_ref, x_ref, y_ref, g_ref, left_ref, right_ref, score_ref, high_ref, total_ref, part_ref, parts, whole, sem, send_sem, recv_sem, send_sem2, recv_sem2):
    blocks = out_ref.shape[0]
    slots = support_ref.shape[0]
    features = x_ref.shape[0]
    rows = blocks // n
    bunches = rows // BUNCH
    me = lax.axis_index(axis)
    tgt_blocks = g_ref.shape[0]
    wide = y_ref.shape[1] // Y_PARTS
    strips = [pl.ds(i * wide, wide) for i in range(Y_PARTS)]
    pairs = ((support_any, support_ref), (counts_any, counts_ref), (x_any, x_ref), (g_any, g_ref))
    pairs = pairs + tuple((y_any.at[:, strip], y_ref.at[:, strip]) for strip in strips)
    fetches = [pltpu.make_async_copy(a, b, sem.at[i]) for i, (a, b) in enumerate(pairs)]
    for fetch in fetches:
        fetch.start()
    all_here = greet(axis, [lax.rem(me + s, n) for s in range(1, n)])
    ones = jnp.where(lax.broadcasted_iota(jnp.int32, (32, BLK), 0) < 24, 1.0, 0.0).astype(BF16)
    fetches[2].wait()

    def prepare(r, _):
        hi, lo = split_source(lane_block(x_ref, r), TO_LOG2 / features)
        right_ref[r] = jnp.concatenate([hi, lo, ones], axis=0)
        return 0

    lax.fori_loop(0, blocks, prepare, 0, unroll=16)
    for i in (0, 1, 3):
        fetches[i].wait()

    def extend(step, _):
        pot = (TO_LOG2 / 8) * g_ref[eight_rows(step), :]
        for q in range(8):
            t = step * 8 + q
            y = lane_block(y_ref, t)
            yf = y.astype(F32)
            sq = yf * yf
            sq = functools.reduce(jnp.add, [sq[i : i + 8] for i in range(0, features, 8)])
            hi, mid, lo = three_parts(pot[q : q + 1] - (TO_LOG2 / (2 * features)) * sq)
            extra = jnp.concatenate([hi, mid, lo, jnp.zeros((8, BLK), F32)], axis=0).astype(BF16)
            left_ref[t] = jnp.concatenate([y, y, extra], axis=0)
        return 0

    each = tgt_blocks // 8 // Y_PARTS
    for i in range(Y_PARTS):
        fetches[4 + i].wait()
        lax.fori_loop(i * each, (i + 1) * each, extend, 0)
    height = left_ref.shape[1]
    first = lax.broadcasted_iota(jnp.int32, (height, BLK), 0) == 2 * features
    left_ref[tgt_blocks] = jnp.where(first, NEG, 0.0).astype(BF16)

    def chunk(i):
        return pl.ds(pl.multiple_of(i * rows, rows), rows)

    def first_row(i):
        owner = lax.rem(me + chunk_offset(lax.div(i, bunches), n), n)
        return owner * rows + lax.rem(i, bunches) * BUNCH

    def begin(r):
        lefts = [left_ref[jnp.where(k < counts_ref[r], support_ref[k, 0, r], tgt_blocks)] for k in range(slots)]
        return jnp.split(tile_score(jnp.concatenate(lefts, axis=1), right_ref[r]), slots, axis=0)

    def end(q):
        sums = [tile_sums(score_ref[q * slots + k]) for k in range(slots)]
        high = functools.reduce(jnp.maximum, [h for h, _ in sums])
        return high, sum(t * jnp.exp2(h - high) for h, t in sums)

    for q in range(BUNCH):
        for k, score in enumerate(begin(first_row(0) + q)):
            score_ref[q * slots + k] = score

    def send(c):
        target = lax.rem(me + chunk_offset(c, n), n)
        return pltpu.make_async_remote_copy(
            src_ref=part_ref.at[chunk(target)],
            dst_ref=parts.at[c],
            send_sem=send_sem.at[c],
            recv_sem=recv_sem.at[c],
            device_id={axis: target},
            device_id_type=MESH,
        )

    def chunk_step(c, _):
        def step(b, _):
            after = first_row(c * bunches + b + 1)
            for q in range(BUNCH):
                at = eight_rows(b * BUNCH + q)
                high_ref[at, :], total_ref[at, :] = end(q)
                for k, score in enumerate(begin(after + q)):
                    score_ref[q * slots + k] = score
            return 0

        lax.fori_loop(0, bunches, step, 0)
        owner = lax.rem(me + chunk_offset(c, n), n)
        for h in range(rows // 8):
            part_ref[eight_rows(owner * (rows // 8) + h), :] = merged_rows(high_ref, total_ref, h, 8)

        @pl.when(c == 0)
        def _():
            all_here()

        @pl.when(c < n - 1)
        def _():
            send(c).start()

        return 0

    lax.fori_loop(0, n, chunk_step, 0)
    for c in range(n - 1):
        send(jnp.int32(c)).wait_recv()
    whole[chunk(me), :] = combined([part_ref[chunk(me), :]] + [parts[c] for c in range(n - 1)])
    after = [
        remote(whole.at[chunk(me)], whole.at[chunk(me)], send_sem2.at[s], recv_sem2.at[s], axis, lax.rem(me + s + 1, n))
        for s in range(n - 1)
    ]
    for copy in after:
        copy.wait_recv()
    out_ref[...] = whole[...]
    for c in range(n - 1):
        send(jnp.int32(c)).wait_send()
    for copy in after:
        copy.wait_send()


def col_kernel(log_total, support_ref, counts_any, x_ref, y_ref, lse_ref, pot_any, out_any, turned_ref, code_ref, counts_ref, list_ref, pot_ref, out_ref, left_ref, high_ref, total_ref, score_ref, sem):
    blocks = pot_ref.shape[0]
    features = x_ref.shape[0]
    tgt_blocks = out_ref.shape[0]

    slots = support_ref.shape[0]
    counts_copy = pltpu.make_async_copy(counts_any, counts_ref, sem.at[4])
    counts_copy.start()
    row = lax.broadcasted_iota(jnp.int32, support_ref.shape, 2)
    slot = lax.broadcasted_iota(jnp.int32, support_ref.shape, 0)
    turned_ref[...] = support_ref[...] * (8 * blocks) + (row * 8 + slot)
    code_copies = [
        pltpu.make_async_copy(turned_ref.at[k, 0], code_ref.at[pl.ds(k * blocks, blocks)], sem.at[7 + k]) for k in range(slots)
    ]
    for copy in code_copies:
        copy.start()

    def clear(step, _):
        at = pl.ds(pl.multiple_of(step * 64, 64), 64)
        high_ref[at, :] = jnp.full((64, BLK), NEG, F32)
        total_ref[at, :] = jnp.zeros((64, BLK), F32)
        return 0

    lax.fori_loop(0, high_ref.shape[0] // 64, clear, 0)
    sub = lax.broadcasted_iota(jnp.int32, (16, BLK), 0)
    ones = jnp.where(sub < 3, 1.0, 0.0).astype(BF16)

    for copy in [counts_copy] + code_copies:
        copy.wait()

    def prepare(r, tail):
        for k in range(slots):
            list_ref[tail + k] = code_ref[k * blocks + r]
        x = lane_block(x_ref, r)
        xf = x.astype(F32)
        pot = -FROM_LOG2 * lse_ref[pl.ds(r, 1), :] + BLUR * log_total
        pot_ref[pl.ds(r, 1), :] = pot + jnp.sum(xf * xf, axis=0, keepdims=True) * (1.0 / (2 * features))
        hi, mid, lo = three_parts(TO_LOG2 * pot)
        extra = jnp.where(sub == 0, hi, jnp.where(sub == 1, mid, jnp.where(sub == 2, lo, 0.0))).astype(BF16)
        left_ref[r] = jnp.concatenate([*split_source(x, TO_LOG2 / features), extra], axis=0)
        return tail + counts_ref[r]

    live = lax.fori_loop(0, blocks, prepare, 0, unroll=16)
    for q in range(2 * GROUP):
        list_ref[live + q] = 7
    pot_copy = pltpu.make_async_copy(pot_ref, pot_any, sem.at[6])
    pot_copy.start()

    slot_bits = (8 * blocks).bit_length() - 1

    def begin(code):
        y = lane_block(y_ref, lax.shift_right_logical(code, slot_bits))
        r = lax.shift_right_logical(jnp.bitwise_and(code, 8 * blocks - 1), 3)
        return tile_score(left_ref[r], jnp.concatenate([y, y, ones], axis=0))

    def end(code, score):
        t = lax.shift_right_logical(code, slot_bits)
        own, own_total = tile_sums(score)
        at = eight_rows(jnp.where(jnp.bitwise_and(code, 7) == 7, tgt_blocks, t))
        old = high_ref[at, :]
        high = jnp.maximum(own, old)
        high_ref[at, :] = high
        total_ref[at, :] = own_total * jnp.exp2(own - high) + total_ref[at, :] * jnp.exp2(old - high)

    pipeline(list_ref, lax.div(live + (GROUP - 1), GROUP), score_ref, begin, end)

    def finish(step, _):
        out_ref[eight_rows(step), :] = merged_rows(high_ref, total_ref, step, 8)
        return 0

    pieces = 4
    size = tgt_blocks // pieces
    copies = []
    for piece in range(pieces):
        lax.fori_loop(piece * size // 8, (piece + 1) * size // 8, finish, 0, unroll=8)
        rows = pl.ds(piece * size, size)
        copies.append(pltpu.make_async_copy(out_ref.at[rows], out_any.at[rows], sem.at[piece]))
        copies[-1].start()
    for copy in copies + [pot_copy]:
        copy.wait()


def remote(source, target, send_sem, recv_sem, axis, peer):
    copy = pltpu.make_async_remote_copy(
        src_ref=source,
        dst_ref=target,
        send_sem=send_sem,
        recv_sem=recv_sem,
        device_id={axis: peer},
        device_id_type=MESH,
    )
    copy.start()
    return copy


def greet(axis, peers):
    barrier = pltpu.get_barrier_semaphore()
    for peer in peers:
        pl.semaphore_signal(barrier, inc=1, device_id={axis: peer}, device_id_type=MESH)
    return lambda: pl.semaphore_wait(barrier, len(peers))


def combined(terms):
    high = functools.reduce(jnp.maximum, terms)
    return high + jnp.log2(sum(jnp.exp2(term - high) for term in terms))


PIECES = 4


def col_exchange_kernel(axis, n, shift, part_any, y_any, out_ref, mine_ref, twin_ref, pair_ref, parts, whole, y_ref, sq_ref, local_sem, send_a, recv_a, send_b, recv_b, send_c, recv_c, send_d, recv_d):
    me = lax.axis_index(axis)
    chips = n // 2
    core = lax.rem(me, 2)
    chip = lax.div(me, 2)
    twin = me + 1 - 2 * core
    rows = part_any.shape[0] // n
    half = chips * rows
    size = half // PIECES
    others = [lax.rem(chip + s, chips) for s in range(1, chips)]

    def chunk(where, i):
        return pl.ds(pl.multiple_of((where * chips + i) * rows, rows), rows)

    def local(i):
        return pl.ds(pl.multiple_of(i * rows, rows), rows)

    def piece(where, p):
        return pl.ds(pl.multiple_of(where * half + p * size, size), size)

    all_here = greet(axis, [twin] + [2 * other + core for other in others])
    mine_copy = pltpu.make_async_copy(part_any.at[pl.ds(pl.multiple_of(core * half, half), half)], mine_ref, local_sem.at[0])
    mine_copy.start()
    width = rows * BLK
    own = core * chips + chip
    y_copy = pltpu.make_async_copy(y_any.at[:, pl.ds(pl.multiple_of(own * width, width), width)], y_ref, local_sem.at[1])
    y_copy.start()
    y_copy.wait()
    y = y_ref[...].astype(F32)
    sq = jnp.sum(y * y, axis=0, keepdims=True) * (1.0 / (2 * y.shape[0]))
    for q in range(rows):
        sq_ref[pl.ds(q, 1), :] = sq[:, q * BLK : (q + 1) * BLK]
    mine_copy.wait()
    all_here()

    first = [
        remote(part_any.at[piece(1 - core, p)], twin_ref.at[pl.ds(p * size, size)], send_a.at[p], recv_a.at[p], axis, twin)
        for p in range(PIECES)
    ]
    for p in range(PIECES):
        first[p].wait_recv()
        at = pl.ds(p * size, size)
        pair_ref[at, :] = combined([mine_ref[at, :], twin_ref[at, :]])
    second = [
        remote(pair_ref.at[local(other)], parts.at[s], send_b.at[s], recv_b.at[s], axis, 2 * other + core)
        for s, other in enumerate(others)
    ]
    for copy in second:
        copy.wait_recv()
    result = combined([pair_ref[local(chip), :]] + [parts[s] for s in range(chips - 1)])
    mine = chunk(core, chip)
    whole[mine, :] = sq_ref[...] - FROM_LOG2 * result + shift
    third = [
        remote(whole.at[mine], whole.at[mine], send_c.at[s], recv_c.at[s], axis, 2 * other + core) for s, other in enumerate(others)
    ]
    fourth = [remote(whole.at[mine], whole.at[mine], send_d.at[chips - 1], recv_d.at[chips - 1], axis, twin)]
    for s in range(chips - 1):
        third[s].wait_recv()
        came = chunk(core, lax.rem(chip + chips - 1 - s, chips))
        fourth.append(remote(whole.at[came], whole.at[came], send_d.at[s], recv_d.at[s], axis, twin))
    for copy in fourth:
        copy.wait_recv()
    out_ref[...] = whole[...]
    for copy in first + second + third + fourth:
        copy.wait_send()


def col_exchange(axis, n, cid, shift, part, y):
    rows, chips = part.shape[0] // n, n // 2
    half = chips * rows
    sems = [pltpu.SemaphoreType.DMA((count,)) for count in (2, PIECES, PIECES, chips - 1, chips - 1, chips - 1, chips - 1, chips, chips)]
    return pl.pallas_call(
        functools.partial(col_exchange_kernel, axis, n, shift),
        out_shape=jax.ShapeDtypeStruct(part.shape, F32),
        in_specs=[ANY, ANY],
        out_specs=VMEM,
        scratch_shapes=[
            pltpu.VMEM((half, BLK), F32),
            pltpu.VMEM((half, BLK), F32),
            pltpu.VMEM((half, BLK), F32),
            pltpu.VMEM((chips - 1, rows, BLK), F32),
            pltpu.VMEM(part.shape, F32),
            pltpu.VMEM((y.shape[0], rows * BLK), BF16),
            pltpu.VMEM((rows, BLK), F32),
            *sems,
        ],
        compiler_params=pltpu.CompilerParams(collective_id=cid, has_side_effects=True, vmem_limit_bytes=8 * 2**20),
        name="exchange_" + axis,
    )(part, y)


VMEM = pl.BlockSpec(memory_space=pltpu.VMEM)
SMEM = pl.BlockSpec(memory_space=pltpu.SMEM)
ANY = pl.BlockSpec(memory_space=pl.ANY)


def row_pass(axis, n, cid, support, counts, x, y, g):
    blocks, slots = counts.shape[0], support.shape[0]
    rows = blocks // n
    return pl.pallas_call(
        functools.partial(row_kernel, axis, n),
        out_shape=jax.ShapeDtypeStruct((blocks, BLK), F32),
        in_specs=[ANY] * 5,
        out_specs=VMEM,
        scratch_shapes=[
            pltpu.SMEM(support.shape, jnp.int32),
            pltpu.SMEM(counts.shape, jnp.int32),
            pltpu.VMEM(x.shape, BF16),
            pltpu.VMEM(y.shape, BF16),
            pltpu.VMEM(g.shape, F32),
            pltpu.VMEM((g.shape[0] + 1, 2 * x.shape[0] + 32, BLK), BF16),
            pltpu.VMEM((blocks, 2 * x.shape[0] + 32, BLK), BF16),
            pltpu.VMEM((BUNCH * slots, BLK, BLK), F32),
            pltpu.VMEM((rows * 8, BLK), F32),
            pltpu.VMEM((rows * 8, BLK), F32),
            pltpu.VMEM((blocks, BLK), F32),
            pltpu.VMEM((n - 1, rows, BLK), F32),
            pltpu.VMEM((blocks, BLK), F32),
            pltpu.SemaphoreType.DMA((4 + Y_PARTS,)),
            pltpu.SemaphoreType.DMA((n - 1,)),
            pltpu.SemaphoreType.DMA((n - 1,)),
            pltpu.SemaphoreType.DMA((n - 1,)),
            pltpu.SemaphoreType.DMA((n - 1,)),
        ],
        compiler_params=pltpu.CompilerParams(collective_id=cid, has_side_effects=True, vmem_limit_bytes=56 * 2**20),
        name="row_pass",
    )(support, counts, x, y, g)


def col_pass(log_total, support, counts, x, y, lse):
    blocks, tgt_blocks = lse.shape[0], y.shape[1] // BLK
    return pl.pallas_call(
        functools.partial(col_kernel, log_total),
        out_shape=(jax.ShapeDtypeStruct((blocks, BLK), F32), jax.ShapeDtypeStruct((tgt_blocks, BLK), F32)),
        in_specs=[VMEM, ANY, VMEM, VMEM, VMEM],
        out_specs=(ANY, ANY),
        scratch_shapes=[
            pltpu.VMEM(support.shape, jnp.int32),
            pltpu.SMEM((blocks * support.shape[0],), jnp.int32),
            pltpu.SMEM(counts.shape, jnp.int32),
            pltpu.SMEM((blocks * support.shape[0] + 2 * GROUP + 8,), jnp.int32),
            pltpu.VMEM((blocks, BLK), F32),
            pltpu.VMEM((tgt_blocks, BLK), F32),
            pltpu.VMEM((blocks, 2 * x.shape[0] + 16, BLK), BF16),
            pltpu.VMEM((tgt_blocks * 8 + 64, BLK), F32),
            pltpu.VMEM((tgt_blocks * 8 + 64, BLK), F32),
            pltpu.VMEM((GROUP, BLK, BLK), F32),
            pltpu.SemaphoreType.DMA((7 + support.shape[0],)),
        ],
        name="col_pass",
        compiler_params=pltpu.CompilerParams(vmem_limit_bytes=40 * 2**20),
    )(support, counts, x, y, lse)


def body(src_points, tgt_points, tgt_potential, support, counts):
    total_src = src_points.shape[1] * lax.axis_size("src")
    total_tgt = tgt_points.shape[1] * lax.axis_size("tgt")
    flat_support = support.transpose(2, 1, 0)
    flat_counts = counts.reshape(-1)
    pot = tgt_potential.reshape(-1, BLK)
    row_lse = row_pass("tgt", lax.axis_size("tgt"), 0, flat_support, flat_counts, src_points, tgt_points, pot)
    src_potential, col_part = col_pass(math.log(total_tgt), flat_support, flat_counts, src_points, tgt_points, row_lse)
    new_tgt = col_exchange("src", lax.axis_size("src"), 1, BLUR * math.log(total_src), col_part, tgt_points)
    return src_potential.reshape(-1), new_tgt.reshape(-1)


def solution(mesh):
    return jax.shard_map(
        body,
        mesh=mesh,
        in_specs=(P(None, "src"), P(None, "tgt"), P("tgt"), P("src", "tgt", None), P("src", "tgt")),
        out_specs=(P("src"), P("tgt")),
        check_vma=False,
    )
```

```python
import functools
import math

import jax
import jax.numpy as jnp
from jax import lax
from jax.experimental import pallas as pl
from jax.experimental.pallas import tpu as pltpu
from jax.sharding import PartitionSpec as P

BLK = 128
BLUR = 0.05
NEG = -1e30
TO_LOG2 = math.log2(math.e) / BLUR
FROM_LOG2 = BLUR * math.log(2.0)
GROUP = 64
BUNCH = 16
Y_PARTS = 8
F32 = jnp.float32
BF16 = jnp.bfloat16
MESH = pl.DeviceIdType.MESH


def three_parts(v):
    hi = v.astype(BF16).astype(F32)
    mid = (v - hi).astype(BF16).astype(F32)
    return hi, mid, v - hi - mid


def split_source(x, scale):
    scaled = x.astype(F32) * scale
    hi = scaled.astype(BF16)
    return hi, (scaled - hi.astype(F32)).astype(BF16)


def lane_block(ref, index):
    return ref[:, pl.ds(pl.multiple_of(index * BLK, BLK), BLK)]


def eight_rows(index):
    return pl.ds(pl.multiple_of(index * 8, 8), 8)


def tile_score(left, right):
    return lax.dot_general(left, right, (((0,), (0,)), ((), ())), preferred_element_type=F32)


def tile_sums(score):
    score = score.reshape(BLK // 8, 8, BLK)
    high = jnp.max(score, axis=0)
    return high, jnp.sum(jnp.exp2(score - high[None]), axis=0)


def pipeline(list_ref, steps, score_ref, begin, end):
    for q in range(GROUP):
        score_ref[q] = begin(list_ref[q])

    def step(i, _):
        for q in range(GROUP):
            end(list_ref[i * GROUP + q], score_ref[q])
            score_ref[q] = begin(list_ref[(i + 1) * GROUP + q])
        return 0

    lax.fori_loop(0, steps, step, 0)


def merged_rows(high_ref, total_ref, step, stride):
    at = [pl.ds(step * 8 * stride + s, 8, stride=stride) for s in range(8)]
    highs = [high_ref[a, :] for a in at]
    high = functools.reduce(jnp.maximum, highs)
    total = sum(total_ref[a, :] * jnp.exp2(h - high) for a, h in zip(at, highs))
    return jnp.where(total > 0.0, high + jnp.log2(total), NEG)


def chunk_offset(c, n):
    return lax.rem(n // 2 + lax.div(c + 1, 2) * (1 - 2 * lax.rem(c + 1, 2)) + n, n)


def row_kernel(axis, n, support_any, counts_any, x_any, y_any, g_any, out_ref, support_ref, counts_ref, x_ref, y_ref, g_ref, left_ref, right_ref, score_ref, high_ref, total_ref, part_ref, parts, whole, sem, send_sem, recv_sem, send_sem2, recv_sem2):
    blocks = out_ref.shape[0]
    slots = support_ref.shape[0]
    features = x_ref.shape[0]
    rows = blocks // n
    bunches = rows // BUNCH
    me = lax.axis_index(axis)
    tgt_blocks = g_ref.shape[0]
    wide = y_ref.shape[1] // Y_PARTS
    strips = [pl.ds(i * wide, wide) for i in range(Y_PARTS)]
    pairs = ((support_any, support_ref), (counts_any, counts_ref), (x_any, x_ref), (g_any, g_ref))
    pairs = pairs + tuple((y_any.at[:, strip], y_ref.at[:, strip]) for strip in strips)
    fetches = [pltpu.make_async_copy(a, b, sem.at[i]) for i, (a, b) in enumerate(pairs)]
    for fetch in fetches:
        fetch.start()
    all_here = greet(axis, [lax.rem(me + s, n) for s in range(1, n)])
    ones = jnp.where(lax.broadcasted_iota(jnp.int32, (32, BLK), 0) < 24, 1.0, 0.0).astype(BF16)
    fetches[2].wait()

    def prepare(r, _):
        hi, lo = split_source(lane_block(x_ref, r), TO_LOG2 / features)
        right_ref[r] = jnp.concatenate([hi, lo, ones], axis=0)
        return 0

    lax.fori_loop(0, blocks, prepare, 0, unroll=16)
    for i in (0, 1, 3):
        fetches[i].wait()

    def extend(step, _):
        pot = (TO_LOG2 / 8) * g_ref[eight_rows(step), :]
        for q in range(8):
            t = step * 8 + q
            y = lane_block(y_ref, t)
            yf = y.astype(F32)
            sq = yf * yf
            sq = functools.reduce(jnp.add, [sq[i : i + 8] for i in range(0, features, 8)])
            hi, mid, lo = three_parts(pot[q : q + 1] - (TO_LOG2 / (2 * features)) * sq)
            extra = jnp.concatenate([hi, mid, lo, jnp.zeros((8, BLK), F32)], axis=0).astype(BF16)
            left_ref[t] = jnp.concatenate([y, y, extra], axis=0)
        return 0

    each = tgt_blocks // 8 // Y_PARTS
    for i in range(Y_PARTS):
        fetches[4 + i].wait()
        lax.fori_loop(i * each, (i + 1) * each, extend, 0)
    height = left_ref.shape[1]
    first = lax.broadcasted_iota(jnp.int32, (height, BLK), 0) == 2 * features
    left_ref[tgt_blocks] = jnp.where(first, NEG, 0.0).astype(BF16)

    def chunk(i):
        return pl.ds(pl.multiple_of(i * rows, rows), rows)

    def first_row(i):
        owner = lax.rem(me + chunk_offset(lax.div(i, bunches), n), n)
        return owner * rows + lax.rem(i, bunches) * BUNCH

    def begin(r):
        lefts = [left_ref[jnp.where(k < counts_ref[r], support_ref[k, 0, r], tgt_blocks)] for k in range(slots)]
        return jnp.split(tile_score(jnp.concatenate(lefts, axis=1), right_ref[r]), slots, axis=0)

    def end(q):
        sums = [tile_sums(score_ref[q * slots + k]) for k in range(slots)]
        high = functools.reduce(jnp.maximum, [h for h, _ in sums])
        return high, sum(t * jnp.exp2(h - high) for h, t in sums)

    for q in range(BUNCH):
        for k, score in enumerate(begin(first_row(0) + q)):
            score_ref[q * slots + k] = score

    def send(c):
        target = lax.rem(me + chunk_offset(c, n), n)
        return pltpu.make_async_remote_copy(
            src_ref=part_ref.at[chunk(target)],
            dst_ref=parts.at[c],
            send_sem=send_sem.at[c],
            recv_sem=recv_sem.at[c],
            device_id={axis: target},
            device_id_type=MESH,
        )

    def chunk_step(c, _):
        def step(b, _):
            after = first_row(c * bunches + b + 1)
            for q in range(BUNCH):
                at = eight_rows(b * BUNCH + q)
                high_ref[at, :], total_ref[at, :] = end(q)
                for k, score in enumerate(begin(after + q)):
                    score_ref[q * slots + k] = score
            return 0

        lax.fori_loop(0, bunches, step, 0)
        owner = lax.rem(me + chunk_offset(c, n), n)
        for h in range(rows // 8):
            part_ref[eight_rows(owner * (rows // 8) + h), :] = merged_rows(high_ref, total_ref, h, 8)

        @pl.when(c == 0)
        def _():
            all_here()

        @pl.when(c < n - 1)
        def _():
            send(c).start()

        return 0

    lax.fori_loop(0, n, chunk_step, 0)
    for c in range(n - 1):
        send(jnp.int32(c)).wait_recv()
    whole[chunk(me), :] = combined([part_ref[chunk(me), :]] + [parts[c] for c in range(n - 1)])
    after = [
        remote(whole.at[chunk(me)], whole.at[chunk(me)], send_sem2.at[s], recv_sem2.at[s], axis, lax.rem(me + chunk_offset(s, n), n))
        for s in range(n - 1)
    ]
    for copy in after:
        copy.wait_recv()
    out_ref[...] = whole[...]
    for c in range(n - 1):
        send(jnp.int32(c)).wait_send()
    for copy in after:
        copy.wait_send()


def col_kernel(log_total, support_ref, counts_any, x_ref, y_ref, lse_ref, pot_any, out_any, turned_ref, code_ref, counts_ref, list_ref, pot_ref, out_ref, left_ref, high_ref, total_ref, score_ref, sem):
    blocks = pot_ref.shape[0]
    features = x_ref.shape[0]
    tgt_blocks = out_ref.shape[0]

    slots = support_ref.shape[0]
    counts_copy = pltpu.make_async_copy(counts_any, counts_ref, sem.at[4])
    counts_copy.start()
    row = lax.broadcasted_iota(jnp.int32, support_ref.shape, 2)
    slot = lax.broadcasted_iota(jnp.int32, support_ref.shape, 0)
    turned_ref[...] = support_ref[...] * (8 * blocks) + (row * 8 + slot)
    code_copies = [
        pltpu.make_async_copy(turned_ref.at[k, 0], code_ref.at[pl.ds(k * blocks, blocks)], sem.at[7 + k]) for k in range(slots)
    ]
    for copy in code_copies:
        copy.start()

    def clear(step, _):
        at = pl.ds(pl.multiple_of(step * 64, 64), 64)
        high_ref[at, :] = jnp.full((64, BLK), NEG, F32)
        total_ref[at, :] = jnp.zeros((64, BLK), F32)
        return 0

    lax.fori_loop(0, high_ref.shape[0] // 64, clear, 0)
    sub = lax.broadcasted_iota(jnp.int32, (16, BLK), 0)
    ones = jnp.where(sub < 3, 1.0, 0.0).astype(BF16)

    for copy in [counts_copy] + code_copies:
        copy.wait()

    def prepare(r, tail):
        for k in range(slots):
            list_ref[tail + k] = code_ref[k * blocks + r]
        x = lane_block(x_ref, r)
        xf = x.astype(F32)
        pot = -FROM_LOG2 * lse_ref[pl.ds(r, 1), :] + BLUR * log_total
        pot_ref[pl.ds(r, 1), :] = pot + jnp.sum(xf * xf, axis=0, keepdims=True) * (1.0 / (2 * features))
        hi, mid, lo = three_parts(TO_LOG2 * pot)
        extra = jnp.where(sub == 0, hi, jnp.where(sub == 1, mid, jnp.where(sub == 2, lo, 0.0))).astype(BF16)
        left_ref[r] = jnp.concatenate([*split_source(x, TO_LOG2 / features), extra], axis=0)
        return tail + counts_ref[r]

    live = lax.fori_loop(0, blocks, prepare, 0, unroll=16)
    for q in range(2 * GROUP):
        list_ref[live + q] = 7
    pot_copy = pltpu.make_async_copy(pot_ref, pot_any, sem.at[6])
    pot_copy.start()

    slot_bits = (8 * blocks).bit_length() - 1

    def begin(code):
        y = lane_block(y_ref, lax.shift_right_logical(code, slot_bits))
        r = lax.shift_right_logical(jnp.bitwise_and(code, 8 * blocks - 1), 3)
        return tile_score(left_ref[r], jnp.concatenate([y, y, ones], axis=0))

    def end(code, score):
        t = lax.shift_right_logical(code, slot_bits)
        own, own_total = tile_sums(score)
        at = eight_rows(jnp.where(jnp.bitwise_and(code, 7) == 7, tgt_blocks, t))
        old = high_ref[at, :]
        high = jnp.maximum(own, old)
        high_ref[at, :] = high
        total_ref[at, :] = own_total * jnp.exp2(own - high) + total_ref[at, :] * jnp.exp2(old - high)

    pipeline(list_ref, lax.div(live + (GROUP - 1), GROUP), score_ref, begin, end)

    def finish(step, _):
        out_ref[eight_rows(step), :] = merged_rows(high_ref, total_ref, step, 8)
        return 0

    pieces = 4
    size = tgt_blocks // pieces
    copies = []
    for piece in range(pieces):
        lax.fori_loop(piece * size // 8, (piece + 1) * size // 8, finish, 0, unroll=8)
        rows = pl.ds(piece * size, size)
        copies.append(pltpu.make_async_copy(out_ref.at[rows], out_any.at[rows], sem.at[piece]))
        copies[-1].start()
    for copy in copies + [pot_copy]:
        copy.wait()


def remote(source, target, send_sem, recv_sem, axis, peer):
    copy = pltpu.make_async_remote_copy(
        src_ref=source,
        dst_ref=target,
        send_sem=send_sem,
        recv_sem=recv_sem,
        device_id={axis: peer},
        device_id_type=MESH,
    )
    copy.start()
    return copy


def greet(axis, peers):
    barrier = pltpu.get_barrier_semaphore()
    for peer in peers:
        pl.semaphore_signal(barrier, inc=1, device_id={axis: peer}, device_id_type=MESH)
    return lambda: pl.semaphore_wait(barrier, len(peers))


def combined(terms):
    high = functools.reduce(jnp.maximum, terms)
    return high + jnp.log2(sum(jnp.exp2(term - high) for term in terms))


PIECES = 4


def hops(step, side):
    return sum(min(d, side - d) for d in step)


def far_count(steps, side):
    return sum(hops(step, side) >= 3 for step in steps)


def col_exchange_kernel(axis, n, shift, part_any, y_any, out_ref, mine_ref, twin_ref, pair_ref, parts, far_parts, whole, y_ref, sq_ref, local_sem, *sems):
    send_a, recv_a, send_b, recv_b, send_c, recv_c, send_d, recv_d, send_e, recv_e, send_f, recv_f = sems
    me = lax.axis_index(axis)
    chips = n // 2
    core = lax.rem(me, 2)
    chip = lax.div(me, 2)
    twin = me + 1 - 2 * core
    rows = part_any.shape[0] // n
    half = chips * rows
    size = half // PIECES
    side = math.isqrt(chips)
    steps = [(dy, dx) for dy in range(side) for dx in range(side)]
    steps = sorted(steps, key=lambda step: -hops(step, side))[:-1]
    far = far_count(steps, side)

    def chip_at(dy, dx):
        return lax.rem(lax.div(chip, side) + side + dy, side) * side + lax.rem(chip + side + dx, side)

    others = [chip_at(dy, dx) for dy, dx in steps]
    senders = [chip_at(-dy, -dx) for dy, dx in steps]

    def chunk(where, i):
        return pl.ds(pl.multiple_of((where * chips + i) * rows, rows), rows)

    def local(i):
        return pl.ds(pl.multiple_of(i * rows, rows), rows)

    def piece(where, p):
        return pl.ds(pl.multiple_of(where * half + p * size, size), size)

    same = [2 * other + core for other in others]
    across = [2 * other + 1 - core for other in others[:far]]
    all_here = greet(axis, same + across + [twin])
    mine_copy = pltpu.make_async_copy(part_any.at[pl.ds(pl.multiple_of(core * half, half), half)], mine_ref, local_sem.at[0])
    mine_copy.start()
    width = rows * BLK
    own = core * chips + chip
    y_copy = pltpu.make_async_copy(y_any.at[:, pl.ds(pl.multiple_of(own * width, width), width)], y_ref, local_sem.at[1])
    y_copy.start()
    y_copy.wait()
    y = y_ref[...].astype(F32)
    sq = jnp.sum(y * y, axis=0, keepdims=True) * (1.0 / (2 * y.shape[0]))
    for q in range(rows):
        sq_ref[pl.ds(q, 1), :] = sq[:, q * BLK : (q + 1) * BLK]
    mine_copy.wait()
    all_here()

    first = [
        remote(part_any.at[piece(1 - core, p)], twin_ref.at[pl.ds(p * size, size)], send_a.at[p], recv_a.at[p], axis, twin)
        for p in range(PIECES)
    ]
    for s in range(far):
        for j, (where, peer) in enumerate(((core, same[s]), (1 - core, across[s]))):
            source = part_any.at[chunk(where, others[s])]
            first.append(remote(source, far_parts.at[2 * s + j], send_e.at[2 * s + j], recv_e.at[2 * s + j], axis, peer))
    for p in range(PIECES):
        first[p].wait_recv()
        at = pl.ds(p * size, size)
        pair_ref[at, :] = combined([mine_ref[at, :], twin_ref[at, :]])
    second = [
        remote(pair_ref.at[local(others[s])], parts.at[s - far], send_b.at[s], recv_b.at[s], axis, same[s])
        for s in range(far, chips - 1)
    ]
    for copy in first[PIECES:] + second:
        copy.wait_recv()
    terms = [parts[s] for s in range(chips - 1 - far)] + [far_parts[s] for s in range(2 * far)]
    result = combined([pair_ref[local(chip), :]] + terms)
    mine = chunk(core, chip)
    whole[mine, :] = sq_ref[...] - FROM_LOG2 * result + shift
    third, crossing = [], []
    for s in range(chips - 1):
        third.append(remote(whole.at[mine], whole.at[mine], send_c.at[s], recv_c.at[s], axis, same[s]))
        if s < far:
            crossing.append(remote(whole.at[mine], whole.at[mine], send_f.at[s], recv_f.at[s], axis, across[s]))
    fourth = [remote(whole.at[mine], whole.at[mine], send_d.at[chips - 1], recv_d.at[chips - 1], axis, twin)]
    for s in reversed(range(far, chips - 1)):
        third[s].wait_recv()
        came = chunk(core, senders[s])
        fourth.append(remote(whole.at[came], whole.at[came], send_d.at[s], recv_d.at[s], axis, twin))
    for copy in third[:far] + crossing + fourth:
        copy.wait_recv()
    out_ref[...] = whole[...]
    for copy in first + second + third + crossing + fourth:
        copy.wait_send()


def col_exchange(axis, n, cid, shift, part, y):
    rows, chips = part.shape[0] // n, n // 2
    half = chips * rows
    side = math.isqrt(chips)
    far = far_count([(dy, dx) for dy in range(side) for dx in range(side)], side)
    counts = (PIECES, chips - 1, chips - 1, chips, 2 * far, far)
    sems = [pltpu.SemaphoreType.DMA((2,))] + [pltpu.SemaphoreType.DMA((count,)) for count in counts for _ in range(2)]
    return pl.pallas_call(
        functools.partial(col_exchange_kernel, axis, n, shift),
        out_shape=jax.ShapeDtypeStruct(part.shape, F32),
        in_specs=[ANY, ANY],
        out_specs=VMEM,
        scratch_shapes=[
            pltpu.VMEM((half, BLK), F32),
            pltpu.VMEM((half, BLK), F32),
            pltpu.VMEM((half, BLK), F32),
            pltpu.VMEM((chips - 1 - far, rows, BLK), F32),
            pltpu.VMEM((2 * far, rows, BLK), F32),
            pltpu.VMEM(part.shape, F32),
            pltpu.VMEM((y.shape[0], rows * BLK), BF16),
            pltpu.VMEM((rows, BLK), F32),
            *sems,
        ],
        compiler_params=pltpu.CompilerParams(collective_id=cid, has_side_effects=True, vmem_limit_bytes=8 * 2**20),
        name="exchange_" + axis,
    )(part, y)


VMEM = pl.BlockSpec(memory_space=pltpu.VMEM)
SMEM = pl.BlockSpec(memory_space=pltpu.SMEM)
ANY = pl.BlockSpec(memory_space=pl.ANY)


def row_pass(axis, n, cid, support, counts, x, y, g):
    blocks, slots = counts.shape[0], support.shape[0]
    rows = blocks // n
    return pl.pallas_call(
        functools.partial(row_kernel, axis, n),
        out_shape=jax.ShapeDtypeStruct((blocks, BLK), F32),
        in_specs=[ANY] * 5,
        out_specs=VMEM,
        scratch_shapes=[
            pltpu.SMEM(support.shape, jnp.int32),
            pltpu.SMEM(counts.shape, jnp.int32),
            pltpu.VMEM(x.shape, BF16),
            pltpu.VMEM(y.shape, BF16),
            pltpu.VMEM(g.shape, F32),
            pltpu.VMEM((g.shape[0] + 1, 2 * x.shape[0] + 32, BLK), BF16),
            pltpu.VMEM((blocks, 2 * x.shape[0] + 32, BLK), BF16),
            pltpu.VMEM((BUNCH * slots, BLK, BLK), F32),
            pltpu.VMEM((rows * 8, BLK), F32),
            pltpu.VMEM((rows * 8, BLK), F32),
            pltpu.VMEM((blocks, BLK), F32),
            pltpu.VMEM((n - 1, rows, BLK), F32),
            pltpu.VMEM((blocks, BLK), F32),
            pltpu.SemaphoreType.DMA((4 + Y_PARTS,)),
            pltpu.SemaphoreType.DMA((n - 1,)),
            pltpu.SemaphoreType.DMA((n - 1,)),
            pltpu.SemaphoreType.DMA((n - 1,)),
            pltpu.SemaphoreType.DMA((n - 1,)),
        ],
        compiler_params=pltpu.CompilerParams(collective_id=cid, has_side_effects=True, vmem_limit_bytes=56 * 2**20),
        name="row_pass",
    )(support, counts, x, y, g)


def col_pass(log_total, support, counts, x, y, lse):
    blocks, tgt_blocks = lse.shape[0], y.shape[1] // BLK
    return pl.pallas_call(
        functools.partial(col_kernel, log_total),
        out_shape=(jax.ShapeDtypeStruct((blocks, BLK), F32), jax.ShapeDtypeStruct((tgt_blocks, BLK), F32)),
        in_specs=[VMEM, ANY, VMEM, VMEM, VMEM],
        out_specs=(ANY, ANY),
        scratch_shapes=[
            pltpu.VMEM(support.shape, jnp.int32),
            pltpu.SMEM((blocks * support.shape[0],), jnp.int32),
            pltpu.SMEM(counts.shape, jnp.int32),
            pltpu.SMEM((blocks * support.shape[0] + 2 * GROUP + 8,), jnp.int32),
            pltpu.VMEM((blocks, BLK), F32),
            pltpu.VMEM((tgt_blocks, BLK), F32),
            pltpu.VMEM((blocks, 2 * x.shape[0] + 16, BLK), BF16),
            pltpu.VMEM((tgt_blocks * 8 + 64, BLK), F32),
            pltpu.VMEM((tgt_blocks * 8 + 64, BLK), F32),
            pltpu.VMEM((GROUP, BLK, BLK), F32),
            pltpu.SemaphoreType.DMA((7 + support.shape[0],)),
        ],
        name="col_pass",
        compiler_params=pltpu.CompilerParams(vmem_limit_bytes=40 * 2**20),
    )(support, counts, x, y, lse)


def body(src_points, tgt_points, tgt_potential, support, counts):
    total_src = src_points.shape[1] * lax.axis_size("src")
    total_tgt = tgt_points.shape[1] * lax.axis_size("tgt")
    flat_support = support.transpose(2, 1, 0)
    flat_counts = counts.reshape(-1)
    pot = tgt_potential.reshape(-1, BLK)
    row_lse = row_pass("tgt", lax.axis_size("tgt"), 0, flat_support, flat_counts, src_points, tgt_points, pot)
    src_potential, col_part = col_pass(math.log(total_tgt), flat_support, flat_counts, src_points, tgt_points, row_lse)
    new_tgt = col_exchange("src", lax.axis_size("src"), 1, BLUR * math.log(total_src), col_part, tgt_points)
    return src_potential.reshape(-1), new_tgt.reshape(-1)


def solution(mesh):
    return jax.shard_map(
        body,
        mesh=mesh,
        in_specs=(P(None, "src"), P(None, "tgt"), P("tgt"), P("src", "tgt", None), P("src", "tgt")),
        out_specs=(P("src"), P("tgt")),
        check_vma=False,
    )
```

```python
import functools
import math

import jax
import jax.numpy as jnp
from jax import lax
from jax.experimental import pallas as pl
from jax.experimental.pallas import tpu as pltpu
from jax.sharding import PartitionSpec as P

BLK = 128
BLUR = 0.05
NEG = -1e30
TO_LOG2 = math.log2(math.e) / BLUR
FROM_LOG2 = BLUR * math.log(2.0)
GROUP = 64
BUNCH = 16
Y_PARTS = 8
F32 = jnp.float32
BF16 = jnp.bfloat16
MESH = pl.DeviceIdType.MESH


def three_parts(v):
    hi = v.astype(BF16).astype(F32)
    mid = (v - hi).astype(BF16).astype(F32)
    return hi, mid, v - hi - mid


def split_source(x, scale):
    scaled = x.astype(F32) * scale
    hi = scaled.astype(BF16)
    return hi, (scaled - hi.astype(F32)).astype(BF16)


def lane_block(ref, index):
    return ref[:, pl.ds(pl.multiple_of(index * BLK, BLK), BLK)]


def eight_rows(index):
    return pl.ds(pl.multiple_of(index * 8, 8), 8)


def tile_score(left, right):
    return lax.dot_general(left, right, (((0,), (0,)), ((), ())), preferred_element_type=F32)


def tile_sums(score):
    score = score.reshape(BLK // 8, 8, BLK)
    high = jnp.max(score, axis=0)
    return high, jnp.sum(jnp.exp2(score - high[None]), axis=0)


def pipeline(list_ref, steps, score_ref, begin, end):
    for q in range(GROUP):
        score_ref[q] = begin(list_ref[q])

    def step(i, _):
        for q in range(GROUP):
            end(list_ref[i * GROUP + q], score_ref[q])
            score_ref[q] = begin(list_ref[(i + 1) * GROUP + q])
        return 0

    step(0, 0)
    lax.fori_loop(1, steps, step, 0)


def merged_rows(high_ref, total_ref, step, stride):
    at = [pl.ds(step * 8 * stride + s, 8, stride=stride) for s in range(8)]
    highs = [high_ref[a, :] for a in at]
    high = functools.reduce(jnp.maximum, highs)
    total = sum(total_ref[a, :] * jnp.exp2(h - high) for a, h in zip(at, highs))
    return jnp.where(total > 0.0, high + jnp.log2(total), NEG)


def chunk_offset(c, n):
    return lax.rem(n // 2 + lax.div(c + 1, 2) * (1 - 2 * lax.rem(c + 1, 2)) + n, n)


def row_kernel(axis, n, support_any, counts_any, x_any, y_any, g_any, out_ref, support_ref, counts_ref, x_ref, y_ref, g_ref, left_ref, right_ref, score_ref, high_ref, total_ref, part_ref, parts, whole, sem, send_sem, recv_sem, send_sem2, recv_sem2):
    blocks = out_ref.shape[0]
    slots = support_ref.shape[0]
    features = x_ref.shape[0]
    rows = blocks // n
    bunches = rows // BUNCH
    me = lax.axis_index(axis)
    tgt_blocks = g_ref.shape[0]
    wide = y_ref.shape[1] // Y_PARTS
    strips = [pl.ds(i * wide, wide) for i in range(Y_PARTS)]
    pairs = ((support_any, support_ref), (counts_any, counts_ref), (x_any, x_ref), (g_any, g_ref))
    pairs = pairs + tuple((y_any.at[:, strip], y_ref.at[:, strip]) for strip in strips)
    fetches = [pltpu.make_async_copy(a, b, sem.at[i]) for i, (a, b) in enumerate(pairs)]
    for fetch in fetches:
        fetch.start()
    all_here = greet(axis, [lax.rem(me + s, n) for s in range(1, n)])
    ones = jnp.where(lax.broadcasted_iota(jnp.int32, (32, BLK), 0) < 24, 1.0, 0.0).astype(BF16)
    fetches[2].wait()

    def prepare(r, _):
        hi, lo = split_source(lane_block(x_ref, r), TO_LOG2 / features)
        right_ref[r] = jnp.concatenate([hi, lo, ones], axis=0)
        return 0

    lax.fori_loop(0, blocks, prepare, 0, unroll=16)
    for i in (0, 1, 3):
        fetches[i].wait()

    def extend(step, _):
        pot = (TO_LOG2 / 8) * g_ref[eight_rows(step), :]
        for q in range(8):
            t = step * 8 + q
            y = lane_block(y_ref, t)
            yf = y.astype(F32)
            sq = yf * yf
            sq = functools.reduce(jnp.add, [sq[i : i + 8] for i in range(0, features, 8)])
            hi, mid, lo = three_parts(pot[q : q + 1] - (TO_LOG2 / (2 * features)) * sq)
            extra = jnp.concatenate([hi, mid, lo, jnp.zeros((8, BLK), F32)], axis=0).astype(BF16)
            left_ref[t] = jnp.concatenate([y, y, extra], axis=0)
        return 0

    each = tgt_blocks // 8 // Y_PARTS
    for i in range(Y_PARTS):
        fetches[4 + i].wait()
        lax.fori_loop(i * each, (i + 1) * each, extend, 0)
    height = left_ref.shape[1]
    first = lax.broadcasted_iota(jnp.int32, (height, BLK), 0) == 2 * features
    left_ref[tgt_blocks] = jnp.where(first, NEG, 0.0).astype(BF16)

    def chunk(i):
        return pl.ds(pl.multiple_of(i * rows, rows), rows)

    def first_row(i):
        owner = lax.rem(me + chunk_offset(lax.div(i, bunches), n), n)
        return owner * rows + lax.rem(i, bunches) * BUNCH

    def begin(r):
        lefts = [left_ref[jnp.where(k < counts_ref[r], support_ref[k, 0, r], tgt_blocks)] for k in range(slots)]
        return jnp.split(tile_score(jnp.concatenate(lefts, axis=1), right_ref[r]), slots, axis=0)

    def end(q):
        sums = [tile_sums(score_ref[q * slots + k]) for k in range(slots)]
        high = functools.reduce(jnp.maximum, [h for h, _ in sums])
        return high, sum(t * jnp.exp2(h - high) for h, t in sums)

    for q in range(BUNCH):
        for k, score in enumerate(begin(first_row(0) + q)):
            score_ref[q * slots + k] = score

    def send(c):
        target = lax.rem(me + chunk_offset(c, n), n)
        return pltpu.make_async_remote_copy(
            src_ref=part_ref.at[chunk(target)],
            dst_ref=parts.at[c],
            send_sem=send_sem.at[c],
            recv_sem=recv_sem.at[c],
            device_id={axis: target},
            device_id_type=MESH,
        )

    def sums(c):
        def step(b):
            after = first_row(c * bunches + b + 1)
            for q in range(BUNCH):
                at = eight_rows(b * BUNCH + q)
                high_ref[at, :], total_ref[at, :] = end(q)
                for k, score in enumerate(begin(after + q)):
                    score_ref[q * slots + k] = score

        for b in range(bunches):
            step(b)

    def settle(c):
        owner = lax.rem(me + chunk_offset(c, n), n)
        for h in range(rows // 8):
            part_ref[eight_rows(owner * (rows // 8) + h), :] = merged_rows(high_ref, total_ref, h, 8)

    def chunk_step(c, _):
        settle(c - 1)
        send(c - 1).start()
        sums(c)
        return 0

    sums(0)
    all_here()
    lax.fori_loop(1, n, chunk_step, 0)
    settle(n - 1)
    for c in range(n - 1):
        send(jnp.int32(c)).wait_recv()
    whole[chunk(me), :] = combined([part_ref[chunk(me), :]] + [parts[c] for c in range(n - 1)])
    after = [
        remote(whole.at[chunk(me)], whole.at[chunk(me)], send_sem2.at[s], recv_sem2.at[s], axis, lax.rem(me + chunk_offset(s, n), n))
        for s in range(n - 1)
    ]
    for copy in after:
        copy.wait_recv()
    out_ref[...] = whole[...]
    for c in range(n - 1):
        send(jnp.int32(c)).wait_send()
    for copy in after:
        copy.wait_send()


def col_kernel(log_total, support_ref, counts_any, x_ref, y_ref, lse_ref, pot_any, out_any, turned_ref, code_ref, counts_ref, list_ref, pot_ref, out_ref, left_ref, high_ref, total_ref, score_ref, sem):
    blocks = pot_ref.shape[0]
    features = x_ref.shape[0]
    tgt_blocks = out_ref.shape[0]

    slots = support_ref.shape[0]
    counts_copy = pltpu.make_async_copy(counts_any, counts_ref, sem.at[4])
    counts_copy.start()
    row = lax.broadcasted_iota(jnp.int32, support_ref.shape, 2)
    slot = lax.broadcasted_iota(jnp.int32, support_ref.shape, 0)
    turned_ref[...] = support_ref[...] * (8 * blocks) + (row * 8 + slot)
    code_copies = [
        pltpu.make_async_copy(turned_ref.at[k, 0], code_ref.at[pl.ds(k * blocks, blocks)], sem.at[7 + k]) for k in range(slots)
    ]
    for copy in code_copies:
        copy.start()

    def clear(step, _):
        at = pl.ds(pl.multiple_of(step * 64, 64), 64)
        high_ref[at, :] = jnp.full((64, BLK), NEG, F32)
        total_ref[at, :] = jnp.zeros((64, BLK), F32)
        return 0

    lax.fori_loop(0, high_ref.shape[0] // 64, clear, 0)
    sub = lax.broadcasted_iota(jnp.int32, (16, BLK), 0)
    ones = jnp.where(sub < 3, 1.0, 0.0).astype(BF16)

    for copy in [counts_copy] + code_copies:
        copy.wait()

    def prepare(r, tail):
        for k in range(slots):
            list_ref[tail + k] = code_ref[k * blocks + r]
        x = lane_block(x_ref, r)
        xf = x.astype(F32)
        pot = -FROM_LOG2 * lse_ref[pl.ds(r, 1), :] + BLUR * log_total
        pot_ref[pl.ds(r, 1), :] = pot + jnp.sum(xf * xf, axis=0, keepdims=True) * (1.0 / (2 * features))
        hi, mid, lo = three_parts(TO_LOG2 * pot)
        extra = jnp.where(sub == 0, hi, jnp.where(sub == 1, mid, jnp.where(sub == 2, lo, 0.0))).astype(BF16)
        left_ref[r] = jnp.concatenate([*split_source(x, TO_LOG2 / features), extra], axis=0)
        return tail + counts_ref[r]

    live = lax.fori_loop(0, blocks, prepare, 0, unroll=16)
    for q in range(2 * GROUP):
        list_ref[live + q] = 7
    pot_copy = pltpu.make_async_copy(pot_ref, pot_any, sem.at[6])
    pot_copy.start()

    slot_bits = (8 * blocks).bit_length() - 1

    def begin(code):
        y = lane_block(y_ref, lax.shift_right_logical(code, slot_bits))
        r = lax.shift_right_logical(jnp.bitwise_and(code, 8 * blocks - 1), 3)
        return tile_score(left_ref[r], jnp.concatenate([y, y, ones], axis=0))

    def end(code, score):
        t = lax.shift_right_logical(code, slot_bits)
        own, own_total = tile_sums(score)
        at = eight_rows(jnp.where(jnp.bitwise_and(code, 7) == 7, tgt_blocks, t))
        old = high_ref[at, :]
        high = jnp.maximum(own, old)
        high_ref[at, :] = high
        total_ref[at, :] = own_total * jnp.exp2(own - high) + total_ref[at, :] * jnp.exp2(old - high)

    pipeline(list_ref, lax.div(live + (GROUP - 1), GROUP), score_ref, begin, end)

    def finish(step, _):
        out_ref[eight_rows(step), :] = merged_rows(high_ref, total_ref, step, 8)
        return 0

    pieces = 4
    size = tgt_blocks // pieces
    copies = []
    for piece in range(pieces):
        lax.fori_loop(piece * size // 8, (piece + 1) * size // 8, finish, 0, unroll=8)
        rows = pl.ds(piece * size, size)
        copies.append(pltpu.make_async_copy(out_ref.at[rows], out_any.at[rows], sem.at[piece]))
        copies[-1].start()
    for copy in copies + [pot_copy]:
        copy.wait()


def remote(source, target, send_sem, recv_sem, axis, peer):
    copy = pltpu.make_async_remote_copy(
        src_ref=source,
        dst_ref=target,
        send_sem=send_sem,
        recv_sem=recv_sem,
        device_id={axis: peer},
        device_id_type=MESH,
    )
    copy.start()
    return copy


def greet(axis, peers):
    barrier = pltpu.get_barrier_semaphore()
    for peer in peers:
        pl.semaphore_signal(barrier, inc=1, device_id={axis: peer}, device_id_type=MESH)
    return lambda: pl.semaphore_wait(barrier, len(peers))


def combined(terms):
    high = functools.reduce(jnp.maximum, terms)
    return high + jnp.log2(sum(jnp.exp2(term - high) for term in terms))


PIECES = 4


def col_exchange_kernel(axis, n, shift, part_any, y_any, out_ref, mine_ref, twin_ref, pair_ref, parts, whole, y_ref, sq_ref, local_sem, send_a, recv_a, send_b, recv_b, send_c, recv_c, send_d, recv_d):
    me = lax.axis_index(axis)
    chips = n // 2
    core = lax.rem(me, 2)
    chip = lax.div(me, 2)
    twin = me + 1 - 2 * core
    rows = part_any.shape[0] // n
    half = chips * rows
    size = half // PIECES
    side = math.isqrt(chips)
    steps = [(dy, dx) for dy in range(side) for dx in range(side)]
    steps = sorted(steps, key=lambda step: -sum(min(d, side - d) for d in step))[:-1]

    def chip_at(dy, dx):
        return lax.rem(lax.div(chip, side) + side + dy, side) * side + lax.rem(chip + side + dx, side)

    others = [chip_at(dy, dx) for dy, dx in steps]
    senders = [chip_at(-dy, -dx) for dy, dx in steps]

    def chunk(where, i):
        return pl.ds(pl.multiple_of((where * chips + i) * rows, rows), rows)

    def local(i):
        return pl.ds(pl.multiple_of(i * rows, rows), rows)

    def piece(where, p):
        return pl.ds(pl.multiple_of(where * half + p * size, size), size)

    all_here = greet(axis, [twin] + [2 * other + core for other in others])
    mine_copy = pltpu.make_async_copy(part_any.at[pl.ds(pl.multiple_of(core * half, half), half)], mine_ref, local_sem.at[0])
    mine_copy.start()
    width = rows * BLK
    own = core * chips + chip
    y_copy = pltpu.make_async_copy(y_any.at[:, pl.ds(pl.multiple_of(own * width, width), width)], y_ref, local_sem.at[1])
    y_copy.start()
    y_copy.wait()
    y = y_ref[...].astype(F32)
    sq = jnp.sum(y * y, axis=0, keepdims=True) * (1.0 / (2 * y.shape[0]))
    for q in range(rows):
        sq_ref[pl.ds(q, 1), :] = sq[:, q * BLK : (q + 1) * BLK]
    mine_copy.wait()
    all_here()

    first = [
        remote(part_any.at[piece(1 - core, p)], twin_ref.at[pl.ds(p * size, size)], send_a.at[p], recv_a.at[p], axis, twin)
        for p in range(PIECES)
    ]
    for p in range(PIECES):
        first[p].wait_recv()
        at = pl.ds(p * size, size)
        pair_ref[at, :] = combined([mine_ref[at, :], twin_ref[at, :]])
    second = [
        remote(pair_ref.at[local(other)], parts.at[s], send_b.at[s], recv_b.at[s], axis, 2 * other + core)
        for s, other in enumerate(others)
    ]
    for copy in second:
        copy.wait_recv()
    result = combined([pair_ref[local(chip), :]] + [parts[s] for s in range(chips - 1)])
    mine = chunk(core, chip)
    whole[mine, :] = sq_ref[...] - FROM_LOG2 * result + shift
    third = [
        remote(whole.at[mine], whole.at[mine], send_c.at[s], recv_c.at[s], axis, 2 * other + core) for s, other in enumerate(others)
    ]
    fourth = [remote(whole.at[mine], whole.at[mine], send_d.at[chips - 1], recv_d.at[chips - 1], axis, twin)]
    for s in reversed(range(chips - 1)):
        third[s].wait_recv()
        came = chunk(core, senders[s])
        fourth.append(remote(whole.at[came], whole.at[came], send_d.at[s], recv_d.at[s], axis, twin))
    for copy in fourth:
        copy.wait_recv()
    out_ref[...] = whole[...]
    for copy in first + second + third + fourth:
        copy.wait_send()


def col_exchange(axis, n, cid, shift, part, y):
    rows, chips = part.shape[0] // n, n // 2
    half = chips * rows
    sems = [pltpu.SemaphoreType.DMA((count,)) for count in (2, PIECES, PIECES, chips - 1, chips - 1, chips - 1, chips - 1, chips, chips)]
    return pl.pallas_call(
        functools.partial(col_exchange_kernel, axis, n, shift),
        out_shape=jax.ShapeDtypeStruct(part.shape, F32),
        in_specs=[ANY, ANY],
        out_specs=VMEM,
        scratch_shapes=[
            pltpu.VMEM((half, BLK), F32),
            pltpu.VMEM((half, BLK), F32),
            pltpu.VMEM((half, BLK), F32),
            pltpu.VMEM((chips - 1, rows, BLK), F32),
            pltpu.VMEM(part.shape, F32),
            pltpu.VMEM((y.shape[0], rows * BLK), BF16),
            pltpu.VMEM((rows, BLK), F32),
            *sems,
        ],
        compiler_params=pltpu.CompilerParams(collective_id=cid, has_side_effects=True, vmem_limit_bytes=8 * 2**20),
        name="exchange_" + axis,
    )(part, y)


VMEM = pl.BlockSpec(memory_space=pltpu.VMEM)
SMEM = pl.BlockSpec(memory_space=pltpu.SMEM)
ANY = pl.BlockSpec(memory_space=pl.ANY)


def row_pass(axis, n, cid, support, counts, x, y, g):
    blocks, slots = counts.shape[0], support.shape[0]
    rows = blocks // n
    return pl.pallas_call(
        functools.partial(row_kernel, axis, n),
        out_shape=jax.ShapeDtypeStruct((blocks, BLK), F32),
        in_specs=[ANY] * 5,
        out_specs=VMEM,
        scratch_shapes=[
            pltpu.SMEM(support.shape, jnp.int32),
            pltpu.SMEM(counts.shape, jnp.int32),
            pltpu.VMEM(x.shape, BF16),
            pltpu.VMEM(y.shape, BF16),
            pltpu.VMEM(g.shape, F32),
            pltpu.VMEM((g.shape[0] + 1, 2 * x.shape[0] + 32, BLK), BF16),
            pltpu.VMEM((blocks, 2 * x.shape[0] + 32, BLK), BF16),
            pltpu.VMEM((BUNCH * slots, BLK, BLK), F32),
            pltpu.VMEM((rows * 8, BLK), F32),
            pltpu.VMEM((rows * 8, BLK), F32),
            pltpu.VMEM((blocks, BLK), F32),
            pltpu.VMEM((n - 1, rows, BLK), F32),
            pltpu.VMEM((blocks, BLK), F32),
            pltpu.SemaphoreType.DMA((4 + Y_PARTS,)),
            pltpu.SemaphoreType.DMA((n - 1,)),
            pltpu.SemaphoreType.DMA((n - 1,)),
            pltpu.SemaphoreType.DMA((n - 1,)),
            pltpu.SemaphoreType.DMA((n - 1,)),
        ],
        compiler_params=pltpu.CompilerParams(collective_id=cid, has_side_effects=True, vmem_limit_bytes=56 * 2**20),
        name="row_pass",
    )(support, counts, x, y, g)


def col_pass(log_total, support, counts, x, y, lse):
    blocks, tgt_blocks = lse.shape[0], y.shape[1] // BLK
    return pl.pallas_call(
        functools.partial(col_kernel, log_total),
        out_shape=(jax.ShapeDtypeStruct((blocks, BLK), F32), jax.ShapeDtypeStruct((tgt_blocks, BLK), F32)),
        in_specs=[VMEM, ANY, VMEM, VMEM, VMEM],
        out_specs=(ANY, ANY),
        scratch_shapes=[
            pltpu.VMEM(support.shape, jnp.int32),
            pltpu.SMEM((blocks * support.shape[0],), jnp.int32),
            pltpu.SMEM(counts.shape, jnp.int32),
            pltpu.SMEM((blocks * support.shape[0] + 2 * GROUP + 8,), jnp.int32),
            pltpu.VMEM((blocks, BLK), F32),
            pltpu.VMEM((tgt_blocks, BLK), F32),
            pltpu.VMEM((blocks, 2 * x.shape[0] + 16, BLK), BF16),
            pltpu.VMEM((tgt_blocks * 8 + 64, BLK), F32),
            pltpu.VMEM((tgt_blocks * 8 + 64, BLK), F32),
            pltpu.VMEM((GROUP, BLK, BLK), F32),
            pltpu.SemaphoreType.DMA((7 + support.shape[0],)),
        ],
        name="col_pass",
        compiler_params=pltpu.CompilerParams(vmem_limit_bytes=40 * 2**20),
    )(support, counts, x, y, lse)


def body(src_points, tgt_points, tgt_potential, support, counts):
    total_src = src_points.shape[1] * lax.axis_size("src")
    total_tgt = tgt_points.shape[1] * lax.axis_size("tgt")
    flat_support = support.transpose(2, 1, 0)
    flat_counts = counts.reshape(-1)
    pot = tgt_potential.reshape(-1, BLK)
    row_lse = row_pass("tgt", lax.axis_size("tgt"), 0, flat_support, flat_counts, src_points, tgt_points, pot)
    src_potential, col_part = col_pass(math.log(total_tgt), flat_support, flat_counts, src_points, tgt_points, row_lse)
    new_tgt = col_exchange("src", lax.axis_size("src"), 1, BLUR * math.log(total_src), col_part, tgt_points)
    return src_potential.reshape(-1), new_tgt.reshape(-1)


def solution(mesh):
    return jax.shard_map(
        body,
        mesh=mesh,
        in_specs=(P(None, "src"), P(None, "tgt"), P("tgt"), P("src", "tgt", None), P("src", "tgt")),
        out_specs=(P("src"), P("tgt")),
        check_vma=False,
    )
```

```python
import functools
import math

import jax
import jax.numpy as jnp
from jax import lax
from jax.experimental import pallas as pl
from jax.experimental.pallas import tpu as pltpu
from jax.sharding import PartitionSpec as P

BLK = 128
BLUR = 0.05
NEG = -1e30
TO_LOG2 = math.log2(math.e) / BLUR
FROM_LOG2 = BLUR * math.log(2.0)
GROUP = 64
BUNCH = 16
Y_PARTS = 8
F32 = jnp.float32
BF16 = jnp.bfloat16
MESH = pl.DeviceIdType.MESH


def three_parts(v):
    hi = v.astype(BF16).astype(F32)
    mid = (v - hi).astype(BF16).astype(F32)
    return hi, mid, v - hi - mid


def split_source(x, scale):
    scaled = x.astype(F32) * scale
    hi = scaled.astype(BF16)
    return hi, (scaled - hi.astype(F32)).astype(BF16)


def lane_block(ref, index):
    return ref[:, pl.ds(pl.multiple_of(index * BLK, BLK), BLK)]


def eight_rows(index):
    return pl.ds(pl.multiple_of(index * 8, 8), 8)


def tile_score(left, right):
    return lax.dot_general(left, right, (((0,), (0,)), ((), ())), preferred_element_type=F32)


def tile_sums(score):
    score = score.reshape(BLK // 8, 8, BLK)
    high = jnp.max(score, axis=0)
    return high, jnp.sum(jnp.exp2(score - high[None]), axis=0)


def pipeline(list_ref, steps, score_ref, begin, end):
    for q in range(GROUP):
        score_ref[q] = begin(list_ref[q])

    def step(i, _):
        for q in range(GROUP):
            end(list_ref[i * GROUP + q], score_ref[q])
            score_ref[q] = begin(list_ref[(i + 1) * GROUP + q])
        return 0

    step(0, 0)
    lax.fori_loop(1, steps, step, 0)


def merged_rows(high_ref, total_ref, step, stride):
    at = [pl.ds(step * 8 * stride + s, 8, stride=stride) for s in range(8)]
    highs = [high_ref[a, :] for a in at]
    high = functools.reduce(jnp.maximum, highs)
    total = sum(total_ref[a, :] * jnp.exp2(h - high) for a, h in zip(at, highs))
    return jnp.where(total > 0.0, high + jnp.log2(total), NEG)


def chunk_offset(c, n):
    return lax.rem(n // 2 + lax.div(c + 1, 2) * (1 - 2 * lax.rem(c + 1, 2)) + n, n)


def row_kernel(axis, n, support_any, counts_any, x_any, y_any, g_any, out_ref, support_ref, counts_ref, x_ref, y_ref, g_ref, left_ref, score_ref, high_ref, total_ref, part_ref, parts, whole, sem, send_sem, recv_sem, send_sem2, recv_sem2):
    blocks = out_ref.shape[0]
    slots = support_ref.shape[0]
    features = x_ref.shape[0]
    rows = blocks // n
    bunches = rows // BUNCH
    me = lax.axis_index(axis)
    tgt_blocks = g_ref.shape[0]
    wide = y_ref.shape[1] // Y_PARTS
    strips = [pl.ds(i * wide, wide) for i in range(Y_PARTS)]
    pairs = ((support_any, support_ref), (counts_any, counts_ref), (g_any, g_ref))
    pairs = pairs + tuple((y_any.at[:, strip], y_ref.at[:, strip]) for strip in strips) + ((x_any, x_ref),)
    fetches = [pltpu.make_async_copy(a, b, sem.at[i]) for i, (a, b) in enumerate(pairs)]
    for fetch in fetches:
        fetch.start()
    all_here = greet(axis, [lax.rem(me + s, n) for s in range(1, n)])
    ones = jnp.where(lax.broadcasted_iota(jnp.int32, (32, BLK), 0) < 24, 1.0, 0.0).astype(BF16)
    for i in range(3):
        fetches[i].wait()

    def extend(step, _):
        pot = (TO_LOG2 / 8) * g_ref[eight_rows(step), :]
        for q in range(8):
            t = step * 8 + q
            y = lane_block(y_ref, t)
            yf = y.astype(F32)
            sq = yf * yf
            sq = functools.reduce(jnp.add, [sq[i : i + 8] for i in range(0, features, 8)])
            hi, mid, lo = three_parts(pot[q : q + 1] - (TO_LOG2 / (2 * features)) * sq)
            extra = jnp.concatenate([hi, mid, lo, jnp.zeros((8, BLK), F32)], axis=0).astype(BF16)
            left_ref[t] = jnp.concatenate([y, y, extra], axis=0)
        return 0

    each = tgt_blocks // 8 // Y_PARTS
    for i in range(Y_PARTS):
        fetches[3 + i].wait()
        lax.fori_loop(i * each, (i + 1) * each, extend, 0, unroll=2)
    fetches[3 + Y_PARTS].wait()
    height = left_ref.shape[1]
    first = lax.broadcasted_iota(jnp.int32, (height, BLK), 0) == 2 * features
    left_ref[tgt_blocks] = jnp.where(first, NEG, 0.0).astype(BF16)

    def chunk(i):
        return pl.ds(pl.multiple_of(i * rows, rows), rows)

    def first_row(i):
        owner = lax.rem(me + chunk_offset(lax.div(i, bunches), n), n)
        return owner * rows + lax.rem(i, bunches) * BUNCH

    def begin(r):
        lefts = [left_ref[jnp.where(k < counts_ref[r], support_ref[k, 0, r], tgt_blocks)] for k in range(slots)]
        right = jnp.concatenate([*split_source(lane_block(x_ref, r), TO_LOG2 / features), ones], axis=0)
        return jnp.split(tile_score(jnp.concatenate(lefts, axis=1), right), slots, axis=0)

    def end(q):
        sums = [tile_sums(score_ref[q * slots + k]) for k in range(slots)]
        high = functools.reduce(jnp.maximum, [h for h, _ in sums])
        return high, sum(t * jnp.exp2(h - high) for h, t in sums)

    for q in range(BUNCH):
        for k, score in enumerate(begin(first_row(0) + q)):
            score_ref[q * slots + k] = score

    def send(c):
        target = lax.rem(me + chunk_offset(c, n), n)
        return pltpu.make_async_remote_copy(
            src_ref=part_ref.at[chunk(target)],
            dst_ref=parts.at[c],
            send_sem=send_sem.at[c],
            recv_sem=recv_sem.at[c],
            device_id={axis: target},
            device_id_type=MESH,
        )

    def sums(c):
        def step(b):
            after = first_row(c * bunches + b + 1)
            for q in range(BUNCH):
                at = eight_rows(b * BUNCH + q)
                high_ref[at, :], total_ref[at, :] = end(q)
                for k, score in enumerate(begin(after + q)):
                    score_ref[q * slots + k] = score

        for b in range(bunches):
            step(b)

    def settle(c):
        owner = lax.rem(me + chunk_offset(c, n), n)
        for h in range(rows // 8):
            part_ref[eight_rows(owner * (rows // 8) + h), :] = merged_rows(high_ref, total_ref, h, 8)

    def chunk_step(c, _):
        settle(c - 1)
        send(c - 1).start()
        sums(c)
        return 0

    sums(0)
    all_here()
    lax.fori_loop(1, n, chunk_step, 0)
    settle(n - 1)
    for c in range(n - 1):
        send(jnp.int32(c)).wait_recv()
    whole[chunk(me), :] = combined([part_ref[chunk(me), :]] + [parts[c] for c in range(n - 1)])
    after = [
        remote(whole.at[chunk(me)], whole.at[chunk(me)], send_sem2.at[s], recv_sem2.at[s], axis, lax.rem(me + chunk_offset(s, n), n))
        for s in range(n - 1)
    ]
    for copy in after:
        copy.wait_recv()
    out_ref[...] = whole[...]
    for c in range(n - 1):
        send(jnp.int32(c)).wait_send()
    for copy in after:
        copy.wait_send()


def col_kernel(log_total, support_ref, counts_any, x_ref, y_ref, lse_ref, pot_any, out_any, turned_ref, code_ref, counts_ref, list_ref, pot_ref, out_ref, left_ref, high_ref, total_ref, score_ref, sem):
    blocks = pot_ref.shape[0]
    features = x_ref.shape[0]
    tgt_blocks = out_ref.shape[0]

    slots = support_ref.shape[0]
    counts_copy = pltpu.make_async_copy(counts_any, counts_ref, sem.at[4])
    counts_copy.start()
    row = lax.broadcasted_iota(jnp.int32, support_ref.shape, 2)
    slot = lax.broadcasted_iota(jnp.int32, support_ref.shape, 0)
    turned_ref[...] = support_ref[...] * (8 * blocks) + (row * 8 + slot)
    code_copies = [
        pltpu.make_async_copy(turned_ref.at[k, 0], code_ref.at[pl.ds(k * blocks, blocks)], sem.at[7 + k]) for k in range(slots)
    ]
    for copy in code_copies:
        copy.start()

    def clear(step, _):
        at = pl.ds(pl.multiple_of(step * 64, 64), 64)
        high_ref[at, :] = jnp.full((64, BLK), NEG, F32)
        total_ref[at, :] = jnp.zeros((64, BLK), F32)
        return 0

    lax.fori_loop(0, high_ref.shape[0] // 64, clear, 0)
    sub = lax.broadcasted_iota(jnp.int32, (16, BLK), 0)
    ones = jnp.where(sub < 3, 1.0, 0.0).astype(BF16)

    for copy in [counts_copy] + code_copies:
        copy.wait()

    def prepare(r, tail):
        for k in range(slots):
            list_ref[tail + k] = code_ref[k * blocks + r]
        x = lane_block(x_ref, r)
        xf = x.astype(F32)
        pot = -FROM_LOG2 * lse_ref[pl.ds(r, 1), :] + BLUR * log_total
        pot_ref[pl.ds(r, 1), :] = pot + jnp.sum(xf * xf, axis=0, keepdims=True) * (1.0 / (2 * features))
        hi, mid, lo = three_parts(TO_LOG2 * pot)
        extra = jnp.where(sub == 0, hi, jnp.where(sub == 1, mid, jnp.where(sub == 2, lo, 0.0))).astype(BF16)
        left_ref[r] = jnp.concatenate([*split_source(x, TO_LOG2 / features), extra], axis=0)
        return tail + counts_ref[r]

    live = lax.fori_loop(0, blocks, prepare, 0, unroll=16)
    for q in range(2 * GROUP):
        list_ref[live + q] = 7
    pot_copy = pltpu.make_async_copy(pot_ref, pot_any, sem.at[6])
    pot_copy.start()

    slot_bits = (8 * blocks).bit_length() - 1

    def begin(code):
        y = lane_block(y_ref, lax.shift_right_logical(code, slot_bits))
        r = lax.shift_right_logical(jnp.bitwise_and(code, 8 * blocks - 1), 3)
        return tile_score(left_ref[r], jnp.concatenate([y, y, ones], axis=0))

    def end(code, score):
        t = lax.shift_right_logical(code, slot_bits)
        own, own_total = tile_sums(score)
        at = eight_rows(jnp.where(jnp.bitwise_and(code, 7) == 7, tgt_blocks, t))
        old = high_ref[at, :]
        high = jnp.maximum(own, old)
        high_ref[at, :] = high
        total_ref[at, :] = own_total * jnp.exp2(own - high) + total_ref[at, :] * jnp.exp2(old - high)

    pipeline(list_ref, lax.div(live + (GROUP - 1), GROUP), score_ref, begin, end)

    def finish(step, _):
        out_ref[eight_rows(step), :] = merged_rows(high_ref, total_ref, step, 8)
        return 0

    pieces = 4
    size = tgt_blocks // pieces
    copies = []
    for piece in range(pieces):
        lax.fori_loop(piece * size // 8, (piece + 1) * size // 8, finish, 0, unroll=8)
        rows = pl.ds(piece * size, size)
        copies.append(pltpu.make_async_copy(out_ref.at[rows], out_any.at[rows], sem.at[piece]))
        copies[-1].start()
    for copy in copies + [pot_copy]:
        copy.wait()


def remote(source, target, send_sem, recv_sem, axis, peer):
    copy = pltpu.make_async_remote_copy(
        src_ref=source,
        dst_ref=target,
        send_sem=send_sem,
        recv_sem=recv_sem,
        device_id={axis: peer},
        device_id_type=MESH,
    )
    copy.start()
    return copy


def greet(axis, peers):
    barrier = pltpu.get_barrier_semaphore()
    for peer in peers:
        pl.semaphore_signal(barrier, inc=1, device_id={axis: peer}, device_id_type=MESH)
    return lambda: pl.semaphore_wait(barrier, len(peers))


def combined(terms):
    high = functools.reduce(jnp.maximum, terms)
    return high + jnp.log2(sum(jnp.exp2(term - high) for term in terms))


PIECES = 4


def col_exchange_kernel(axis, n, shift, part_any, y_any, out_ref, mine_ref, twin_ref, pair_ref, parts, whole, y_ref, sq_ref, local_sem, send_a, recv_a, send_b, recv_b, send_c, recv_c, send_d, recv_d):
    me = lax.axis_index(axis)
    chips = n // 2
    core = lax.rem(me, 2)
    chip = lax.div(me, 2)
    twin = me + 1 - 2 * core
    rows = part_any.shape[0] // n
    half = chips * rows
    size = half // PIECES
    side = math.isqrt(chips)
    steps = [(dy, dx) for dy in range(side) for dx in range(side)]
    steps = sorted(steps, key=lambda step: -sum(min(d, side - d) for d in step))[:-1]

    def chip_at(dy, dx):
        return lax.rem(lax.div(chip, side) + side + dy, side) * side + lax.rem(chip + side + dx, side)

    others = [chip_at(dy, dx) for dy, dx in steps]
    senders = [chip_at(-dy, -dx) for dy, dx in steps]

    def chunk(where, i):
        return pl.ds(pl.multiple_of((where * chips + i) * rows, rows), rows)

    def local(i):
        return pl.ds(pl.multiple_of(i * rows, rows), rows)

    def piece(where, p):
        return pl.ds(pl.multiple_of(where * half + p * size, size), size)

    all_here = greet(axis, [twin] + [2 * other + core for other in others])
    mine_copy = pltpu.make_async_copy(part_any.at[pl.ds(pl.multiple_of(core * half, half), half)], mine_ref, local_sem.at[0])
    mine_copy.start()
    width = rows * BLK
    own = core * chips + chip
    y_copy = pltpu.make_async_copy(y_any.at[:, pl.ds(pl.multiple_of(own * width, width), width)], y_ref, local_sem.at[1])
    y_copy.start()
    y_copy.wait()
    y = y_ref[...].astype(F32)
    sq = jnp.sum(y * y, axis=0, keepdims=True) * (1.0 / (2 * y.shape[0]))
    for q in range(rows):
        sq_ref[pl.ds(q, 1), :] = sq[:, q * BLK : (q + 1) * BLK]
    mine_copy.wait()
    all_here()

    first = [
        remote(part_any.at[piece(1 - core, p)], twin_ref.at[pl.ds(p * size, size)], send_a.at[p], recv_a.at[p], axis, twin)
        for p in range(PIECES)
    ]
    for p in range(PIECES):
        first[p].wait_recv()
        at = pl.ds(p * size, size)
        pair_ref[at, :] = combined([mine_ref[at, :], twin_ref[at, :]])
    second = [
        remote(pair_ref.at[local(other)], parts.at[s], send_b.at[s], recv_b.at[s], axis, 2 * other + core)
        for s, other in enumerate(others)
    ]
    for copy in second:
        copy.wait_recv()
    result = combined([pair_ref[local(chip), :]] + [parts[s] for s in range(chips - 1)])
    mine = chunk(core, chip)
    whole[mine, :] = sq_ref[...] - FROM_LOG2 * result + shift
    third = [
        remote(whole.at[mine], whole.at[mine], send_c.at[s], recv_c.at[s], axis, 2 * other + core) for s, other in enumerate(others)
    ]
    fourth = [remote(whole.at[mine], whole.at[mine], send_d.at[chips - 1], recv_d.at[chips - 1], axis, twin)]
    for s in reversed(range(chips - 1)):
        third[s].wait_recv()
        came = chunk(core, senders[s])
        fourth.append(remote(whole.at[came], whole.at[came], send_d.at[s], recv_d.at[s], axis, twin))
    for copy in fourth:
        copy.wait_recv()
    out_ref[...] = whole[...]
    for copy in first + second + third + fourth:
        copy.wait_send()


def col_exchange(axis, n, cid, shift, part, y):
    rows, chips = part.shape[0] // n, n // 2
    half = chips * rows
    sems = [pltpu.SemaphoreType.DMA((count,)) for count in (2, PIECES, PIECES, chips - 1, chips - 1, chips - 1, chips - 1, chips, chips)]
    return pl.pallas_call(
        functools.partial(col_exchange_kernel, axis, n, shift),
        out_shape=jax.ShapeDtypeStruct(part.shape, F32),
        in_specs=[ANY, ANY],
        out_specs=VMEM,
        scratch_shapes=[
            pltpu.VMEM((half, BLK), F32),
            pltpu.VMEM((half, BLK), F32),
            pltpu.VMEM((half, BLK), F32),
            pltpu.VMEM((chips - 1, rows, BLK), F32),
            pltpu.VMEM(part.shape, F32),
            pltpu.VMEM((y.shape[0], rows * BLK), BF16),
            pltpu.VMEM((rows, BLK), F32),
            *sems,
        ],
        compiler_params=pltpu.CompilerParams(collective_id=cid, has_side_effects=True, vmem_limit_bytes=8 * 2**20),
        name="exchange_" + axis,
    )(part, y)


VMEM = pl.BlockSpec(memory_space=pltpu.VMEM)
SMEM = pl.BlockSpec(memory_space=pltpu.SMEM)
ANY = pl.BlockSpec(memory_space=pl.ANY)


def row_pass(axis, n, cid, support, counts, x, y, g):
    blocks, slots = counts.shape[0], support.shape[0]
    rows = blocks // n
    return pl.pallas_call(
        functools.partial(row_kernel, axis, n),
        out_shape=jax.ShapeDtypeStruct((blocks, BLK), F32),
        in_specs=[ANY] * 5,
        out_specs=VMEM,
        scratch_shapes=[
            pltpu.SMEM(support.shape, jnp.int32),
            pltpu.SMEM(counts.shape, jnp.int32),
            pltpu.VMEM(x.shape, BF16),
            pltpu.VMEM(y.shape, BF16),
            pltpu.VMEM(g.shape, F32),
            pltpu.VMEM((g.shape[0] + 1, 2 * x.shape[0] + 32, BLK), BF16),
            pltpu.VMEM((BUNCH * slots, BLK, BLK), F32),
            pltpu.VMEM((rows * 8, BLK), F32),
            pltpu.VMEM((rows * 8, BLK), F32),
            pltpu.VMEM((blocks, BLK), F32),
            pltpu.VMEM((n - 1, rows, BLK), F32),
            pltpu.VMEM((blocks, BLK), F32),
            pltpu.SemaphoreType.DMA((4 + Y_PARTS,)),
            pltpu.SemaphoreType.DMA((n - 1,)),
            pltpu.SemaphoreType.DMA((n - 1,)),
            pltpu.SemaphoreType.DMA((n - 1,)),
            pltpu.SemaphoreType.DMA((n - 1,)),
        ],
        compiler_params=pltpu.CompilerParams(collective_id=cid, has_side_effects=True, vmem_limit_bytes=56 * 2**20),
        name="row_pass",
    )(support, counts, x, y, g)


def col_pass(log_total, support, counts, x, y, lse):
    blocks, tgt_blocks = lse.shape[0], y.shape[1] // BLK
    return pl.pallas_call(
        functools.partial(col_kernel, log_total),
        out_shape=(jax.ShapeDtypeStruct((blocks, BLK), F32), jax.ShapeDtypeStruct((tgt_blocks, BLK), F32)),
        in_specs=[VMEM, ANY, VMEM, VMEM, VMEM],
        out_specs=(ANY, ANY),
        scratch_shapes=[
            pltpu.VMEM(support.shape, jnp.int32),
            pltpu.SMEM((blocks * support.shape[0],), jnp.int32),
            pltpu.SMEM(counts.shape, jnp.int32),
            pltpu.SMEM((blocks * support.shape[0] + 2 * GROUP + 8,), jnp.int32),
            pltpu.VMEM((blocks, BLK), F32),
            pltpu.VMEM((tgt_blocks, BLK), F32),
            pltpu.VMEM((blocks, 2 * x.shape[0] + 16, BLK), BF16),
            pltpu.VMEM((tgt_blocks * 8 + 64, BLK), F32),
            pltpu.VMEM((tgt_blocks * 8 + 64, BLK), F32),
            pltpu.VMEM((GROUP, BLK, BLK), F32),
            pltpu.SemaphoreType.DMA((7 + support.shape[0],)),
        ],
        name="col_pass",
        compiler_params=pltpu.CompilerParams(vmem_limit_bytes=40 * 2**20),
    )(support, counts, x, y, lse)


def body(src_points, tgt_points, tgt_potential, support, counts):
    total_src = src_points.shape[1] * lax.axis_size("src")
    total_tgt = tgt_points.shape[1] * lax.axis_size("tgt")
    flat_support = support.transpose(2, 1, 0)
    flat_counts = counts.reshape(-1)
    pot = tgt_potential.reshape(-1, BLK)
    row_lse = row_pass("tgt", lax.axis_size("tgt"), 0, flat_support, flat_counts, src_points, tgt_points, pot)
    src_potential, col_part = col_pass(math.log(total_tgt), flat_support, flat_counts, src_points, tgt_points, row_lse)
    new_tgt = col_exchange("src", lax.axis_size("src"), 1, BLUR * math.log(total_src), col_part, tgt_points)
    return src_potential.reshape(-1), new_tgt.reshape(-1)


def solution(mesh):
    return jax.shard_map(
        body,
        mesh=mesh,
        in_specs=(P(None, "src"), P(None, "tgt"), P("tgt"), P("src", "tgt", None), P("src", "tgt")),
        out_specs=(P("src"), P("tgt")),
        check_vma=False,
    )
```

```python
import functools
import math

import jax
import jax.numpy as jnp
from jax import lax
from jax.experimental import pallas as pl
from jax.experimental.pallas import tpu as pltpu
from jax.sharding import PartitionSpec as P

BLK = 128
BLUR = 0.05
NEG = -1e30
TO_LOG2 = math.log2(math.e) / BLUR
FROM_LOG2 = BLUR * math.log(2.0)
GROUP = 64
BUNCH = 16
Y_PARTS = 8
F32 = jnp.float32
BF16 = jnp.bfloat16
MESH = pl.DeviceIdType.MESH


def three_parts(v):
    hi = v.astype(BF16).astype(F32)
    mid = (v - hi).astype(BF16).astype(F32)
    return hi, mid, v - hi - mid


def split_source(x, scale):
    scaled = x.astype(F32) * scale
    hi = scaled.astype(BF16)
    return hi, (scaled - hi.astype(F32)).astype(BF16)


def lane_block(ref, index):
    return ref[:, pl.ds(pl.multiple_of(index * BLK, BLK), BLK)]


def eight_rows(index):
    return pl.ds(pl.multiple_of(index * 8, 8), 8)


def tile_score(left, right):
    return lax.dot_general(left, right, (((0,), (0,)), ((), ())), preferred_element_type=F32)


def tile_sums(score):
    score = score.reshape(BLK // 8, 8, BLK)
    high = jnp.max(score, axis=0)
    return high, jnp.sum(jnp.exp2(score - high[None]), axis=0)


def pipeline(list_ref, steps, score_ref, begin, end):
    for q in range(GROUP):
        score_ref[q] = begin(list_ref[q])

    def step(i, _):
        for q in range(GROUP):
            end(list_ref[i * GROUP + q], score_ref[q])
            score_ref[q] = begin(list_ref[(i + 1) * GROUP + q])
        return 0

    step(0, 0)
    lax.fori_loop(1, steps, step, 0)


def merged_rows(high_ref, total_ref, step, stride):
    at = [pl.ds(step * 8 * stride + s, 8, stride=stride) for s in range(8)]
    highs = [high_ref[a, :] for a in at]
    high = functools.reduce(jnp.maximum, highs)
    total = sum(total_ref[a, :] * jnp.exp2(h - high) for a, h in zip(at, highs))
    return jnp.where(total > 0.0, high + jnp.log2(total), NEG)


def chunk_offset(c, n):
    return lax.rem(n // 2 + lax.div(c + 1, 2) * (1 - 2 * lax.rem(c + 1, 2)) + n, n)


def row_kernel(axis, n, support_any, counts_any, x_any, y_any, g_any, out_ref, support_ref, counts_ref, x_ref, y_ref, g_ref, left_ref, score_ref, high_ref, total_ref, part_ref, parts, whole, sem, send_sem, recv_sem, send_sem2, recv_sem2):
    blocks = out_ref.shape[0]
    slots = support_ref.shape[0]
    features = x_ref.shape[0]
    rows = blocks // n
    bunches = rows // BUNCH
    me = lax.axis_index(axis)
    tgt_blocks = g_ref.shape[0]
    wide = y_ref.shape[1] // Y_PARTS
    strips = [pl.ds(i * wide, wide) for i in range(Y_PARTS)]
    pairs = ((support_any, support_ref), (counts_any, counts_ref), (g_any, g_ref))
    pairs = pairs + tuple((y_any.at[:, strip], y_ref.at[:, strip]) for strip in strips) + ((x_any, x_ref),)
    fetches = [pltpu.make_async_copy(a, b, sem.at[i]) for i, (a, b) in enumerate(pairs)]
    for fetch in fetches:
        fetch.start()
    all_here = greet(axis, [lax.rem(me + s, n) for s in range(1, n)])
    ones = jnp.where(lax.broadcasted_iota(jnp.int32, (32, BLK), 0) < 24, 1.0, 0.0).astype(BF16)
    for i in range(3):
        fetches[i].wait()

    def extend(step, _):
        pot = (TO_LOG2 / 8) * g_ref[eight_rows(step), :]
        for q in range(8):
            t = step * 8 + q
            y = lane_block(y_ref, t)
            yf = y.astype(F32)
            sq = yf * yf
            sq = functools.reduce(jnp.add, [sq[i : i + 8] for i in range(0, features, 8)])
            hi, mid, lo = three_parts(pot[q : q + 1] - (TO_LOG2 / (2 * features)) * sq)
            extra = jnp.concatenate([hi, mid, lo, jnp.zeros((8, BLK), F32)], axis=0).astype(BF16)
            left_ref[t] = jnp.concatenate([y, y, extra], axis=0)
        return 0

    each = tgt_blocks // 8 // Y_PARTS
    for i in range(Y_PARTS):
        fetches[3 + i].wait()
        lax.fori_loop(i * each, (i + 1) * each, extend, 0, unroll=4)
    fetches[3 + Y_PARTS].wait()
    height = left_ref.shape[1]
    first = lax.broadcasted_iota(jnp.int32, (height, BLK), 0) == 2 * features
    left_ref[tgt_blocks] = jnp.where(first, NEG, 0.0).astype(BF16)

    def chunk(i):
        return pl.ds(pl.multiple_of(i * rows, rows), rows)

    def first_row(i):
        owner = lax.rem(me + chunk_offset(lax.div(i, bunches), n), n)
        return owner * rows + lax.rem(i, bunches) * BUNCH

    def begin(r):
        lefts = [left_ref[jnp.where(k < counts_ref[r], support_ref[k, 0, r], tgt_blocks)] for k in range(slots)]
        right = jnp.concatenate([*split_source(lane_block(x_ref, r), TO_LOG2 / features), ones], axis=0)
        return jnp.split(tile_score(jnp.concatenate(lefts, axis=1), right), slots, axis=0)

    def end(q):
        sums = [tile_sums(score_ref[q * slots + k]) for k in range(slots)]
        high = functools.reduce(jnp.maximum, [h for h, _ in sums])
        return high, sum(t * jnp.exp2(h - high) for h, t in sums)

    for q in range(BUNCH):
        for k, score in enumerate(begin(first_row(0) + q)):
            score_ref[q * slots + k] = score

    def send(c):
        target = lax.rem(me + chunk_offset(c, n), n)
        return pltpu.make_async_remote_copy(
            src_ref=part_ref.at[chunk(target)],
            dst_ref=parts.at[c],
            send_sem=send_sem.at[c],
            recv_sem=recv_sem.at[c],
            device_id={axis: target},
            device_id_type=MESH,
        )

    def sums(c):
        def step(b):
            after = first_row(c * bunches + b + 1)
            for q in range(BUNCH):
                at = eight_rows(b * BUNCH + q)
                high_ref[at, :], total_ref[at, :] = end(q)
                for k, score in enumerate(begin(after + q)):
                    score_ref[q * slots + k] = score

        for b in range(bunches):
            step(b)

    def settle(c):
        owner = lax.rem(me + chunk_offset(c, n), n)
        for h in range(rows // 8):
            part_ref[eight_rows(owner * (rows // 8) + h), :] = merged_rows(high_ref, total_ref, h, 8)

    def chunk_step(c, _):
        settle(c - 1)
        send(c - 1).start()
        sums(c)
        return 0

    sums(0)
    all_here()
    lax.fori_loop(1, n, chunk_step, 0)
    settle(n - 1)
    for c in range(n - 1):
        send(jnp.int32(c)).wait_recv()
    whole[chunk(me), :] = combined([part_ref[chunk(me), :]] + [parts[c] for c in range(n - 1)])
    after = [
        remote(whole.at[chunk(me)], whole.at[chunk(me)], send_sem2.at[s], recv_sem2.at[s], axis, lax.rem(me + chunk_offset(s, n), n))
        for s in range(n - 1)
    ]
    for copy in after:
        copy.wait_recv()
    out_ref[...] = whole[...]
    for c in range(n - 1):
        send(jnp.int32(c)).wait_send()
    for copy in after:
        copy.wait_send()


def col_kernel(log_total, support_ref, counts_any, x_ref, y_ref, lse_ref, pot_any, out_any, turned_ref, code_ref, counts_ref, list_ref, pot_ref, out_ref, left_ref, high_ref, total_ref, score_ref, sem):
    blocks = pot_ref.shape[0]
    features = x_ref.shape[0]
    tgt_blocks = out_ref.shape[0]

    slots = support_ref.shape[0]
    counts_copy = pltpu.make_async_copy(counts_any, counts_ref, sem.at[4])
    counts_copy.start()
    row = lax.broadcasted_iota(jnp.int32, support_ref.shape, 2)
    slot = lax.broadcasted_iota(jnp.int32, support_ref.shape, 0)
    turned_ref[...] = support_ref[...] * (8 * blocks) + (row * 8 + slot)
    code_copies = [
        pltpu.make_async_copy(turned_ref.at[k, 0], code_ref.at[pl.ds(k * blocks, blocks)], sem.at[7 + k]) for k in range(slots)
    ]
    for copy in code_copies:
        copy.start()

    def clear(step, _):
        at = pl.ds(pl.multiple_of(step * 64, 64), 64)
        high_ref[at, :] = jnp.full((64, BLK), NEG, F32)
        total_ref[at, :] = jnp.zeros((64, BLK), F32)
        return 0

    lax.fori_loop(0, high_ref.shape[0] // 64, clear, 0)
    sub = lax.broadcasted_iota(jnp.int32, (16, BLK), 0)
    ones = jnp.where(sub < 3, 1.0, 0.0).astype(BF16)

    for copy in [counts_copy] + code_copies:
        copy.wait()

    def prepare(r, tail):
        for k in range(slots):
            list_ref[tail + k] = code_ref[k * blocks + r]
        x = lane_block(x_ref, r)
        xf = x.astype(F32)
        pot = -FROM_LOG2 * lse_ref[pl.ds(r, 1), :] + BLUR * log_total
        pot_ref[pl.ds(r, 1), :] = pot + jnp.sum(xf * xf, axis=0, keepdims=True) * (1.0 / (2 * features))
        hi, mid, lo = three_parts(TO_LOG2 * pot)
        extra = jnp.where(sub == 0, hi, jnp.where(sub == 1, mid, jnp.where(sub == 2, lo, 0.0))).astype(BF16)
        left_ref[r] = jnp.concatenate([*split_source(x, TO_LOG2 / features), extra], axis=0)
        return tail + counts_ref[r]

    live = lax.fori_loop(0, blocks, prepare, 0, unroll=16)
    for q in range(2 * GROUP):
        list_ref[live + q] = 7
    pot_copy = pltpu.make_async_copy(pot_ref, pot_any, sem.at[6])
    pot_copy.start()

    slot_bits = (8 * blocks).bit_length() - 1

    def begin(code):
        y = lane_block(y_ref, lax.shift_right_logical(code, slot_bits))
        r = lax.shift_right_logical(jnp.bitwise_and(code, 8 * blocks - 1), 3)
        return tile_score(left_ref[r], jnp.concatenate([y, y, ones], axis=0))

    def end(code, score):
        t = lax.shift_right_logical(code, slot_bits)
        own, own_total = tile_sums(score)
        at = eight_rows(jnp.where(jnp.bitwise_and(code, 7) == 7, tgt_blocks, t))
        old = high_ref[at, :]
        high = jnp.maximum(own, old)
        high_ref[at, :] = high
        total_ref[at, :] = own_total * jnp.exp2(own - high) + total_ref[at, :] * jnp.exp2(old - high)

    pipeline(list_ref, lax.div(live + (GROUP - 1), GROUP), score_ref, begin, end)

    def finish(step, _):
        out_ref[eight_rows(step), :] = merged_rows(high_ref, total_ref, step, 8)
        return 0

    pieces = 4
    size = tgt_blocks // pieces
    copies = []
    for piece in range(pieces):
        lax.fori_loop(piece * size // 8, (piece + 1) * size // 8, finish, 0, unroll=8)
        rows = pl.ds(piece * size, size)
        copies.append(pltpu.make_async_copy(out_ref.at[rows], out_any.at[rows], sem.at[piece]))
        copies[-1].start()
    for copy in copies + [pot_copy]:
        copy.wait()


def remote(source, target, send_sem, recv_sem, axis, peer):
    copy = pltpu.make_async_remote_copy(
        src_ref=source,
        dst_ref=target,
        send_sem=send_sem,
        recv_sem=recv_sem,
        device_id={axis: peer},
        device_id_type=MESH,
    )
    copy.start()
    return copy


def greet(axis, peers):
    barrier = pltpu.get_barrier_semaphore()
    for peer in peers:
        pl.semaphore_signal(barrier, inc=1, device_id={axis: peer}, device_id_type=MESH)
    return lambda: pl.semaphore_wait(barrier, len(peers))


def combined(terms):
    high = functools.reduce(jnp.maximum, terms)
    return high + jnp.log2(sum(jnp.exp2(term - high) for term in terms))


PIECES = 2


def col_exchange_kernel(axis, n, shift, part_any, y_any, out_ref, mine_ref, twin_ref, pair_ref, parts, whole, y_ref, sq_ref, local_sem, send_a, recv_a, send_b, recv_b, send_c, recv_c, send_d, recv_d):
    me = lax.axis_index(axis)
    chips = n // 2
    core = lax.rem(me, 2)
    chip = lax.div(me, 2)
    twin = me + 1 - 2 * core
    rows = part_any.shape[0] // n
    half = chips * rows
    size = half // PIECES
    side = math.isqrt(chips)
    steps = [(dy, dx) for dy in range(side) for dx in range(side)]
    steps = sorted(steps, key=lambda step: -sum(min(d, side - d) for d in step))[:-1]

    def chip_at(dy, dx):
        return lax.rem(lax.div(chip, side) + side + dy, side) * side + lax.rem(chip + side + dx, side)

    others = [chip_at(dy, dx) for dy, dx in steps]
    senders = [chip_at(-dy, -dx) for dy, dx in steps]

    def chunk(where, i):
        return pl.ds(pl.multiple_of((where * chips + i) * rows, rows), rows)

    def local(i):
        return pl.ds(pl.multiple_of(i * rows, rows), rows)

    def piece(where, p):
        return pl.ds(pl.multiple_of(where * half + p * size, size), size)

    all_here = greet(axis, [twin] + [2 * other + core for other in others])
    mine_copy = pltpu.make_async_copy(part_any.at[pl.ds(pl.multiple_of(core * half, half), half)], mine_ref, local_sem.at[0])
    mine_copy.start()
    width = rows * BLK
    own = core * chips + chip
    y_copy = pltpu.make_async_copy(y_any.at[:, pl.ds(pl.multiple_of(own * width, width), width)], y_ref, local_sem.at[1])
    y_copy.start()
    y_copy.wait()
    y = y_ref[...].astype(F32)
    sq = jnp.sum(y * y, axis=0, keepdims=True) * (1.0 / (2 * y.shape[0]))
    for q in range(rows):
        sq_ref[pl.ds(q, 1), :] = sq[:, q * BLK : (q + 1) * BLK]
    mine_copy.wait()
    all_here()

    first = [
        remote(part_any.at[piece(1 - core, p)], twin_ref.at[pl.ds(p * size, size)], send_a.at[p], recv_a.at[p], axis, twin)
        for p in range(PIECES)
    ]
    for p in range(PIECES):
        first[p].wait_recv()
        at = pl.ds(p * size, size)
        pair_ref[at, :] = combined([mine_ref[at, :], twin_ref[at, :]])
    second = [
        remote(pair_ref.at[local(other)], parts.at[s], send_b.at[s], recv_b.at[s], axis, 2 * other + core)
        for s, other in enumerate(others)
    ]
    for copy in second:
        copy.wait_recv()
    result = combined([pair_ref[local(chip), :]] + [parts[s] for s in range(chips - 1)])
    mine = chunk(core, chip)
    whole[mine, :] = sq_ref[...] - FROM_LOG2 * result + shift
    third = [
        remote(whole.at[mine], whole.at[mine], send_c.at[s], recv_c.at[s], axis, 2 * other + core) for s, other in enumerate(others)
    ]
    fourth = [remote(whole.at[mine], whole.at[mine], send_d.at[chips - 1], recv_d.at[chips - 1], axis, twin)]
    for s in reversed(range(chips - 1)):
        third[s].wait_recv()
        came = chunk(core, senders[s])
        fourth.append(remote(whole.at[came], whole.at[came], send_d.at[s], recv_d.at[s], axis, twin))
    own_half = pl.ds(pl.multiple_of(core * half, half), half)
    twin_half = pl.ds(pl.multiple_of((1 - core) * half, half), half)
    out_ref[own_half, :] = whole[own_half, :]
    for copy in fourth:
        copy.wait_recv()
    out_ref[twin_half, :] = whole[twin_half, :]
    for copy in first + second + third + fourth:
        copy.wait_send()


def col_exchange(axis, n, cid, shift, part, y):
    rows, chips = part.shape[0] // n, n // 2
    half = chips * rows
    sems = [pltpu.SemaphoreType.DMA((count,)) for count in (2, PIECES, PIECES, chips - 1, chips - 1, chips - 1, chips - 1, chips, chips)]
    return pl.pallas_call(
        functools.partial(col_exchange_kernel, axis, n, shift),
        out_shape=jax.ShapeDtypeStruct(part.shape, F32),
        in_specs=[ANY, ANY],
        out_specs=VMEM,
        scratch_shapes=[
            pltpu.VMEM((half, BLK), F32),
            pltpu.VMEM((half, BLK), F32),
            pltpu.VMEM((half, BLK), F32),
            pltpu.VMEM((chips - 1, rows, BLK), F32),
            pltpu.VMEM(part.shape, F32),
            pltpu.VMEM((y.shape[0], rows * BLK), BF16),
            pltpu.VMEM((rows, BLK), F32),
            *sems,
        ],
        compiler_params=pltpu.CompilerParams(collective_id=cid, has_side_effects=True, vmem_limit_bytes=8 * 2**20),
        name="exchange_" + axis,
    )(part, y)


VMEM = pl.BlockSpec(memory_space=pltpu.VMEM)
SMEM = pl.BlockSpec(memory_space=pltpu.SMEM)
ANY = pl.BlockSpec(memory_space=pl.ANY)


def row_pass(axis, n, cid, support, counts, x, y, g):
    blocks, slots = counts.shape[0], support.shape[0]
    rows = blocks // n
    return pl.pallas_call(
        functools.partial(row_kernel, axis, n),
        out_shape=jax.ShapeDtypeStruct((blocks, BLK), F32),
        in_specs=[ANY] * 5,
        out_specs=VMEM,
        scratch_shapes=[
            pltpu.SMEM(support.shape, jnp.int32),
            pltpu.SMEM(counts.shape, jnp.int32),
            pltpu.VMEM(x.shape, BF16),
            pltpu.VMEM(y.shape, BF16),
            pltpu.VMEM(g.shape, F32),
            pltpu.VMEM((g.shape[0] + 1, 2 * x.shape[0] + 32, BLK), BF16),
            pltpu.VMEM((BUNCH * slots, BLK, BLK), F32),
            pltpu.VMEM((rows * 8, BLK), F32),
            pltpu.VMEM((rows * 8, BLK), F32),
            pltpu.VMEM((blocks, BLK), F32),
            pltpu.VMEM((n - 1, rows, BLK), F32),
            pltpu.VMEM((blocks, BLK), F32),
            pltpu.SemaphoreType.DMA((4 + Y_PARTS,)),
            pltpu.SemaphoreType.DMA((n - 1,)),
            pltpu.SemaphoreType.DMA((n - 1,)),
            pltpu.SemaphoreType.DMA((n - 1,)),
            pltpu.SemaphoreType.DMA((n - 1,)),
        ],
        compiler_params=pltpu.CompilerParams(collective_id=cid, has_side_effects=True, vmem_limit_bytes=56 * 2**20),
        name="row_pass",
    )(support, counts, x, y, g)


def col_pass(log_total, support, counts, x, y, lse):
    blocks, tgt_blocks = lse.shape[0], y.shape[1] // BLK
    return pl.pallas_call(
        functools.partial(col_kernel, log_total),
        out_shape=(jax.ShapeDtypeStruct((blocks, BLK), F32), jax.ShapeDtypeStruct((tgt_blocks, BLK), F32)),
        in_specs=[VMEM, ANY, VMEM, VMEM, VMEM],
        out_specs=(ANY, ANY),
        scratch_shapes=[
            pltpu.VMEM(support.shape, jnp.int32),
            pltpu.SMEM((blocks * support.shape[0],), jnp.int32),
            pltpu.SMEM(counts.shape, jnp.int32),
            pltpu.SMEM((blocks * support.shape[0] + 2 * GROUP + 8,), jnp.int32),
            pltpu.VMEM((blocks, BLK), F32),
            pltpu.VMEM((tgt_blocks, BLK), F32),
            pltpu.VMEM((blocks, 2 * x.shape[0] + 16, BLK), BF16),
            pltpu.VMEM((tgt_blocks * 8 + 64, BLK), F32),
            pltpu.VMEM((tgt_blocks * 8 + 64, BLK), F32),
            pltpu.VMEM((GROUP, BLK, BLK), F32),
            pltpu.SemaphoreType.DMA((7 + support.shape[0],)),
        ],
        name="col_pass",
        compiler_params=pltpu.CompilerParams(vmem_limit_bytes=40 * 2**20),
    )(support, counts, x, y, lse)


def body(src_points, tgt_points, tgt_potential, support, counts):
    total_src = src_points.shape[1] * lax.axis_size("src")
    total_tgt = tgt_points.shape[1] * lax.axis_size("tgt")
    flat_support = support.transpose(2, 1, 0)
    flat_counts = counts.reshape(-1)
    pot = tgt_potential.reshape(-1, BLK)
    row_lse = row_pass("tgt", lax.axis_size("tgt"), 0, flat_support, flat_counts, src_points, tgt_points, pot)
    src_potential, col_part = col_pass(math.log(total_tgt), flat_support, flat_counts, src_points, tgt_points, row_lse)
    new_tgt = col_exchange("src", lax.axis_size("src"), 1, BLUR * math.log(total_src), col_part, tgt_points)
    return src_potential.reshape(-1), new_tgt.reshape(-1)


def solution(mesh):
    return jax.shard_map(
        body,
        mesh=mesh,
        in_specs=(P(None, "src"), P(None, "tgt"), P("tgt"), P("src", "tgt", None), P("src", "tgt")),
        out_specs=(P("src"), P("tgt")),
        check_vma=False,
    )
```

```python
import functools
import math

import jax
import jax.numpy as jnp
from jax import lax
from jax.experimental import pallas as pl
from jax.experimental.pallas import tpu as pltpu
from jax.sharding import PartitionSpec as P

BLK = 128
BLUR = 0.05
NEG = -1e30
TO_LOG2 = math.log2(math.e) / BLUR
FROM_LOG2 = BLUR * math.log(2.0)
GROUP = 64
BUNCH = 16
Y_PARTS = 8
F32 = jnp.float32
BF16 = jnp.bfloat16
MESH = pl.DeviceIdType.MESH


def three_parts(v):
    hi = v.astype(BF16).astype(F32)
    mid = (v - hi).astype(BF16).astype(F32)
    return hi, mid, v - hi - mid


def split_source(x, scale):
    scaled = x.astype(F32) * scale
    hi = scaled.astype(BF16)
    return hi, (scaled - hi.astype(F32)).astype(BF16)


def lane_block(ref, index):
    return ref[:, pl.ds(pl.multiple_of(index * BLK, BLK), BLK)]


def eight_rows(index):
    return pl.ds(pl.multiple_of(index * 8, 8), 8)


def tile_score(left, right):
    return lax.dot_general(left, right, (((0,), (0,)), ((), ())), preferred_element_type=F32)


def tile_sums(score):
    score = score.reshape(BLK // 8, 8, BLK)
    high = jnp.max(score, axis=0)
    return high, jnp.sum(jnp.exp2(score - high[None]), axis=0)


def pipeline(list_ref, steps, score_ref, begin, end):
    for q in range(GROUP):
        score_ref[q] = begin(list_ref[q])

    def step(i, _):
        for q in range(GROUP):
            end(list_ref[i * GROUP + q], score_ref[q])
            score_ref[q] = begin(list_ref[(i + 1) * GROUP + q])
        return 0

    step(0, 0)
    lax.fori_loop(1, steps, step, 0)


def merged_rows(high_ref, total_ref, step, stride):
    at = [pl.ds(step * 8 * stride + s, 8, stride=stride) for s in range(8)]
    highs = [high_ref[a, :] for a in at]
    high = functools.reduce(jnp.maximum, highs)
    total = sum(total_ref[a, :] * jnp.exp2(h - high) for a, h in zip(at, highs))
    return jnp.where(total > 0.0, high + jnp.log2(total), NEG)


def chunk_offset(c, n):
    return lax.rem(n // 2 + lax.div(c + 1, 2) * (1 - 2 * lax.rem(c + 1, 2)) + n, n)


def row_kernel(axis, n, support_any, counts_any, x_any, y_any, g_any, out_ref, support_ref, counts_ref, x_ref, y_ref, g_ref, left_ref, score_ref, high_ref, total_ref, part_ref, parts, whole, sem, send_sem, recv_sem, send_sem2, recv_sem2):
    blocks = out_ref.shape[0]
    slots = support_ref.shape[0]
    features = x_ref.shape[0]
    rows = blocks // n
    bunches = rows // BUNCH
    me = lax.axis_index(axis)
    tgt_blocks = g_ref.shape[0]
    wide = y_ref.shape[1] // Y_PARTS
    strips = [pl.ds(i * wide, wide) for i in range(Y_PARTS)]
    pairs = ((support_any, support_ref), (counts_any, counts_ref), (g_any, g_ref))
    pairs = pairs + tuple((y_any.at[:, strip], y_ref.at[:, strip]) for strip in strips) + ((x_any, x_ref),)
    fetches = [pltpu.make_async_copy(a, b, sem.at[i]) for i, (a, b) in enumerate(pairs)]
    for fetch in fetches:
        fetch.start()
    all_here = greet(axis, [lax.rem(me + s, n) for s in range(1, n)])
    ones = jnp.where(lax.broadcasted_iota(jnp.int32, (32, BLK), 0) < 24, 1.0, 0.0).astype(BF16)
    for i in range(3):
        fetches[i].wait()

    def extend(step, _):
        pot = (TO_LOG2 / 8) * g_ref[eight_rows(step), :]
        for q in range(8):
            t = step * 8 + q
            y = lane_block(y_ref, t)
            yf = y.astype(F32)
            sq = yf * yf
            sq = functools.reduce(jnp.add, [sq[i : i + 8] for i in range(0, features, 8)])
            hi, mid, lo = three_parts(pot[q : q + 1] - (TO_LOG2 / (2 * features)) * sq)
            extra = jnp.concatenate([hi, mid, lo, jnp.zeros((8, BLK), F32)], axis=0).astype(BF16)
            left_ref[t] = jnp.concatenate([y, y, extra], axis=0)
        return 0

    each = tgt_blocks // 8 // Y_PARTS
    for i in range(Y_PARTS):
        fetches[3 + i].wait()
        lax.fori_loop(i * each, (i + 1) * each, extend, 0, unroll=8)
    fetches[3 + Y_PARTS].wait()
    height = left_ref.shape[1]
    first = lax.broadcasted_iota(jnp.int32, (height, BLK), 0) == 2 * features
    left_ref[tgt_blocks] = jnp.where(first, NEG, 0.0).astype(BF16)

    def chunk(i):
        return pl.ds(pl.multiple_of(i * rows, rows), rows)

    def first_row(i):
        owner = lax.rem(me + chunk_offset(lax.div(i, bunches), n), n)
        return owner * rows + lax.rem(i, bunches) * BUNCH

    def begin(r):
        lefts = [left_ref[jnp.where(k < counts_ref[r], support_ref[k, 0, r], tgt_blocks)] for k in range(slots)]
        right = jnp.concatenate([*split_source(lane_block(x_ref, r), TO_LOG2 / features), ones], axis=0)
        return jnp.split(tile_score(jnp.concatenate(lefts, axis=1), right), slots, axis=0)

    def end(q):
        sums = [tile_sums(score_ref[q * slots + k]) for k in range(slots)]
        high = functools.reduce(jnp.maximum, [h for h, _ in sums])
        return high, sum(t * jnp.exp2(h - high) for h, t in sums)

    for q in range(BUNCH):
        for k, score in enumerate(begin(first_row(0) + q)):
            score_ref[q * slots + k] = score

    def send(c):
        target = lax.rem(me + chunk_offset(c, n), n)
        return pltpu.make_async_remote_copy(
            src_ref=part_ref.at[chunk(target)],
            dst_ref=parts.at[c],
            send_sem=send_sem.at[c],
            recv_sem=recv_sem.at[c],
            device_id={axis: target},
            device_id_type=MESH,
        )

    def sums(c):
        def step(b):
            after = first_row(c * bunches + b + 1)
            for q in range(BUNCH):
                at = eight_rows(b * BUNCH + q)
                high_ref[at, :], total_ref[at, :] = end(q)
                for k, score in enumerate(begin(after + q)):
                    score_ref[q * slots + k] = score

        for b in range(bunches):
            step(b)

    def settle(c):
        owner = lax.rem(me + chunk_offset(c, n), n)
        for h in range(rows // 8):
            part_ref[eight_rows(owner * (rows // 8) + h), :] = merged_rows(high_ref, total_ref, h, 8)

    def chunk_step(c, _):
        settle(c - 1)
        send(c - 1).start()
        sums(c)
        return 0

    sums(0)
    all_here()
    lax.fori_loop(1, n, chunk_step, 0)
    settle(n - 1)
    for c in range(n - 1):
        send(jnp.int32(c)).wait_recv()
    whole[chunk(me), :] = combined([part_ref[chunk(me), :]] + [parts[c] for c in range(n - 1)])
    after = [
        remote(whole.at[chunk(me)], whole.at[chunk(me)], send_sem2.at[s], recv_sem2.at[s], axis, lax.rem(me + chunk_offset(s, n), n))
        for s in range(n - 1)
    ]
    for copy in after:
        copy.wait_recv()
    out_ref[...] = whole[...]
    for c in range(n - 1):
        send(jnp.int32(c)).wait_send()
    for copy in after:
        copy.wait_send()


def col_kernel(log_total, support_ref, counts_any, x_ref, y_ref, lse_ref, pot_any, out_any, turned_ref, code_ref, counts_ref, list_ref, pot_ref, out_ref, left_ref, high_ref, total_ref, score_ref, sem):
    blocks = pot_ref.shape[0]
    features = x_ref.shape[0]
    tgt_blocks = out_ref.shape[0]

    slots = support_ref.shape[0]
    counts_copy = pltpu.make_async_copy(counts_any, counts_ref, sem.at[4])
    counts_copy.start()
    row = lax.broadcasted_iota(jnp.int32, support_ref.shape, 2)
    slot = lax.broadcasted_iota(jnp.int32, support_ref.shape, 0)
    turned_ref[...] = support_ref[...] * (8 * blocks) + (row * 8 + slot)
    code_copies = [
        pltpu.make_async_copy(turned_ref.at[k, 0], code_ref.at[pl.ds(k * blocks, blocks)], sem.at[7 + k]) for k in range(slots)
    ]
    for copy in code_copies:
        copy.start()

    def clear(step, _):
        at = pl.ds(pl.multiple_of(step * 64, 64), 64)
        high_ref[at, :] = jnp.full((64, BLK), NEG, F32)
        total_ref[at, :] = jnp.zeros((64, BLK), F32)
        return 0

    lax.fori_loop(0, high_ref.shape[0] // 64, clear, 0)
    sub = lax.broadcasted_iota(jnp.int32, (16, BLK), 0)
    ones = jnp.where(sub < 3, 1.0, 0.0).astype(BF16)

    for copy in [counts_copy] + code_copies:
        copy.wait()

    def prepare(r, tail):
        for k in range(slots):
            list_ref[tail + k] = code_ref[k * blocks + r]
        x = lane_block(x_ref, r)
        xf = x.astype(F32)
        pot = -FROM_LOG2 * lse_ref[pl.ds(r, 1), :] + BLUR * log_total
        pot_ref[pl.ds(r, 1), :] = pot + jnp.sum(xf * xf, axis=0, keepdims=True) * (1.0 / (2 * features))
        hi, mid, lo = three_parts(TO_LOG2 * pot)
        extra = jnp.where(sub == 0, hi, jnp.where(sub == 1, mid, jnp.where(sub == 2, lo, 0.0))).astype(BF16)
        left_ref[r] = jnp.concatenate([*split_source(x, TO_LOG2 / features), extra], axis=0)
        return tail + counts_ref[r]

    live = lax.fori_loop(0, blocks, prepare, 0, unroll=16)
    for q in range(2 * GROUP):
        list_ref[live + q] = 7
    pot_copy = pltpu.make_async_copy(pot_ref, pot_any, sem.at[6])
    pot_copy.start()

    slot_bits = (8 * blocks).bit_length() - 1

    def begin(code):
        y = lane_block(y_ref, lax.shift_right_logical(code, slot_bits))
        r = lax.shift_right_logical(jnp.bitwise_and(code, 8 * blocks - 1), 3)
        return tile_score(left_ref[r], jnp.concatenate([y, y, ones], axis=0))

    def end(code, score):
        t = lax.shift_right_logical(code, slot_bits)
        own, own_total = tile_sums(score)
        at = eight_rows(jnp.where(jnp.bitwise_and(code, 7) == 7, tgt_blocks, t))
        old = high_ref[at, :]
        high = jnp.maximum(own, old)
        high_ref[at, :] = high
        total_ref[at, :] = own_total * jnp.exp2(own - high) + total_ref[at, :] * jnp.exp2(old - high)

    pipeline(list_ref, lax.div(live + (GROUP - 1), GROUP), score_ref, begin, end)

    def finish(step, _):
        out_ref[eight_rows(step), :] = merged_rows(high_ref, total_ref, step, 8)
        return 0

    pieces = 4
    size = tgt_blocks // pieces
    copies = []
    for piece in range(pieces):
        lax.fori_loop(piece * size // 8, (piece + 1) * size // 8, finish, 0, unroll=8)
        rows = pl.ds(piece * size, size)
        copies.append(pltpu.make_async_copy(out_ref.at[rows], out_any.at[rows], sem.at[piece]))
        copies[-1].start()
    for copy in copies + [pot_copy]:
        copy.wait()


def remote(source, target, send_sem, recv_sem, axis, peer):
    copy = pltpu.make_async_remote_copy(
        src_ref=source,
        dst_ref=target,
        send_sem=send_sem,
        recv_sem=recv_sem,
        device_id={axis: peer},
        device_id_type=MESH,
    )
    copy.start()
    return copy


def greet(axis, peers):
    barrier = pltpu.get_barrier_semaphore()
    for peer in peers:
        pl.semaphore_signal(barrier, inc=1, device_id={axis: peer}, device_id_type=MESH)
    return lambda: pl.semaphore_wait(barrier, len(peers))


def combined(terms):
    high = functools.reduce(jnp.maximum, terms)
    return high + jnp.log2(sum(jnp.exp2(term - high) for term in terms))


PIECES = 1


def col_exchange_kernel(axis, n, shift, part_any, y_any, out_ref, mine_ref, twin_ref, pair_ref, parts, whole, y_ref, sq_ref, local_sem, send_a, recv_a, send_b, recv_b, send_c, recv_c, send_d, recv_d):
    me = lax.axis_index(axis)
    chips = n // 2
    core = lax.rem(me, 2)
    chip = lax.div(me, 2)
    twin = me + 1 - 2 * core
    rows = part_any.shape[0] // n
    half = chips * rows
    size = half // PIECES
    side = math.isqrt(chips)
    steps = [(dy, dx) for dy in range(side) for dx in range(side)]
    steps = sorted(steps, key=lambda step: -sum(min(d, side - d) for d in step))[:-1]

    def chip_at(dy, dx):
        return lax.rem(lax.div(chip, side) + side + dy, side) * side + lax.rem(chip + side + dx, side)

    others = [chip_at(dy, dx) for dy, dx in steps]
    senders = [chip_at(-dy, -dx) for dy, dx in steps]

    def chunk(where, i):
        return pl.ds(pl.multiple_of((where * chips + i) * rows, rows), rows)

    def local(i):
        return pl.ds(pl.multiple_of(i * rows, rows), rows)

    def piece(where, p):
        return pl.ds(pl.multiple_of(where * half + p * size, size), size)

    all_here = greet(axis, [twin] + [2 * other + core for other in others])
    mine_copy = pltpu.make_async_copy(part_any.at[pl.ds(pl.multiple_of(core * half, half), half)], mine_ref, local_sem.at[0])
    mine_copy.start()
    width = rows * BLK
    own = core * chips + chip
    y_copy = pltpu.make_async_copy(y_any.at[:, pl.ds(pl.multiple_of(own * width, width), width)], y_ref, local_sem.at[1])
    y_copy.start()
    y_copy.wait()
    y = y_ref[...].astype(F32)
    sq = jnp.sum(y * y, axis=0, keepdims=True) * (1.0 / (2 * y.shape[0]))
    for q in range(rows):
        sq_ref[pl.ds(q, 1), :] = sq[:, q * BLK : (q + 1) * BLK]
    mine_copy.wait()
    all_here()

    first = [
        remote(part_any.at[piece(1 - core, p)], twin_ref.at[pl.ds(p * size, size)], send_a.at[p], recv_a.at[p], axis, twin)
        for p in range(PIECES)
    ]
    for p in range(PIECES):
        first[p].wait_recv()
        at = pl.ds(p * size, size)
        pair_ref[at, :] = combined([mine_ref[at, :], twin_ref[at, :]])
    second = [
        remote(pair_ref.at[local(other)], parts.at[s], send_b.at[s], recv_b.at[s], axis, 2 * other + core)
        for s, other in enumerate(others)
    ]
    for copy in second:
        copy.wait_recv()
    result = combined([pair_ref[local(chip), :]] + [parts[s] for s in range(chips - 1)])
    mine = chunk(core, chip)
    whole[mine, :] = sq_ref[...] - FROM_LOG2 * result + shift
    third = [
        remote(whole.at[mine], whole.at[mine], send_c.at[s], recv_c.at[s], axis, 2 * other + core) for s, other in enumerate(others)
    ]
    fourth = [remote(whole.at[mine], whole.at[mine], send_d.at[chips - 1], recv_d.at[chips - 1], axis, twin)]
    for s in reversed(range(chips - 1)):
        third[s].wait_recv()
        came = chunk(core, senders[s])
        fourth.append(remote(whole.at[came], whole.at[came], send_d.at[s], recv_d.at[s], axis, twin))
    own_half = pl.ds(pl.multiple_of(core * half, half), half)
    twin_half = pl.ds(pl.multiple_of((1 - core) * half, half), half)
    out_ref[own_half, :] = whole[own_half, :]
    for copy in fourth:
        copy.wait_recv()
    out_ref[twin_half, :] = whole[twin_half, :]
    for copy in first + second + third + fourth:
        copy.wait_send()


def col_exchange(axis, n, cid, shift, part, y):
    rows, chips = part.shape[0] // n, n // 2
    half = chips * rows
    sems = [pltpu.SemaphoreType.DMA((count,)) for count in (2, PIECES, PIECES, chips - 1, chips - 1, chips - 1, chips - 1, chips, chips)]
    return pl.pallas_call(
        functools.partial(col_exchange_kernel, axis, n, shift),
        out_shape=jax.ShapeDtypeStruct(part.shape, F32),
        in_specs=[ANY, ANY],
        out_specs=VMEM,
        scratch_shapes=[
            pltpu.VMEM((half, BLK), F32),
            pltpu.VMEM((half, BLK), F32),
            pltpu.VMEM((half, BLK), F32),
            pltpu.VMEM((chips - 1, rows, BLK), F32),
            pltpu.VMEM(part.shape, F32),
            pltpu.VMEM((y.shape[0], rows * BLK), BF16),
            pltpu.VMEM((rows, BLK), F32),
            *sems,
        ],
        compiler_params=pltpu.CompilerParams(collective_id=cid, has_side_effects=True, vmem_limit_bytes=8 * 2**20),
        name="exchange_" + axis,
    )(part, y)


VMEM = pl.BlockSpec(memory_space=pltpu.VMEM)
SMEM = pl.BlockSpec(memory_space=pltpu.SMEM)
ANY = pl.BlockSpec(memory_space=pl.ANY)


def row_pass(axis, n, cid, support, counts, x, y, g):
    blocks, slots = counts.shape[0], support.shape[0]
    rows = blocks // n
    return pl.pallas_call(
        functools.partial(row_kernel, axis, n),
        out_shape=jax.ShapeDtypeStruct((blocks, BLK), F32),
        in_specs=[ANY] * 5,
        out_specs=VMEM,
        scratch_shapes=[
            pltpu.SMEM(support.shape, jnp.int32),
            pltpu.SMEM(counts.shape, jnp.int32),
            pltpu.VMEM(x.shape, BF16),
            pltpu.VMEM(y.shape, BF16),
            pltpu.VMEM(g.shape, F32),
            pltpu.VMEM((g.shape[0] + 1, 2 * x.shape[0] + 32, BLK), BF16),
            pltpu.VMEM((BUNCH * slots, BLK, BLK), F32),
            pltpu.VMEM((rows * 8, BLK), F32),
            pltpu.VMEM((rows * 8, BLK), F32),
            pltpu.VMEM((blocks, BLK), F32),
            pltpu.VMEM((n - 1, rows, BLK), F32),
            pltpu.VMEM((blocks, BLK), F32),
            pltpu.SemaphoreType.DMA((4 + Y_PARTS,)),
            pltpu.SemaphoreType.DMA((n - 1,)),
            pltpu.SemaphoreType.DMA((n - 1,)),
            pltpu.SemaphoreType.DMA((n - 1,)),
            pltpu.SemaphoreType.DMA((n - 1,)),
        ],
        compiler_params=pltpu.CompilerParams(collective_id=cid, has_side_effects=True, vmem_limit_bytes=56 * 2**20),
        name="row_pass",
    )(support, counts, x, y, g)


def col_pass(log_total, support, counts, x, y, lse):
    blocks, tgt_blocks = lse.shape[0], y.shape[1] // BLK
    return pl.pallas_call(
        functools.partial(col_kernel, log_total),
        out_shape=(jax.ShapeDtypeStruct((blocks, BLK), F32), jax.ShapeDtypeStruct((tgt_blocks, BLK), F32)),
        in_specs=[VMEM, ANY, VMEM, VMEM, VMEM],
        out_specs=(ANY, ANY),
        scratch_shapes=[
            pltpu.VMEM(support.shape, jnp.int32),
            pltpu.SMEM((blocks * support.shape[0],), jnp.int32),
            pltpu.SMEM(counts.shape, jnp.int32),
            pltpu.SMEM((blocks * support.shape[0] + 2 * GROUP + 8,), jnp.int32),
            pltpu.VMEM((blocks, BLK), F32),
            pltpu.VMEM((tgt_blocks, BLK), F32),
            pltpu.VMEM((blocks, 2 * x.shape[0] + 16, BLK), BF16),
            pltpu.VMEM((tgt_blocks * 8 + 64, BLK), F32),
            pltpu.VMEM((tgt_blocks * 8 + 64, BLK), F32),
            pltpu.VMEM((GROUP, BLK, BLK), F32),
            pltpu.SemaphoreType.DMA((7 + support.shape[0],)),
        ],
        name="col_pass",
        compiler_params=pltpu.CompilerParams(vmem_limit_bytes=40 * 2**20),
    )(support, counts, x, y, lse)


def body(src_points, tgt_points, tgt_potential, support, counts):
    total_src = src_points.shape[1] * lax.axis_size("src")
    total_tgt = tgt_points.shape[1] * lax.axis_size("tgt")
    flat_support = support.transpose(2, 1, 0)
    flat_counts = counts.reshape(-1)
    pot = tgt_potential.reshape(-1, BLK)
    row_lse = row_pass("tgt", lax.axis_size("tgt"), 0, flat_support, flat_counts, src_points, tgt_points, pot)
    src_potential, col_part = col_pass(math.log(total_tgt), flat_support, flat_counts, src_points, tgt_points, row_lse)
    new_tgt = col_exchange("src", lax.axis_size("src"), 1, BLUR * math.log(total_src), col_part, tgt_points)
    return src_potential.reshape(-1), new_tgt.reshape(-1)


def solution(mesh):
    return jax.shard_map(
        body,
        mesh=mesh,
        in_specs=(P(None, "src"), P(None, "tgt"), P("tgt"), P("src", "tgt", None), P("src", "tgt")),
        out_specs=(P("src"), P("tgt")),
        check_vma=False,
    )
```
